128 devices in a mesh: dp: 8 (over y_hi, x), ctx: 8 (over z, core), tensor: 2 (over y_lo).
Axes of the slice: x: 4, y: 4 (y_hi: 2, y_lo: 2; y = y_hi * 2 + y_lo), z: 4, core: 2. Of those that a mesh axis runs over, the one named last changes fastest.
Arguments:
- hidden_in: float32 [16384, 1536], P(('dp', 'ctx')), may hold values from -6 to 6
- out_grad: float32 [16384, 1536], P(('dp', 'ctx')), may hold values from -6 to 6
- expert_choice: int32 [16384, 4], P(('dp', 'ctx')), may hold values from 0 to 31, all different within a row; in each aligned block of 256 rows (0 to 255, 256 to 511, ...) at most 36 rows name the same one
- segments: int32 [8, 2048], P('dp'), may hold values from 0 to 3, never falling along the last dimension, each value on 1 to 1793 neighbouring positions
- expert_weights: float32 [32, 3, 1536, 768], P('dp', None, 'ctx', 'tensor'), may hold values from -0.8660254 to 0.8660254
- expert_moment: float32 [32, 3, 1536, 768], P('dp', None, 'ctx', 'tensor'), may hold values from -217.2232 to 217.2232
- attention_weights: float32 [2, 14, 1536, 128], P('tensor', None, 'ctx'), may hold values from -1.5 to 1.5
- attention_first: float32 [2, 14, 1536, 128], P('tensor', None, 'ctx'), may hold values from -24 to 24
- attention_second: float32 [2, 14, 1536, 128], P('tensor', None, 'ctx'), may hold values from 44.2368 to 294.912
- router_weights: float32 [1536, 32], P('ctx'), may hold values from -0.078125 to 0.078125
- router_first: float32 [1536, 32], P('ctx'), may hold values from -640 to 640
- router_second: float32 [1536, 32], P('ctx'), may hold values from 24576 to 163840
- norm_gains: float32 [2, 1536], P(None, 'ctx'), may hold values from 0.5 to 1.5
- gains_first: float32 [2, 1536], P(None, 'ctx'), may hold values from -160 to 160
- gains_second: float32 [2, 1536], P(None, 'ctx'), may hold values from 1966.08 to 13107.2
Outputs:
- layer_output: float32 [16384, 1536], P(('dp', 'ctx'), 'tensor')
- input_grad: float32 [16384, 1536], P(('dp', 'ctx'))
- expert_moment_new: float32 [32, 3, 1536, 768], P('dp', None, 'ctx', 'tensor')
- expert_new: float32 [32, 3, 1536, 768], P('dp', None, 'ctx', 'tensor')
- attention_first_new: float32 [2, 14, 1536, 128], P('tensor', None, 'ctx')
- attention_second_new: float32 [2, 14, 1536, 128], P('tensor', None, 'ctx')
- attention_new: float32 [2, 14, 1536, 128], P('tensor', None, 'ctx')
- router_first_new: float32 [1536, 32], P('ctx')
- router_second_new: float32 [1536, 32], P('ctx')
- router_new: float32 [1536, 32], P('ctx')
- gains_first_new: float32 [2, 1536], P(None, 'ctx')
- gains_second_new: float32 [2, 1536], P(None, 'ctx')
- gains_new: float32 [2, 1536], P(None, 'ctx')
The draws below stay inside these ranges and needn't reach their ends.
Inputs may be any that keep to these rules, and one draw needn't show every extreme that they name: `expert_choice`: each row names 4 different experts; within the rows of one index of dp and ctx (aligned blocks of 256 rows) no expert is named more than 36 times, and some expert reaches 36. `segments`: within a sequence document numbers never fall; one document holds 1793 positions.
All inputs are finite; a program needn't handle non-finite values.
Results may differ from the reference program's by a relative error of at most 0.035.
Values may be sent and summed in bfloat16 or wider, within the bound.
A program may use at most 192 MiB of HBM per device.

```python
import math
import jax
import jax.numpy as jnp
import numpy as np
from jax import lax

D = 1536
KV_HEADS = 2
HEAD_DIM = 128
FF = 768
TOP = 4
TOK_DEV = 256
DOCS = 4
STEP = 10
NS_STEPS = 5
EXPERTS = 32
GROUP_Q = 6
SLOTS = 14
LENGTH = 2048
SEQS = 8
TOKENS = 16384
CAP = 36


def draw_expert_weights(key, part):
    key = jax.random.fold_in(key, 11)
    base = jax.random.truncated_normal(key, -6.0, 6.0, (EXPERTS, 3, D, FF), jnp.float32)
    scales = jnp.array([D ** (-0.5), D ** (-0.5), 4.0 * FF ** (-0.5)], jnp.float32)
    return base * scales[None, :, None, None]


def draw_expert_moment(key, part):
    key = jax.random.fold_in(key, 23)
    base = jax.random.truncated_normal(key, -6.0, 6.0, (EXPERTS, 3, D, FF), jnp.float32)
    scales = jnp.array([0.8, 0.8, 0.15], jnp.float32) * (TOKENS * TOP // EXPERTS) ** 0.5
    return base * scales[None, :, None, None]


def draw_attention_weights(key, part):
    key = jax.random.fold_in(key, 37)
    base = jax.random.truncated_normal(key, -6.0, 6.0, (KV_HEADS, SLOTS, D, HEAD_DIM), jnp.float32)
    scales = jnp.where(jnp.arange(SLOTS) >= GROUP_Q + 2, 0.25, D ** (-0.5)).astype(jnp.float32)
    return base * scales[None, :, None, None]


def steps_of(stream_key, extent, cuts, low, high):
    level, own = 1.0, jax.random.fold_in(stream_key, 6)
    for dim, blocks in cuts:
        draws = jnp.exp(jax.random.uniform(jax.random.fold_in(own, dim), (blocks,), jnp.float32, low / len(cuts), high / len(cuts)))
        level = level * jnp.repeat(draws, extent[dim] // blocks).reshape([-1 if axis == dim else 1 for axis in range(len(extent))])
    return level


def profile(count, total, limit, slope):
    loads = [(1 << 20) // math.isqrt(grade ** slope) + 1 for grade in range(2, count + 1)]
    spare, given = total - limit - (count - 1), [1] * (count - 1)
    while spare > 0:
        free = [i for i in range(count - 1) if given[i] < limit]
        pool, left = sum([loads[i] for i in free]), spare
        for i in free:
            extra = min(limit - given[i], max(1, left * loads[i] // pool), spare)
            given[i] = given[i] + extra
            spare = spare - extra
    return np.array([limit] + given)


def ragged_sizes(rng, count, total, most, lean):
    if count == 2:
        one = jax.random.randint(rng, (), max(1, total - most), min(most, total - 1) + 1)
        return jnp.stack([one, total - one])
    tallies = jnp.asarray(profile(count, total, most, lean), jnp.int32)
    twos = (count - 1) // 2
    giver, receiver = tallies[1:1 + 2 * twos:2], tallies[2:2 + 2 * twos:2]
    room = jnp.minimum(giver - 1, most - receiver)
    moved = jax.random.randint(jax.random.fold_in(rng, 1), (twos,), 0, 1 << 20) % (room + 1)
    tallies = tallies.at[1:1 + 2 * twos:2].set(giver - moved).at[2:2 + 2 * twos:2].set(receiver + moved)
    return tallies[jax.random.permutation(jax.random.fold_in(rng, 2), count)]


def assign_block(rng, own, number, rows, count, top, most, lean):
    sequence = jax.random.permutation(rng, count)
    heavy_load, ordinary = portions_of(count, rows * top, most, lean, True), portions_of(count, rows * top, most, lean, False)
    places = jnp.arange(count)

    def named(tallies, turn):
        used = int((tallies > 0).sum())
        fixed = max(1, used // 4)
        shifted = fixed + (places - fixed + turn * (used - fixed)) % max(1, count - fixed)
        return jnp.zeros((count,), jnp.int32).at[sequence[jnp.where(places < fixed, places, shifted)]].set(jnp.asarray(tallies, jnp.int32))

    tallies = jnp.where(number % 4 == 0, named(heavy_load, number // 4), named(ordinary, number - number // 4 - 1))
    mixed = jax.random.permutation(jax.random.fold_in(own, 3), count)
    giver, sink = mixed[0:count // 2 * 2:2], mixed[1:count // 2 * 2:2]
    room = jnp.minimum(tallies[giver] - 1, most - tallies[sink]) // 2
    room = jnp.where((giver == sequence[0]) | (sink == sequence[0]) | (tallies[sink] == 0), 0, jnp.maximum(room, 0))
    shifted = jax.random.randint(jax.random.fold_in(own, 4), (count // 2,), 0, 1 << 20) % (room + 1)
    tallies = tallies.at[giver].add(-shifted).at[sink].add(shifted)
    items = jnp.searchsorted(jnp.cumsum(tallies), jnp.arange(rows * top), side="right").astype(jnp.int32)
    listing = items.reshape(top, rows).T
    listing = listing[jax.random.permutation(jax.random.fold_in(own, 1), rows)]
    turn = jax.random.randint(jax.random.fold_in(own, 2), (rows, 1), 0, top)
    return jnp.take_along_axis(listing, (jnp.arange(top)[None, :] + turn) % top, axis=1)


def portions_of(count, total, reach, skew, full):
    weights = [(1 << 20) // math.isqrt(rank ** skew) + 1 for rank in range(1, count + 1)]
    largest = reach if full else min(reach, max(-(-total // count), total * weights[0] // sum(weights)))
    least = 1 if total - largest >= count - 1 else 0
    holding, rest = [largest] + [least] * (count - 1), total - largest - least * (count - 1)
    while rest > 0:
        movable = [i for i in range(1, count) if holding[i] < largest] or [i for i in range(1, count) if holding[i] < reach]
        mass, left = sum([weights[i] for i in movable]), rest
        for i in movable:
            addition = min(reach - holding[i], max(1, left * weights[i] // mass), rest)
            holding[i] = holding[i] + addition
            rest = rest - addition
    return np.array(holding)


def bell_draw(rng, dims, scale, reach, shards=(), kind=jnp.bfloat16):
    factor_of = steps_of(rng, dims, shards, -0.22, 0.18) if shards else 1.0
    result = jax.random.normal(rng, dims, jnp.float32) * scale * factor_of
    return jnp.minimum(jnp.maximum(result, -reach), reach).astype(kind)


def setup_inputs(seed: int = 0) -> dict:
    splits = jax.random.split(jax.random.key(seed), 16)
    hidden_in = bell_draw(splits[0], (TOKENS, D), 1.0, 6.0, ((0, 64),), jnp.float32)
    out_grad = bell_draw(splits[1], (TOKENS, D), 1.0, 6.0, ((0, 64),), jnp.float32)
    expert_choice_keys = jax.random.split(jax.random.fold_in(splits[2], 1), TOKENS // TOK_DEV)
    expert_choice_turns = jax.random.permutation(jax.random.fold_in(splits[2], 3), TOKENS // TOK_DEV)
    expert_choice = jax.vmap(lambda own, number: assign_block(jax.random.fold_in(splits[2], 2), own, number, TOK_DEV, EXPERTS, TOP, CAP, 1))(expert_choice_keys, expert_choice_turns).reshape((TOKENS, TOP))
    segments = jax.vmap(lambda own: jnp.searchsorted(jnp.cumsum(ragged_sizes(own, DOCS, LENGTH, LENGTH - TOK_DEV + 1, 0)), jnp.arange(LENGTH), side="right"))(jax.random.split(splits[3], SEQS)).reshape((SEQS, LENGTH)).astype(jnp.int32)
    expert_weights = draw_expert_weights(jax.random.fold_in(splits[15], 71), 0)
    expert_moment = draw_expert_moment(jax.random.fold_in(splits[15], 71), 0)
    attention_weights = draw_attention_weights(jax.random.fold_in(splits[15], 71), 0)
    attention_first = bell_draw(splits[7], (KV_HEADS, SLOTS, D, HEAD_DIM), (0.033 * TOKENS ** 0.5), 24.0, ((0, 2), (2, 8)), jnp.float32)
    attention_second = jnp.clip(jnp.exp(math.log(294.912) - 1.8971199 * jax.random.uniform(splits[8], (KV_HEADS, SLOTS, D, HEAD_DIM), jnp.float32) ** steps_of(splits[8], (KV_HEADS, SLOTS, D, HEAD_DIM), ((0, 2), (2, 8)), -0.2, 0.2)), 44.2368, 294.912)
    router_weights = bell_draw(splits[9], (D, EXPERTS), (4 * D) ** -0.5, 0.078125, ((0, 8),), jnp.float32)
    router_first = bell_draw(splits[10], (D, EXPERTS), (2.2 * (TOKENS * TOP // EXPERTS) ** 0.5), 640.0, ((0, 8),), jnp.float32)
    router_second = jnp.clip(jnp.exp(math.log(163840.0) - 1.89712 * jax.random.uniform(splits[11], (D, EXPERTS), jnp.float32) ** steps_of(splits[11], (D, EXPERTS), ((0, 8),), -0.2, 0.2)), 24576.0, 163840.0)
    norm_gains = jnp.clip(1.0 + 0.1 * jax.random.normal(splits[12], (2, D), jnp.float32), 0.5, 1.5)
    gains_first = bell_draw(splits[13], (2, D), (0.22 * TOKENS ** 0.5), 160.0, ((1, 8),), jnp.float32)
    gains_second = jnp.clip(jnp.exp(math.log(13107.2) - 1.89712 * jax.random.uniform(splits[14], (2, D), jnp.float32) ** steps_of(splits[14], (2, D), ((1, 8),), -0.2, 0.2)), 1966.08, 13107.2)
    return dict(hidden_in=hidden_in, out_grad=out_grad, expert_choice=expert_choice, segments=segments, expert_weights=expert_weights, expert_moment=expert_moment, attention_weights=attention_weights, attention_first=attention_first, attention_second=attention_second, router_weights=router_weights, router_first=router_first, router_second=router_second, norm_gains=norm_gains, gains_first=gains_first, gains_second=gains_second)


HIGH = lax.Precision.HIGHEST
NORM_EPS = 1e-06
MUON_RATES = (0.15, 0.15, 0.6)
MUON_DECAY = 0.1
NS_A = 3.4445
NS_B = -4.775
NS_C = 2.0315

@jax.custom_vjp
def low(v):
    return lax.optimization_barrier(v.astype(jnp.bfloat16)).astype(jnp.float32)

@jax.custom_vjp
def low_back(v):
    return v

def low_keep(v):
    return (low(v), None)

def low_pass(kept, grad):
    return (grad,)

def back_keep(v):
    return (v, None)

def back_low(kept, grad):
    return (low(grad),)
low.defvjp(low_keep, low_pass)
low_back.defvjp(back_keep, back_low)

def round_both(value):
    return low(low_back(value))

def rms_norm(value, gain):
    inverse = lax.rsqrt(lax.optimization_barrier(jnp.mean(value * value, axis=-1, keepdims=True)) + NORM_EPS)
    return value * inverse * gain

def sequence_attention(queries, keys, values, segment_row):
    raw_scores = low_back(jnp.einsum('qgjc,kgc->gjqk', queries, keys, precision=HIGH))
    scores = raw_scores * HEAD_DIM ** (-0.5)
    places = jnp.arange(LENGTH, dtype=jnp.int32)
    allowed = (places[None, :] <= places[:, None]) & (segment_row[None, :] == segment_row[:, None])
    weights = jax.nn.softmax(jnp.where(allowed, scores, -1e+30), axis=-1)
    return jnp.einsum('gjqk,kgc->qgjc', low(weights), values, precision=HIGH)

def routing_tables(expert_choice):
    block_total = TOKENS // TOK_DEV
    chosen = expert_choice.reshape(block_total, TOK_DEV * TOP).astype(jnp.int32)
    onehot = (chosen[:, :, None] == jnp.arange(EXPERTS, dtype=jnp.int32)[None, None, :]).astype(jnp.int32)
    before = jnp.cumsum(onehot, axis=1, dtype=jnp.int32) - onehot
    slot_index = lax.optimization_barrier(jnp.sum(before * onehot, axis=-1, dtype=jnp.int32))
    block_ids = jnp.arange(block_total, dtype=jnp.int32)[:, None]
    position = (chosen * (block_total * CAP) + block_ids * CAP + slot_index).reshape(-1).astype(jnp.int32)
    token_ids = jnp.repeat(jnp.arange(TOKENS, dtype=jnp.int32), TOP)
    route_table = jnp.zeros((EXPERTS * block_total * CAP,), jnp.int32).at[position].set(token_ids)
    return (position, route_table.reshape(EXPERTS, block_total * CAP))

def forward(hidden_in, expert_weights, attention_weights, router_weights, norm_gains, expert_choice, position, route_table, segments):
    expert_low = low(expert_weights)
    attention_low = low(attention_weights)
    router_low = low(router_weights)
    gains_low = low(norm_gains)
    normed_a = low(rms_norm(hidden_in, gains_low[0]))
    query_w = attention_low[:, :GROUP_Q]
    key_w = attention_low[:, GROUP_Q]
    value_w = attention_low[:, GROUP_Q + 1]
    output_w = attention_low[:, GROUP_Q + 2:]
    queries = round_both(jnp.einsum('td,gjdc->tgjc', normed_a, query_w, precision=HIGH))
    keys = round_both(jnp.einsum('td,gdc->tgc', normed_a, key_w, precision=HIGH))
    values = round_both(jnp.einsum('td,gdc->tgc', normed_a, value_w, precision=HIGH))
    checked = jax.checkpoint(sequence_attention)
    heads = lax.map(lambda pieces: checked(*pieces), (queries.reshape(SEQS, LENGTH, KV_HEADS, GROUP_Q, HEAD_DIM), keys.reshape(SEQS, LENGTH, KV_HEADS, HEAD_DIM), values.reshape(SEQS, LENGTH, KV_HEADS, HEAD_DIM), segments))
    heads = round_both(heads.reshape(TOKENS, KV_HEADS, GROUP_Q, HEAD_DIM))
    attention_out = low_back(jnp.einsum('tgjc,gjdc->td', heads, output_w, precision=HIGH))
    resid = hidden_in + attention_out
    normed_b = low(rms_norm(resid, gains_low[1]))
    logits = jnp.dot(normed_b, router_low, precision=HIGH)
    picked = jnp.take_along_axis(logits, expert_choice, axis=1)
    gates = jax.nn.softmax(picked, axis=-1)

    def one_expert(pieces):
        weights, row_ids = pieces
        rows = normed_b[row_ids]
        gate_pre = low_back(jnp.dot(rows, weights[0], precision=HIGH))
        up_pre = low_back(jnp.dot(rows, weights[1], precision=HIGH))
        hidden = low(jax.nn.gelu(gate_pre) * up_pre)
        return jnp.dot(hidden, weights[2].T, precision=HIGH)
    expert_out = lax.map(jax.checkpoint(one_expert), (expert_low, route_table))
    expert_out = low_back(expert_out.reshape(-1, D)[position].reshape(TOKENS, TOP, D))
    return resid + lax.optimization_barrier(jnp.sum(gates[:, :, None] * expert_out, axis=1))

def orthogonalize(matrix):
    frob = jnp.sqrt(jnp.sum(matrix * matrix))
    current = low(matrix / (frob + 1e-07))
    for turn_number in range(NS_STEPS):
        gram = low(jnp.dot(current.T, current, precision=HIGH))
        square = jnp.dot(gram, gram, precision=HIGH)
        mixer = low(NS_B * gram + NS_C * square)
        current = NS_A * current + jnp.dot(current, mixer, precision=HIGH)
        if turn_number + 1 < NS_STEPS:
            current = low(current)
    return current

def adam_update(weight, first, second, grad, rate, decay):
    first_new = 0.9 * first + 0.1 * grad
    second_new = 0.95 * second + 0.05 * grad * grad
    corrected = first_new / (1.0 - 0.9 ** STEP)
    denominator = jnp.sqrt(second_new / (1.0 - 0.95 ** STEP)) + 1e-08
    return (first_new, second_new, weight * (1.0 - rate * decay) - rate * corrected / denominator)

def reference(hidden_in, out_grad, expert_choice, segments, expert_weights, expert_moment, attention_weights, attention_first, attention_second, router_weights, router_first, router_second, norm_gains, gains_first, gains_second):
    position, route_table = routing_tables(expert_choice)

    def run(hidden_value, expert_value, attention_value, router_value, gains_value):
        return forward(hidden_value, expert_value, attention_value, router_value, gains_value, expert_choice, position, route_table, segments)
    layer_output, pull = jax.vjp(run, hidden_in, expert_weights, attention_weights, router_weights, norm_gains)
    input_grad, expert_grad, attention_grad, router_grad, gains_grad = pull(out_grad)
    moment_new = 0.95 * expert_moment + expert_grad
    ortho = lax.map(orthogonalize, moment_new.reshape(EXPERTS * 3, D, FF)).reshape(EXPERTS, 3, D, FF)
    rates = jnp.array(MUON_RATES, jnp.float32)[None, :, None, None]
    expert_new = expert_weights * (1.0 - rates * MUON_DECAY) - rates * (0.2 * max(D, FF) ** 0.5) * ortho
    slot_rates = jnp.where(jnp.arange(SLOTS) >= GROUP_Q + 2, 0.5, 0.05)[None, :, None, None]
    attention_first_new, attention_second_new, attention_new = adam_update(attention_weights, attention_first, attention_second, attention_grad, slot_rates, 0.1)
    router_first_new, router_second_new, router_new = adam_update(router_weights, router_first, router_second, router_grad, 0.025, 0.1)
    gains_first_new, gains_second_new, gains_new = adam_update(norm_gains, gains_first, gains_second, gains_grad, 1.0, 0.0)
    return (layer_output, input_grad, moment_new, expert_new, attention_first_new, attention_second_new, attention_new, router_first_new, router_second_new, router_new, gains_first_new, gains_second_new, gains_new)
```

```python
import functools

import jax
import jax.numpy as jnp
from jax import lax
from jax.experimental import pallas as pl
from jax.experimental.pallas import tpu as pltpu
from jax.sharding import PartitionSpec as P

MESH = pl.DeviceIdType.MESH
F32 = jnp.float32
BF16 = jnp.bfloat16
EPS = 1e-06
TOK = 256
D = 1536
FF = 768
ROWS = 192
HALF = 384
SCALE = 128.0 ** (-0.5)
MiB = 2**20


def dot(a, b):
    return jnp.dot(a, b, preferred_element_type=F32)


def dot_nt(a, b):
    return lax.dot_general(a, b, (((1,), (1,)), ((), ())), preferred_element_type=F32)


def dot_tn(a, b):
    return lax.dot_general(a, b, (((0,), (0,)), ((), ())), preferred_element_type=F32)


def iota(shape, axis):
    return lax.broadcasted_iota(jnp.int32, shape, axis)


def remote(src, dst, send_sem, recv_sem, **device):
    return pltpu.make_async_remote_copy(
        src_ref=src,
        dst_ref=dst,
        send_sem=send_sem,
        recv_sem=recv_sem,
        device_id=device,
        device_id_type=MESH,
    )


def place():
    ctx = lax.axis_index("ctx")
    return lax.axis_index("dp"), ctx, lax.axis_index("tensor"), lax.div(ctx, 2), lax.rem(ctx, 2)


def row_to_column(row):
    n = row.shape[1]
    same = iota((n, n), 0) == iota((n, n), 1)
    return jnp.sum(jnp.where(same, row, jnp.zeros_like(row)), axis=1, keepdims=True)


def codes_by_expert(choice_rows):
    expert = iota((32, TOK), 0)
    hit = jnp.zeros((32, TOK), F32)
    for k in range(4):
        hit = hit + jnp.where(choice_rows[k : k + 1, :] == expert, 1.0, 0.0)
    before = jnp.where(iota((TOK, TOK), 0) < iota((TOK, TOK), 1), 1.0, 0.0).astype(BF16)
    slot = dot(hit.astype(BF16), before)
    return jnp.where(hit > 0.5, slot, -1.0)


def codes_by_token(choice_rows):
    expert = iota((TOK, 128), 1)
    hit = jnp.zeros((TOK, 128), F32)
    for k in range(4):
        hit = hit + jnp.where(row_to_column(choice_rows[k : k + 1, :]) == expert, 1.0, 0.0)
    before = jnp.where(iota((TOK, TOK), 0) > iota((TOK, TOK), 1), 1.0, 0.0).astype(BF16)
    slot = dot(before, hit.astype(BF16))
    return hit, jnp.where(hit > 0.5, slot, -1.0)


def fill_onehot(code_ref, main_ref, left_ref):
    def one(e, carry):
        code = code_ref[pl.ds(e, 1), :]
        main_ref[pl.ds(pl.multiple_of(e * 32, 32), 32), :] = jnp.where(
            iota((32, TOK), 0).astype(F32) == code, 1.0, 0.0
        ).astype(BF16)
        left_ref[pl.ds(pl.multiple_of(e * 16, 16), 16), :] = jnp.where(
            (32 + lax.rem(iota((16, TOK), 0), 4)).astype(F32) == code, 1.0, 0.0
        ).astype(BF16)
        return carry

    lax.fori_loop(0, 32, one, 0)


def pack_rows(onehot_main, onehot_left, rows_ref, out_main, out_left):
    width = rows_ref.shape[1]

    def main_block(b, carry):
        at = pl.ds(pl.multiple_of(b * 256, 256), 256)
        out_main[at, :] = dot(onehot_main[at, :], rows_ref[...]).astype(BF16)
        return carry

    lax.fori_loop(0, 4, main_block, 0)

    def left_block(b, carry):
        at = pl.ds(pl.multiple_of(b * 256, 256), 256)
        quarter = lax.rem(lax.div(iota((256, HALF), 0), 4), 4)
        total = jnp.zeros((256, HALF), F32)
        for q in range(4):
            piece = dot(onehot_left[at, :], rows_ref[:, q * HALF : (q + 1) * HALF])
            total = total + jnp.where(quarter == q, piece, 0.0)
        out_left[at, 0:HALF] = total.astype(BF16)
        if width > D:
            out_left[at, HALF:] = dot(onehot_left[at, :], rows_ref[:, D:]).astype(BF16)
        return carry

    lax.fori_loop(0, 2, left_block, 0)


def send_rows(src_main, src_left, dst_main, dst_left, send_sem, recv_sem):
    dp, ctx, ten, z, c = place()
    core = lax.rem(z, 2)
    source = dp * 2 + lax.div(z, 2)

    def one(e, carry):
        to_dp, to_z = lax.div(e, 4), lax.rem(e, 4)
        here = (to_dp == dp) & (to_z == z) & (c == core)
        for i, (src, dst, n) in enumerate(((src_main, dst_main, 32), (src_left, dst_left, 16))):
            src_at = src.at[pl.ds(pl.multiple_of(e * n, n), n)]
            dst_at = dst.at[pl.ds(pl.multiple_of(source * n, n), n)]

            @pl.when(here)
            def _(i=i, src_at=src_at, dst_at=dst_at):
                pltpu.make_async_copy(src_at, dst_at, recv_sem.at[i, source]).start()

            @pl.when(jnp.logical_not(here))
            def _(i=i, src_at=src_at, dst_at=dst_at):
                remote(
                    src_at,
                    dst_at,
                    send_sem.at[i, e],
                    recv_sem.at[i, source],
                    dp=to_dp,
                    ctx=to_z * 2 + core,
                    tensor=ten,
                ).start()

        return carry

    lax.fori_loop(0, 32, one, 0)


def wait_sent_rows(src_main, src_left, dst_main, dst_left, send_sem, recv_sem):
    dp, ctx, ten, z, c = place()

    def one(e, carry):
        here = (lax.div(e, 4) == dp) & (lax.rem(e, 4) == z) & (c == lax.rem(z, 2))

        @pl.when(jnp.logical_not(here))
        def _():
            for i, (src, dst, n) in enumerate(((src_main, dst_main, 32), (src_left, dst_left, 16))):
                remote(
                    src.at[pl.ds(pl.multiple_of(e * n, n), n)],
                    dst.at[pl.ds(0, n)],
                    send_sem.at[i, e],
                    recv_sem.at[i, 0],
                    dp=dp,
                    ctx=ctx,
                    tensor=1 - ten,
                ).wait_send()

        return carry

    lax.fori_loop(0, 32, one, 0)


def wait_received_rows(src_main, src_left, dst_main, dst_left, send_sem, recv_sem):
    dp, ctx, ten, z, c = place()

    def one(s, carry):
        for i, (src, dst, n) in enumerate(((src_main, dst_main, 32), (src_left, dst_left, 16))):
            remote(
                src.at[pl.ds(0, n)],
                dst.at[pl.ds(pl.multiple_of(s * n, n), n)],
                send_sem.at[i, 0],
                recv_sem.at[i, s],
                dp=dp,
                ctx=ctx,
                tensor=1 - ten,
            ).wait_recv()
        return carry

    lax.fori_loop(0, 16, one, 0)


def greet_row_senders(barrier):
    dp, ctx, ten, z, c = place()
    main = c == ten

    def one(s, carry):
        from_dp, from_z = lax.div(s, 2), lax.rem(s, 2) * 2 + c
        here = main & (from_dp == dp) & (from_z == z)

        @pl.when(jnp.logical_not(here))
        def _():
            pl.semaphore_signal(
                barrier,
                inc=1,
                device_id={"dp": from_dp, "ctx": from_z * 2 + ten, "tensor": ten},
                device_id_type=MESH,
            )

        return carry

    lax.fori_loop(0, 16, one, 0)
    self_in = (c == lax.rem(z, 2)).astype(jnp.int32)
    return jnp.where(main, 32 - self_in, 0)


PAIRS = (3, 0, 1, 2, 4, 5, 6)


def forward_kernel(
    hid_ref,
    og_ref,
    choice_ref,
    seg_ref,
    aw_ref,
    rw_ref,
    gains_ref,
    elow_ref,
    q_ref,
    kv_ref,
    heads_ref,
    lse_ref,
    w_ref,
    resid_ref,
    nba_ref,
    nbb_ref,
    gate_ref,
    gain_ref,
    router_ref,
    wexp_ref,
    xmain_ref,
    xleft_ref,
    ogmain_ref,
    ogleft_ref,
    ws,
    rs,
    gs,
    grecv,
    bias,
    code_ref,
    onehot_main,
    onehot_left,
    nbx,
    ogl,
    send_main,
    send_left,
    send_ogmain,
    send_ogleft,
    part,
    prec,
    w_s,
    w_r,
    wf_s,
    wf_r,
    sm_s,
    sm_r,
    kv_s,
    kv_r,
    kvf_s,
    kvf_r,
    pe_s,
    pe_r,
    og_s,
    og_r,
    x_s,
    x_r,
    wz_s,
    wz_r,
    wy_s,
    wy_r,
    wc_s,
    wc_r,
):
    dp, ctx, ten, z, c = place()
    main = c == ten
    core_peer = z * 2 + 1 - c

    def z_peer(d):
        return lax.rem(z + d, 4) * 2 + c

    barrier = pltpu.get_barrier_semaphore()
    for j in range(1, 8):
        pl.semaphore_signal(
            barrier, inc=1, device_id={"ctx": lax.rem(ctx + j, 8)}, device_id_type=MESH
        )
    pl.semaphore_signal(barrier, inc=1, device_id={"tensor": 1 - ten}, device_id_type=MESH)
    extra = greet_row_senders(barrier)

    for p in range(7):
        ws[p, :, 0:128] = aw_ref[0, 2 * p].astype(BF16)
        ws[p, :, 128:256] = aw_ref[0, 2 * p + 1].astype(BF16)
    rs[...] = jnp.zeros_like(rs)
    rs[:, 0:32] = rw_ref[...].astype(BF16)
    shift = jnp.where(iota((ROWS, D), 1) == iota((ROWS, D), 0) + ctx * ROWS, 1.0, 0.0).astype(BF16)
    gs[...] = jnp.zeros_like(gs)
    gs[0:2, :] = dot(gains_ref[...].astype(BF16), shift)

    pl.semaphore_wait(barrier, 8 + extra)

    def rows_at(index):
        return pl.ds(pl.multiple_of(index * ROWS, 64), ROWS)

    small = []
    for j in range(1, 8):
        to = lax.rem(ctx + j, 8)
        for i, (src, dst) in enumerate(
            ((gs, grecv.at[j - 1]), (rs, router_ref.at[rows_at(ctx)]))
        ):
            copy = remote(src, dst, sm_s.at[i, j - 1], sm_r.at[i, j - 1], ctx=to)
            copy.start()
            small.append(copy)
    weight_copies = {}
    for p in PAIRS:
        dst = w_ref.at[p, rows_at(ctx)]
        for d in (1, 3, 2, 0):
            to = core_peer if d == 0 else z_peer(d)
            copy = remote(ws.at[p], dst, w_s.at[p, d], w_r.at[p, d], ctx=to)
            copy.start()
            weight_copies[p, d] = copy
        w_ref[p, rows_at(ctx), :] = ws[p]
    router_ref[rows_at(ctx), :] = rs[...]

    choice = choice_ref[...]
    hit, _ = codes_by_token(choice)

    @pl.when(main)
    def _():
        code_ref[...] = codes_by_expert(choice)
        fill_onehot(code_ref, onehot_main, onehot_left)
        ogl[...] = og_ref[...].astype(BF16)
        pack_rows(onehot_main, onehot_left, ogl, send_ogmain, send_ogleft)

    seg_here = seg_ref[:, pl.ds(pl.multiple_of(ctx * TOK, TOK), TOK)]
    seg_col = row_to_column(seg_here)
    for b in range(8):
        at = slice(b * 256, (b + 1) * 256)
        key_pos = b * 256 + iota((TOK, 256), 1)
        query_pos = ctx * TOK + iota((TOK, 256), 0)
        allowed = (key_pos <= query_pos) & (seg_ref[:, at] == seg_col)
        bias[:, at] = jnp.where(allowed, 0.0, -1e30)

    for copy in small:
        copy.wait_recv()
    gain_ref[...] = gs[...]
    for j in range(7):
        gain_ref[...] += grecv[j]
    hid = hid_ref[...]
    inverse = lax.rsqrt(jnp.mean(hid * hid, axis=1, keepdims=True) + EPS)
    nba_ref[...] = (hid * inverse * gain_ref[0:1, :]).astype(BF16)

    forwards = {}

    def take_pair(p):
        for d in (1, 3, 2):
            weight_copies[p, d].wait_recv()
            share = w_ref.at[p, rows_at(lax.rem(z + 4 - d, 4) * 2 + c)]
            copy = remote(share, share, wf_s.at[p, d - 1], wf_r.at[p, d - 1], ctx=core_peer)
            copy.start()
            forwards[p, d] = copy
        weight_copies[p, 0].wait_recv()
        for d in (1, 3, 2):
            forwards[p, d].wait_recv()

    def kv_rows(index):
        return kv_ref.at[pl.ds(pl.multiple_of(index * TOK, TOK), TOK)]

    take_pair(3)
    kv_ref[pl.ds(pl.multiple_of(ctx * TOK, TOK), TOK), :] = dot(nba_ref[...], w_ref[3]).astype(BF16)
    kv_copies = []
    for d in (1, 3, 2, 0):
        to = core_peer if d == 0 else z_peer(d)
        copy = remote(kv_rows(ctx), kv_rows(ctx), kv_s.at[d], kv_r.at[d], ctx=to)
        copy.start()
        kv_copies.append(copy)
    for p in range(3):
        take_pair(p)
        q_ref[p] = dot(nba_ref[...], w_ref[p]).astype(BF16)

    for d, copy in zip((1, 3, 2), kv_copies):
        copy.wait_recv()
        rows = kv_rows(lax.rem(z + 4 - d, 4) * 2 + c)
        fcopy = remote(rows, rows, kvf_s.at[d - 1], kvf_r.at[d - 1], ctx=core_peer)
        fcopy.start()
        forwards["kv", d] = fcopy
    kv_copies[3].wait_recv()
    for d in (1, 3, 2):
        forwards["kv", d].wait_recv()

    og_args = (send_ogmain, send_ogleft, ogmain_ref, ogleft_ref, og_s, og_r)
    x_args = (send_main, send_left, xmain_ref, xleft_ref, x_s, x_r)

    @pl.when(main)
    def _():
        send_rows(*og_args)

    cols = pl.ds(pl.multiple_of(ten * HALF, 128), HALF)
    spread = {}
    for k in range(3):
        for d in range(4):
            to_z = lax.rem(z + d, 4)
            src, dst = elow_ref.at[to_z, k], wexp_ref.at[k, z, c, :, cols]
            if d == 0:
                copy = pltpu.make_async_copy(src, dst, wz_r.at[k, 0])
            else:
                copy = remote(src, dst, wz_s.at[k, d], wz_r.at[k, d], ctx=z_peer(d))
            copy.start()
            spread[k, d] = copy

    lse_ref[...] = jnp.zeros_like(lse_ref)
    outgoing = []
    for half in range(2):
        at = slice(half * 128, (half + 1) * 128)
        for j in range(6):
            lanes = slice((j % 2) * 128, (j % 2) * 128 + 128)
            scores = dot_nt(q_ref[j // 2, at, lanes], kv_ref[:, 0:128]) * SCALE + bias[at, :]
            top = jnp.max(scores, axis=1, keepdims=True)
            terms = jnp.exp(scores - top)
            total = jnp.sum(terms, axis=1, keepdims=True)
            mixed = dot(terms.astype(BF16), kv_ref[:, 128:256]) / total
            heads_ref[j // 2, at, lanes] = mixed.astype(BF16)
            lse_ref[at, :] = jnp.where(
                iota((128, 128), 1) == j, top + jnp.log(total), lse_ref[at, :]
            )
        if half == 0:
            for p in (4, 5, 6):
                take_pair(p)
        total = dot_nt(heads_ref[0, at, :], w_ref[4])
        total = total + dot_nt(heads_ref[1, at, :], w_ref[5])
        total = total + dot_nt(heads_ref[2, at, :], w_ref[6])
        part[at, :] = total.astype(BF16)
        copy = remote(part.at[at], prec.at[at], pe_s.at[half], pe_r.at[half], tensor=1 - ten)
        outgoing.append(copy)

        @pl.when(jnp.logical_not(main))
        def _(copy=copy):
            copy.start()

    for k in range(3):
        for d in range(4):
            if d == 0:
                spread[k, d].wait()
            else:
                spread[k, d].wait_recv()
        own = wexp_ref.at[k, :, c, :, cols]
        spread[k, "y"] = remote(own, own, wy_s.at[k], wy_r.at[k], tensor=1 - ten)
        spread[k, "c"] = remote(own, own, wc_s.at[k, 0], wc_r.at[k, 0], ctx=core_peer)
        spread[k, "y"].start()
        spread[k, "c"].start()

    for copy in outgoing:

        @pl.when(main)
        def _(copy=copy):
            copy.wait_recv()
            copy.start()

        @pl.when(jnp.logical_not(main))
        def _(copy=copy):
            copy.wait_recv()

    resid = hid_ref[...] + (part[...].astype(F32) + prec[...].astype(F32))
    resid_ref[...] = resid
    inverse = lax.rsqrt(jnp.mean(resid * resid, axis=1, keepdims=True) + EPS)
    nbb = (resid * inverse * gain_ref[1:2, :]).astype(BF16)
    nbb_ref[...] = nbb
    logits = jnp.where(hit > 0.5, dot(nbb, router_ref[...]), -1e30)
    top = jnp.max(logits, axis=1, keepdims=True)
    terms = jnp.where(hit > 0.5, jnp.exp(logits - top), 0.0)
    gates = terms / jnp.sum(terms, axis=1, keepdims=True)
    gate_ref[...] = gates

    @pl.when(main)
    def _():
        nbx[:, 0:D] = nbb
        high = gates.astype(BF16).astype(F32)
        nbx[:, D:] = (high + pltpu.roll(gates - high, 32, 1)).astype(BF16)
        pack_rows(onehot_main, onehot_left, nbx, send_main, send_left)
        send_rows(*x_args)

    for k in range(3):
        spread[k, "y"].wait_recv()
        there = wexp_ref.at[k, :, c, :, pl.ds(pl.multiple_of((1 - ten) * HALF, 128), HALF)]
        spread[k, "cy"] = remote(there, there, wc_s.at[k, 1], wc_r.at[k, 1], ctx=core_peer)
        spread[k, "cy"].start()
    for k in range(3):
        spread[k, "c"].wait_recv()
        spread[k, "cy"].wait_recv()
        for d in (1, 2, 3):
            spread[k, d].wait_send()
        for name in ("y", "c", "cy"):
            spread[k, name].wait_send()
    wait_received_rows(*og_args)
    wait_received_rows(*x_args)

    @pl.when(main)
    def _():
        wait_sent_rows(*og_args)
        wait_sent_rows(*x_args)

    for copy in small + list(weight_copies.values()) + list(forwards.values()) + kv_copies:
        copy.wait_send()
    for copy in outgoing:
        copy.wait_send()


def sems(*shape):
    return pltpu.SemaphoreType.DMA(shape)


def run_forward(hid, og, choice_rows, seg, aw, rw, gains, elow):
    vmem = pl.BlockSpec(memory_space=pltpu.VMEM)
    hbm = pl.BlockSpec(memory_space=pl.ANY)
    S = jax.ShapeDtypeStruct
    outs = [
        S((3, TOK, 256), BF16),
        S((2048, 256), BF16),
        S((3, TOK, 256), BF16),
        S((TOK, 128), F32),
        S((7, D, 256), BF16),
        S((TOK, D), F32),
        S((TOK, D), BF16),
        S((TOK, D), BF16),
        S((TOK, 128), F32),
        S((8, D), F32),
        S((D, 128), BF16),
        S((3, 4, 2, ROWS, FF), BF16),
        S((512, D + 128), BF16),
        S((256, HALF + 128), BF16),
        S((512, D), BF16),
        S((256, HALF), BF16),
    ]
    V = pltpu.VMEM
    return pl.pallas_call(
        forward_kernel,
        out_shape=outs,
        in_specs=[vmem] * 7 + [hbm],
        out_specs=[vmem] * 11 + [hbm] * 5,
        scratch_shapes=[
            V((7, ROWS, 256), BF16),
            V((ROWS, 128), BF16),
            V((8, D), F32),
            V((7, 8, D), F32),
            V((TOK, 2048), F32),
            V((32, TOK), F32),
            V((1024, TOK), BF16),
            V((512, TOK), BF16),
            V((TOK, D + 128), BF16),
            V((TOK, D), BF16),
            V((1024, D + 128), BF16),
            V((512, HALF + 128), BF16),
            V((1024, D), BF16),
            V((512, HALF), BF16),
            V((TOK, D), BF16),
            V((TOK, D), BF16),
            sems(7, 4),
            sems(7, 4),
            sems(7, 3),
            sems(7, 3),
            sems(2, 7),
            sems(2, 7),
            sems(4),
            sems(4),
            sems(3),
            sems(3),
            sems(2),
            sems(2),
            sems(2, 32),
            sems(2, 16),
            sems(2, 32),
            sems(2, 16),
            sems(3, 4),
            sems(3, 4),
            sems(3),
            sems(3),
            sems(3, 2),
            sems(3, 2),
        ],
        compiler_params=pltpu.CompilerParams(
            collective_id=0, has_side_effects=True, vmem_limit_bytes=56 * MiB
        ),
        name="attention_forward",
    )(hid, og, choice_rows, seg, aw, rw, gains, elow)
GATE, UP, DOWN = 0, 1, 2
OWNER_PLANE = (0, 1, 0)
OWNER_CORE = (0, 1, 1)
CORE_SLOT = (0, 0, 1)
GELU_A = 0.7978845608028654
GELU_B = 0.044715


def is_owner(c, ten):
    return jnp.logical_not((c == 0) & (ten == 1))


def half_columns(index):
    return pl.ds(pl.multiple_of(index * HALF, 128), HALF)


def greet_group(barrier):
    _, ctx, ten, _, _ = place()
    for j in range(8):
        for t in range(2):
            if j or t:
                pl.semaphore_signal(
                    barrier,
                    inc=1,
                    device_id={"ctx": lax.rem(ctx + j, 8), "tensor": lax.rem(ten + t, 2)},
                    device_id_type=MESH,
                )


def send_block(src, dst, send_sem, recv_sem, to_ctx, to_ten):
    _, ctx, ten, _, _ = place()
    here = (ctx == to_ctx) & (ten == to_ten)

    @pl.when(here)
    def _():
        pltpu.make_async_copy(src, dst, recv_sem).start()

    @pl.when(jnp.logical_not(here))
    def _():
        remote(src, dst, send_sem, recv_sem, ctx=to_ctx, tensor=to_ten).start()


def wait_block_sent(src, dst, send_sem, recv_sem, to_ctx, to_ten):
    _, ctx, ten, _, _ = place()
    here = (ctx == to_ctx) & (ten == to_ten)

    @pl.when(jnp.logical_not(here))
    def _():
        remote(src, dst, send_sem, recv_sem, ctx=to_ctx, tensor=to_ten).wait_send()


def wait_block_received(block, send_sem, recv_sem):
    _, ctx, ten, _, _ = place()
    remote(block, block, send_sem, recv_sem, ctx=ctx, tensor=1 - ten).wait_recv()


def return_rows(src_main, src_left, dst_main, dst_left, send_sem, recv_sem):
    dp, ctx, ten, z, c = place()
    expert = dp * 4 + z

    def one(s, carry):
        to_dp, to_z = lax.div(s, 2), lax.rem(s, 2) * 2 + c
        here = (to_dp == dp) & (to_z == z) & (c == ten)
        for i, (src, dst, n) in enumerate(((src_main, dst_main, 32), (src_left, dst_left, 16))):
            src_at = src.at[pl.ds(pl.multiple_of(s * n, n), n)]
            dst_at = dst.at[pl.ds(pl.multiple_of(expert * n, n), n)]

            @pl.when(here)
            def _(i=i, src_at=src_at, dst_at=dst_at):
                pltpu.make_async_copy(src_at, dst_at, recv_sem.at[i, expert]).start()

            @pl.when(jnp.logical_not(here))
            def _(i=i, src_at=src_at, dst_at=dst_at):
                remote(
                    src_at,
                    dst_at,
                    send_sem.at[i, s],
                    recv_sem.at[i, expert],
                    dp=to_dp,
                    ctx=to_z * 2 + ten,
                    tensor=ten,
                ).start()

        return carry

    lax.fori_loop(0, 16, one, 0)


def wait_returned(src_main, src_left, dst_main, dst_left, send_sem, recv_sem):
    dp, ctx, ten, z, c = place()

    def one(e, carry):
        for i, (src, dst, n) in enumerate(((src_main, dst_main, 32), (src_left, dst_left, 16))):
            remote(
                src.at[pl.ds(0, n)],
                dst.at[pl.ds(pl.multiple_of(e * n, n), n)],
                send_sem.at[i, 0],
                recv_sem.at[i, e],
                dp=dp,
                ctx=ctx,
                tensor=1 - ten,
            ).wait_recv()
        return carry

    lax.fori_loop(0, 32, one, 0)


def wait_return_sent(src_main, src_left, dst_main, dst_left, send_sem, recv_sem):
    dp, ctx, ten, z, c = place()

    def one(s, carry):
        here = (lax.div(s, 2) == dp) & (lax.rem(s, 2) * 2 + c == z) & (c == ten)

        @pl.when(jnp.logical_not(here))
        def _():
            for i, (src, dst, n) in enumerate(((src_main, dst_main, 32), (src_left, dst_left, 16))):
                remote(
                    src.at[pl.ds(pl.multiple_of(s * n, n), n)],
                    dst.at[pl.ds(0, n)],
                    send_sem.at[i, s],
                    recv_sem.at[i, 0],
                    dp=dp,
                    ctx=ctx,
                    tensor=1 - ten,
                ).wait_send()

        return carry

    lax.fori_loop(0, 16, one, 0)


def greet_expert_devices(barrier):
    dp, ctx, ten, z, c = place()
    core = lax.rem(z, 2)

    def one(e, carry):
        to_dp, to_z = lax.div(e, 4), lax.rem(e, 4)
        here = (to_dp == dp) & (to_z == z) & (c == core)

        @pl.when(jnp.logical_not(here))
        def _():
            pl.semaphore_signal(
                barrier,
                inc=1,
                device_id={"dp": to_dp, "ctx": to_z * 2 + core, "tensor": ten},
                device_id_type=MESH,
            )

        return carry

    @pl.when(c == ten)
    def _():
        lax.fori_loop(0, 32, one, 0)

    return 16 - ((c == ten) & (core == c)).astype(jnp.int32)


def left_picker(quarter):
    row, col = iota((64, 256), 0), iota((64, 256), 1)
    return jnp.where(col == lax.div(row, 4) * 16 + quarter * 4 + lax.rem(row, 4), 1.0, 0.0).astype(
        BF16
    )


def left_packer(quarter):
    row, col = iota((256, 64), 0), iota((256, 64), 1)
    return jnp.where(row == lax.div(col, 4) * 16 + quarter * 4 + lax.rem(col, 4), 1.0, 0.0).astype(
        BF16
    )


def fill_token_onehot(code, main_ref, left_ref):
    code = code.astype(BF16)
    for b in range(4):
        expert, col = iota((128, 256), 0), iota((128, 256), 1) + b * 256
        spread = dot(code, jnp.where(lax.div(col, 32) == expert, 1.0, 0.0).astype(BF16))
        slot = lax.rem(iota((TOK, 256), 1), 32).astype(F32)
        main_ref[:, b * 256 : (b + 1) * 256] = jnp.where(spread == slot, 1.0, 0.0).astype(BF16)
    for b in range(2):
        expert, col = iota((128, 256), 0), iota((128, 256), 1) + b * 256
        spread = dot(code, jnp.where(lax.div(col, 16) == expert, 1.0, 0.0).astype(BF16))
        slot = (32 + lax.rem(iota((TOK, 256), 1), 4)).astype(F32)
        left_ref[:, b * 256 : (b + 1) * 256] = jnp.where(spread == slot, 1.0, 0.0).astype(BF16)


def left_quarter(left_ref, quarter):
    keep = lax.rem(lax.div(iota((TOK, 512), 1), 4), 4) == quarter
    return jnp.where(keep, left_ref[...].astype(F32), 0.0).astype(BF16)


def backward_kernel(
    choice_ref,
    seg_ref,
    gate_ref,
    lse_ref,
    gain_ref,
    router_ref,
    xmain_h,
    xleft_h,
    ogmain_h,
    ogleft_h,
    wexp_h,
    w_h,
    q_h,
    kv_h,
    heads_h,
    nba_h,
    nbb_h,
    resid_h,
    og_h,
    mlow_h,
    dw_h,
    gres_ref,
    gna_ref,
    gnap_ref,
    msum_ref,
    mom_h,
    omain_h,
    oleft_h,
    xall,
    gx,
    xleft,
    ogall,
    ogleft,
    w9,
    ggp,
    gup,
    hidden,
    ghid,
    gmain,
    gleft,
    omain,
    oleft,
    dw9,
    rcore,
    ry,
    cmain,
    cleft,
    ptm,
    ptl,
    ext,
    extr,
    kv,
    q,
    heads,
    nba,
    nbb,
    resid,
    og,
    gheads,
    dq,
    dkv,
    rkv,
    skv,
    r2kv,
    stage,
    ld,
    lw,
    dw_s,
    g_s,
    g_r,
    o_s,
    o_r,
    mc_s,
    mc_r,
    my_s,
    my_r,
    e_s,
    e_r,
    k1_s,
    k1_r,
    k2_s,
    k2_r,
    gn_s,
    gn_r,
    mo_s,
    mo_r,
):
    dp, ctx, ten, z, c = place()
    main = c == ten
    core_peer = z * 2 + 1 - c
    expert = dp * 4 + z

    def z_peer(d):
        return lax.rem(z + d, 4) * 2 + c

    barrier = pltpu.get_barrier_semaphore()
    greet_group(barrier)
    extra = greet_expert_devices(barrier)

    loads = [
        pltpu.make_async_copy(xmain_h.at[:, 0:D], xall.at[0:512], ld.at[0]),
        pltpu.make_async_copy(xmain_h.at[:, D:], gx.at[0:512], ld.at[1]),
        pltpu.make_async_copy(xleft_h, xleft, ld.at[2]),
        pltpu.make_async_copy(ogmain_h, ogall.at[0:512], ld.at[3]),
        pltpu.make_async_copy(ogleft_h, ogleft, ld.at[4]),
    ]
    expert_loads = []
    for n in range(3):
        for k in range(3):
            expert_loads.append(
                pltpu.make_async_copy(
                    wexp_h.at[k, :, n * 256 : (n + 1) * 256], w9.at[3 * k + n], lw.at[3 * k + n]
                )
            )
    later = [
        pltpu.make_async_copy(src, dst, ld.at[5 + i])
        for i, (src, dst) in enumerate(
            (
                (kv_h, kv),
                (q_h, q),
                (heads_h, heads),
                (nba_h, nba),
                (nbb_h, nbb),
                (resid_h, resid),
                (og_h, og),
            )
        )
    ]
    for copy in loads + expert_loads + later:
        copy.start()

    @pl.when(main)
    def _():
        _, code = codes_by_token(choice_ref[...])
        fill_token_onehot(code, ptm, ptl)

    for copy in loads:
        copy.wait()
    for n in range(4):
        at = slice(n * HALF, (n + 1) * HALF)
        pick = left_picker(n)
        xall[512:576, at] = dot(pick, xleft[:, 0:HALF]).astype(BF16)
        ogall[512:576, at] = dot(pick, ogleft[...]).astype(BF16)
    gx[512:576, :] = dot(left_picker(0), xleft[:, HALF:]).astype(BF16)
    lane = iota((576, 128), 1)
    mine = (lane == expert) | (lane == expert + 32)
    gate = jnp.sum(jnp.where(mine, gx[...].astype(F32), 0.0), axis=1, keepdims=True)

    pl.semaphore_wait(barrier, 15 + extra)
    for i in range(4):
        for k in range(3):
            send_block(
                mlow_h.at[i, k],
                mom_h.at[z, c, :, half_columns(ten)],
                mo_s.at[i, k],
                mo_r.at[ctx * 2 + ten],
                2 * i + OWNER_CORE[k],
                OWNER_PLANE[k],
            )

    grad_gate = jnp.zeros((576, 1), F32)
    for n in range(3):
        for k in range(3):
            expert_loads[3 * n + k].wait()
        at = slice(n * 256, (n + 1) * 256)
        pre = dot(xall[...], w9[n])
        up = dot(xall[...], w9[3 + n])
        back = dot(ogall[...], w9[6 + n])
        bent = jnp.tanh(GELU_A * (pre + GELU_B * pre * pre * pre))
        value = 0.5 * pre * (1.0 + bent)
        slope = 0.5 * (1.0 + bent) + 0.5 * pre * (1.0 - bent * bent) * GELU_A * (
            1.0 + 3.0 * GELU_B * pre * pre
        )
        hid = (value * up).astype(BF16).astype(F32)
        grad_gate = grad_gate + jnp.sum(hid * back, axis=1, keepdims=True)
        scaled = back * gate
        ghid[:, at] = (hid * gate).astype(BF16)
        ggp[:, at] = (scaled * up * slope).astype(BF16)
        gup[:, at] = (scaled * value).astype(BF16)

    high = grad_gate.astype(BF16).astype(F32)
    marks = jnp.where(lane == expert, high, jnp.where(lane == expert + 32, grad_gate - high, 0.0))
    marks = marks.astype(BF16)
    gmain[:, D:] = marks[0:512]
    gleft[:, HALF:] = dot(left_packer(0), marks[512:576]).astype(BF16)
    packed = jnp.zeros((256, HALF), F32)
    for m in range(4):
        at = slice(m * HALF, (m + 1) * HALF)
        total = jnp.zeros((576, HALF), F32)
        for n in range(3):
            cols = slice(n * 256, (n + 1) * 256)
            total = total + dot_nt(ggp[:, cols], w9[n, at, :])
            total = total + dot_nt(gup[:, cols], w9[3 + n, at, :])
        gmain[:, at] = total[0:512].astype(BF16)
        packed = packed + dot(left_packer(m), total[512:576].astype(BF16))
    gleft[:, 0:HALF] = packed.astype(BF16)
    g_args = (gmain, gleft, cmain, cleft, g_s, g_r)
    o_args = (omain, oleft, omain_h, oleft_h, o_s, o_r)
    return_rows(*g_args)

    core_copies, plane_copies = {}, {}
    order = [(k, n) for k in (GATE, DOWN, UP) for n in range(3)]
    for k, n in order:
        at = slice(n * 256, (n + 1) * 256)
        rows, right = (ogall, ghid) if k == DOWN else (xall, ggp if k == GATE else gup)
        dw9[3 * k + n] = dot_tn(rows[...], right[:, at]).astype(BF16)
        copy = remote(
            dw9.at[3 * k + n],
            rcore.at[CORE_SLOT[k], n],
            mc_s.at[k, n],
            mc_r.at[k, n],
            ctx=core_peer,
        )
        core_copies[k, n] = copy

        @pl.when(c != OWNER_CORE[k])
        def _(copy=copy):
            copy.start()

    packed = jnp.zeros((256, HALF), F32)
    for m in range(4):
        at = slice(m * HALF, (m + 1) * HALF)
        total = jnp.zeros((576, HALF), F32)
        for n in range(3):
            total = total + dot_nt(ghid[:, n * 256 : (n + 1) * 256], w9[6 + n, at, :])
        omain[:, at] = total[0:512].astype(BF16)
        packed = packed + dot(left_packer(m), total[512:576].astype(BF16))
    oleft[...] = packed.astype(BF16)

    for k, n in order:
        copy = remote(
            dw9.at[3 * k + n], ry.at[n], my_s.at[k, n], my_r.at[k, n], tensor=1 - ten
        )
        plane_copies[k, n] = copy

        @pl.when(c == OWNER_CORE[k])
        def _(k=k, n=n, copy=copy):
            core_copies[k, n].wait_recv()
            dw9[3 * k + n] = (
                dw9[3 * k + n].astype(F32) + rcore[CORE_SLOT[k], n].astype(F32)
            ).astype(BF16)

            @pl.when(ten != OWNER_PLANE[k])
            def _():
                copy.start()

    return_rows(*o_args)

    weight_loads = [pltpu.make_async_copy(w_h.at[p], w9.at[p], lw.at[p]) for p in range(7)]
    for copy in weight_loads:
        copy.start()

    @pl.when(main)
    def _():
        wait_returned(*g_args)
        extras = dot(ptm[...], cmain[:, D:]) + dot(left_quarter(ptl, 0), cleft[:, HALF:])
        grads = jnp.where(iota((TOK, 128), 1) < 32, extras + pltpu.roll(extras, 96, 1), 0.0)
        gates = gate_ref[...]
        grad_logits = gates * (grads - jnp.sum(gates * grads, axis=1, keepdims=True))
        high = grad_logits.astype(BF16)
        low = (grad_logits - high.astype(F32)).astype(BF16)
        ext[:, D:] = (high.astype(F32) + pltpu.roll(low.astype(F32), 32, 1)).astype(BF16)
        for m in range(4):
            at = slice(m * HALF, (m + 1) * HALF)
            total = dot(ptm[...], cmain[:, at]) + dot(left_quarter(ptl, m), cleft[:, 0:HALF])
            total = total + dot_nt(high, router_ref[at, :]) + dot_nt(low, router_ref[at, :])
            ext[:, at] = total.astype(BF16)

    share = remote(ext, extr, e_s, e_r, tensor=1 - ten)

    @pl.when(main)
    def _():
        share.start()
        share.wait_send()

    @pl.when(jnp.logical_not(main))
    def _():
        share.wait_recv()
        ext[...] = extr[...]

    for copy in later:
        copy.wait()
    gnb = ext[:, 0:D].astype(F32)
    value = resid[...]
    inverse = lax.rsqrt(jnp.mean(value * value, axis=1, keepdims=True) + EPS)
    scaled = gnb * gain_ref[1:2, :]
    inner = jnp.mean(scaled * value, axis=1, keepdims=True)
    gres_ref[...] = og[...] + inverse * scaled - value * (inverse * inverse * inverse) * inner
    gatt = gres_ref[...].astype(BF16)
    flat = gnb * value * inverse
    flat_high = flat.astype(BF16)
    flat_low = (flat - flat_high.astype(F32)).astype(BF16)
    ones = jnp.where(iota((TOK, 128), 1) == 32, 1.0, 0.0).astype(BF16)
    both = ext[:, D:].astype(F32)
    logit_part = jnp.where(iota((TOK, 128), 1) < 32, both, 0.0).astype(BF16)
    logit_low = jnp.where(iota((TOK, 128), 1) < 32, pltpu.roll(both, 96, 1), 0.0).astype(BF16)
    slab = dot_tn(nbb[...], logit_part) + dot_tn(nbb[...], logit_low)
    slab = slab + dot_tn(flat_high, ones) + dot_tn(flat_low, ones)
    slab = jnp.concatenate([slab, jnp.zeros((D, 128), F32)], axis=1).astype(BF16)

    stores = {}

    def store(p, value):
        if p < 4:
            stores[p + 4].wait()
        stage[p % 4] = value
        stores[p] = pltpu.make_async_copy(stage.at[p % 4], dw_h.at[p], dw_s.at[p])
        stores[p].start()

    for copy in weight_loads:
        copy.wait()
    store(7, slab)
    terms = jnp.zeros((TOK, 128), F32)
    for p in range(3):
        gheads[p] = dot(gatt, w9[4 + p]).astype(BF16)
        store(4 + p, dot_tn(gatt, heads[p]).astype(BF16))
        prod = gheads[p].astype(F32) * heads[p].astype(F32)
        for i in range(2):
            term = jnp.sum(prod[:, i * 128 : (i + 1) * 128], axis=1, keepdims=True)
            terms = jnp.where(iota((TOK, 128), 1) == 2 * p + i, term, terms)
    lse_rows = jnp.transpose(lse_ref[...])
    term_rows = jnp.transpose(terms)
    dkv[...] = jnp.zeros_like(dkv)
    dq[...] = jnp.zeros_like(dq)
    seg_here = seg_ref[:, pl.ds(pl.multiple_of(ctx * TOK, TOK), TOK)]

    def key_block(b, carry):
        at = pl.ds(pl.multiple_of(b * TOK, TOK), TOK)
        seg_col = row_to_column(seg_ref[:, at])
        key_pos = b * TOK + iota((TOK, TOK), 0)
        query_pos = ctx * TOK + iota((TOK, TOK), 1)
        allowed = (key_pos <= query_pos) & (seg_here == seg_col)
        keys, values = kv[at, 0:128], kv[at, 128:256]
        dk = jnp.zeros((TOK, 128), F32)
        dv = jnp.zeros((TOK, 128), F32)
        for j in range(6):
            lanes = slice((j % 2) * 128, (j % 2) * 128 + 128)
            qj, gj = q[j // 2, :, lanes], gheads[j // 2, :, lanes]
            scores = dot_nt(keys, qj) * SCALE
            probs = jnp.where(allowed, jnp.exp(scores - lse_rows[j : j + 1, :]), 0.0)
            grad = dot_nt(values, gj)
            grad_scores = (probs * (grad - term_rows[j : j + 1, :]) * SCALE).astype(BF16)
            dv = dv + dot(probs.astype(BF16), gj)
            dk = dk + dot(grad_scores, qj)
            dq[j // 2, :, lanes] += dot_tn(grad_scores, keys)
        dkv[at, 0:128] = dk.astype(BF16)
        dkv[at, 128:256] = dv.astype(BF16)
        return carry

    lax.fori_loop(0, ctx + 1, key_block, 0)

    pair = []
    for to_z in range(4):
        src = dkv.at[pl.ds(pl.multiple_of((to_z * 2 + 1 - c) * TOK, TOK), TOK)]
        copy = remote(src, rkv.at[to_z], k1_s.at[to_z], k1_r.at[to_z], ctx=core_peer)
        copy.start()
        pair.append(copy)
    for p in range(3):
        store(p, dot_tn(nba[...], dq[p].astype(BF16)).astype(BF16))
    total = dot_nt(dq[0].astype(BF16), w9[0])
    total = total + dot_nt(dq[1].astype(BF16), w9[1])
    total = total + dot_nt(dq[2].astype(BF16), w9[2])
    for to_z in range(4):
        pair[to_z].wait_recv()
        own = dkv[pl.ds(pl.multiple_of((to_z * 2 + c) * TOK, TOK), TOK), :]
        skv[to_z] = (own.astype(F32) + rkv[to_z].astype(F32)).astype(BF16)
    ring = []
    for d in (1, 3, 2):
        copy = remote(
            skv.at[lax.rem(z + d, 4)], r2kv.at[d - 1], k2_s.at[d - 1], k2_r.at[d - 1], ctx=z_peer(d)
        )
        copy.start()
        ring.append(copy)
    for copy in ring:
        copy.wait_recv()
    gkv = skv[z].astype(F32) + r2kv[0].astype(F32) + r2kv[1].astype(F32) + r2kv[2].astype(F32)
    gkv = gkv.astype(BF16)
    store(3, dot_tn(nba[...], gkv).astype(BF16))
    total = total + dot_nt(gkv, w9[3])
    gna_ref[...] = total.astype(BF16)
    swap = remote(gna_ref, gnap_ref, gn_s, gn_r, tensor=1 - ten)
    swap.start()

    for k in range(3):
        for n in range(3):
            plane = plane_copies[k, n]

            @pl.when((c == OWNER_CORE[k]) & (ten == OWNER_PLANE[k]))
            def _(k=k, n=n, plane=plane):
                plane.wait_recv()
                msum_ref[:, n * 256 : (n + 1) * 256] = (
                    dw9[3 * k + n].astype(F32) + ry[n].astype(F32)
                ).astype(BF16)

            @pl.when((c == OWNER_CORE[k]) & (ten != OWNER_PLANE[k]))
            def _(plane=plane):
                plane.wait_send()

            @pl.when(c != OWNER_CORE[k])
            def _(k=k, n=n):
                core_copies[k, n].wait_send()

    @pl.when((c == 0) & (ten == 1))
    def _():
        msum_ref[...] = jnp.zeros_like(msum_ref)

    for i in range(4):
        for k in range(3):
            wait_block_sent(
                mlow_h.at[i, k],
                mom_h.at[z, c, :, half_columns(ten)],
                mo_s.at[i, k],
                mo_r.at[ctx * 2 + ten],
                2 * i + OWNER_CORE[k],
                OWNER_PLANE[k],
            )

    @pl.when(is_owner(c, ten))
    def _():
        for index in range(16):
            wait_block_received(mlow_h.at[0, 0], mo_s.at[0, 0], mo_r.at[index])

    swap.wait()
    for copy in pair + ring:
        copy.wait_send()
    wait_return_sent(*g_args)
    wait_return_sent(*o_args)

    @pl.when(main)
    def _():
        wait_returned(*o_args)

    for p in range(4):
        stores[p].wait()


def run_backward(choice_rows, seg, fwd, og, mlow):
    (q, kv, heads, lse, w, resid, nba, nbb, gate, gain, router, wexp, xm, xl, om, ol) = fwd
    vmem = pl.BlockSpec(memory_space=pltpu.VMEM)
    hbm = pl.BlockSpec(memory_space=pl.ANY)
    S = jax.ShapeDtypeStruct
    V = pltpu.VMEM
    return pl.pallas_call(
        backward_kernel,
        out_shape=[
            S((8, D, 256), BF16),
            S((TOK, D), F32),
            S((TOK, D), BF16),
            S((TOK, D), BF16),
            S((D, FF), BF16),
            S((4, 2, ROWS, FF), BF16),
            S((1024, D), BF16),
            S((512, HALF), BF16),
        ],
        in_specs=[vmem] * 6 + [hbm] * 14,
        out_specs=[hbm, vmem, vmem, vmem, vmem, hbm, hbm, hbm],
        scratch_shapes=[
            V((576, D), BF16),
            V((576, 128), BF16),
            V((256, HALF + 128), BF16),
            V((576, D), BF16),
            V((256, HALF), BF16),
            V((9, D, 256), BF16),
            V((576, FF), BF16),
            V((576, FF), BF16),
            V((8, 128), BF16),
            V((576, FF), BF16),
            V((512, D + 128), BF16),
            V((256, HALF + 128), BF16),
            V((512, D), BF16),
            V((256, HALF), BF16),
            V((9, D, 256), BF16),
            V((2, 3, D, 256), BF16),
            V((3, D, 256), BF16),
            V((1024, D + 128), BF16),
            V((512, HALF + 128), BF16),
            V((TOK, 1024), BF16),
            V((TOK, 512), BF16),
            V((TOK, D + 128), BF16),
            V((TOK, D + 128), BF16),
            V((2048, 256), BF16),
            V((3, TOK, 256), BF16),
            V((3, TOK, 256), BF16),
            V((TOK, D), BF16),
            V((TOK, D), BF16),
            V((TOK, D), F32),
            V((TOK, D), F32),
            V((3, TOK, 256), BF16),
            V((3, TOK, 256), F32),
            V((2048, 256), BF16),
            V((4, TOK, 256), BF16),
            V((4, TOK, 256), BF16),
            V((3, TOK, 256), BF16),
            V((4, D, 256), BF16),
            sems(12),
            sems(9),
            sems(8),
            sems(2, 16),
            sems(2, 32),
            sems(2, 16),
            sems(2, 32),
            sems(3, 3),
            sems(3, 3),
            sems(3, 3),
            sems(3, 3),
            pltpu.SemaphoreType.DMA,
            pltpu.SemaphoreType.DMA,
            sems(4),
            sems(4),
            sems(3),
            sems(3),
            pltpu.SemaphoreType.DMA,
            pltpu.SemaphoreType.DMA,
            sems(4, 3),
            sems(16),
        ],
        compiler_params=pltpu.CompilerParams(
            collective_id=1, has_side_effects=True, vmem_limit_bytes=63 * MiB
        ),
        name="backward",
    )(
        choice_rows, seg, gate, lse, gain, router, xm, xl, om, ol, wexp.reshape(3, D, FF),
        w, q, kv, heads, nba, nbb, resid, og, mlow,
    )
NS_A = 3.4445
NS_B = -4.775
NS_C = 2.0315
MUON_RATES = (0.15, 0.15, 0.6)


def update_kernel(
    choice_ref,
    hid_ref,
    gain_ref,
    gna_ref,
    gnap_ref,
    msum_ref,
    mom_ref,
    dw_h,
    omain_h,
    oleft_h,
    fin_ref,
    term_ref,
    moe_ref,
    ghome_h,
    ohome_h,
    own,
    r1,
    r2,
    r3,
    s2,
    slab,
    omain,
    oleft,
    ptm,
    ptl,
    moe_send,
    ns_x,
    ns_b,
    ns_m,
    ld,
    a_s,
    a_r,
    b_s,
    b_r,
    c_s,
    c_r,
    d_s,
    d_r,
    l_s,
    l_r,
    gh_s,
    gh_r,
    oh_s,
    oh_r,
):
    dp, ctx, ten, z, c = place()
    main = c == ten
    core_peer = z * 2 + 1 - c

    def z_peer(d):
        return lax.rem(z + d, 4) * 2 + c

    barrier = pltpu.get_barrier_semaphore()
    greet_group(barrier)
    for j in range(1, 8):
        pl.semaphore_signal(
            barrier, inc=1, device_id={"dp": lax.rem(dp + j, 8)}, device_id_type=MESH
        )

    loads = [
        pltpu.make_async_copy(dw_h.at[7], slab, ld.at[0]),
        pltpu.make_async_copy(omain_h, omain, ld.at[1]),
        pltpu.make_async_copy(oleft_h, oleft, ld.at[2]),
    ]
    own_loads = []
    for p in range(7):
        for to_z in range(4):
            rows = pl.ds(pl.multiple_of((to_z * 2 + c) * ROWS, 64), ROWS)
            own_loads.append(
                pltpu.make_async_copy(dw_h.at[p, rows], own.at[p, to_z], ld.at[3 + p * 4 + to_z])
            )
    for copy in loads + own_loads:
        copy.start()

    owner = is_owner(c, ten)

    gna = gna_ref[...].astype(F32) + gnap_ref[...].astype(F32)
    hid = hid_ref[...]
    inverse = lax.rsqrt(jnp.mean(hid * hid, axis=1, keepdims=True) + EPS)
    scaled = gna * gain_ref[0:1, :]
    inner = jnp.mean(scaled * hid, axis=1, keepdims=True)
    term_ref[...] = inverse * scaled - hid * (inverse * inverse * inverse) * inner
    flat = gna * hid * inverse
    high = flat.astype(BF16)
    low = (flat - high.astype(F32)).astype(BF16)
    ones = jnp.where(iota((TOK, 128), 1) == 33, 1.0, 0.0).astype(BF16)
    loads[0].wait()
    slab[:, 0:128] = (slab[:, 0:128].astype(F32) + dot_tn(high, ones) + dot_tn(low, ones)).astype(BF16)

    pl.semaphore_wait(barrier, 22)

    first = {}
    for p in (7, 4, 5, 6, 0, 1, 2, 3):
        for to_z in range(4):
            rows = pl.ds(pl.multiple_of((to_z * 2 + 1 - c) * ROWS, 64), ROWS)
            src = slab.at[rows] if p == 7 else dw_h.at[p, rows]
            first[p, to_z] = remote(
                src, r1.at[p, to_z], a_s.at[p, to_z], a_r.at[p, to_z], ctx=core_peer
            )
            first[p, to_z].start()
    for to_z in range(4):
        rows = pl.ds(pl.multiple_of((to_z * 2 + c) * ROWS, 64), ROWS)
        own[7, to_z] = slab[rows, :]

    def spread(src, dst_h, send_sem, recv_sem, act):
        for k in range(3):

            @pl.when((c == OWNER_CORE[k]) & (ten == OWNER_PLANE[k]))
            def _(k=k):
                for to in range(8):
                    for t in range(2):
                        act(
                            src.at[to * ROWS : (to + 1) * ROWS, t * HALF : (t + 1) * HALF],
                            dst_h.at[z, k],
                            send_sem.at[to, t],
                            recv_sem.at[z, k],
                            to,
                            t,
                        )

    spread(msum_ref, ghome_h, gh_s, gh_r, send_block)

    for copy in own_loads:
        copy.wait()
    second = {}
    for p in (7, 4, 5, 6, 0, 1, 2, 3):
        for to_z in range(4):
            first[p, to_z].wait_recv()
        own[p] = (own[p].astype(F32) + r1[p].astype(F32)).astype(BF16)
        for d in (1, 3, 2):
            second[p, d] = remote(
                own.at[p, lax.rem(z + d, 4)],
                r2.at[p, d - 1],
                b_s.at[p, d - 1],
                b_r.at[p, d - 1],
                ctx=z_peer(d),
            )
            second[p, d].start()

    _, code = codes_by_token(choice_ref[...])
    loads[1].wait()
    loads[2].wait()
    away = remote(moe_send, moe_ref, l_s, l_r, tensor=1 - ten)

    @pl.when(main)
    def _():
        fill_token_onehot(code, ptm, ptl)
        for m in range(4):
            at = slice(m * HALF, (m + 1) * HALF)
            total = dot(ptm[...], omain[:, at]) + dot(left_quarter(ptl, m), oleft[...])
            to = slice((m % 2) * HALF, (m % 2 + 1) * HALF)

            @pl.when(ten == m // 2)
            def _(total=total, to=to):
                moe_ref[:, to] = total.astype(BF16)

            @pl.when(ten != m // 2)
            def _(total=total, to=to):
                moe_send[:, to] = total.astype(BF16)

        away.start()

    @pl.when(owner)
    def _():
        ns_m[...] = mom_ref[...].reshape(D, FF).astype(F32) + msum_ref[...].astype(F32)
        norm = jnp.sqrt(jnp.sum(ns_m[...] * ns_m[...])) + 1e-07
        ns_x[...] = (ns_m[...] / norm).astype(BF16)

    def step(turn, carry):
        @pl.when(owner)
        def _():
            gram = dot_tn(ns_x[...], ns_x[...]).astype(BF16)
            ns_b[...] = gram
            square = dot(ns_b[...], ns_b[...])
            ns_b[...] = (NS_B * ns_b[...].astype(F32) + NS_C * square).astype(BF16)
            for r in range(6):
                at = slice(r * 256, (r + 1) * 256)
                ns_x[at, :] = (
                    NS_A * ns_x[at, :].astype(F32) + dot(ns_x[at, :], ns_b[...])
                ).astype(BF16)

        @pl.when(turn < 4)
        def _():
            for i in range(2):
                p = turn * 2 + i
                total = own[p, z].astype(F32)
                for d in (1, 2, 3):
                    remote(
                        r2.at[p, d - 1], r2.at[p, d - 1], b_s.at[p, d - 1], b_r.at[p, d - 1],
                        ctx=z_peer(d),
                    ).wait_recv()
                    total = total + r2[p, d - 1].astype(F32)
                s2[p] = total.astype(BF16)

                @pl.when(p != dp)
                def _(p=p):
                    remote(s2.at[p], r3.at[dp], c_s.at[p], c_r.at[dp], dp=p).start()

                @pl.when(p == dp)
                def _(p=p):
                    r3[dp] = s2[p]

        @pl.when(turn == 4)
        def _():
            def arrived(s, carry):
                @pl.when(s != dp)
                def _():
                    remote(r3.at[s], r3.at[s], c_s.at[s], c_r.at[s], dp=s).wait_recv()

                return carry

            lax.fori_loop(0, 8, arrived, 0)
            total = r3[0].astype(F32)
            for s in range(1, 8):
                total = total + r3[s].astype(F32)
            fin_ref[dp] = total.astype(BF16)

            def give(j, carry):
                to = lax.rem(dp + j, 8)
                remote(fin_ref.at[dp], fin_ref.at[dp], d_s.at[to], d_r.at[dp], dp=to).start()
                return carry

            lax.fori_loop(1, 8, give, 0)

        return carry

    lax.fori_loop(0, 5, step, 0)

    spread(ns_x, ohome_h, oh_s, oh_r, send_block)

    spread(msum_ref, ghome_h, gh_s, gh_r, wait_block_sent)
    for i in range(4):
        for k in range(3):
            wait_block_received(ghome_h.at[i, k], gh_s.at[0, 0], gh_r.at[i, k])
    for copy in list(first.values()) + list(second.values()):
        copy.wait_send()

    def others(j, carry):
        to = lax.rem(dp + j, 8)
        remote(s2.at[to], r3.at[dp], c_s.at[to], c_r.at[dp], dp=to).wait_send()
        remote(fin_ref.at[dp], fin_ref.at[dp], d_s.at[to], d_r.at[dp], dp=to).wait_send()
        remote(fin_ref.at[to], fin_ref.at[to], d_s.at[to], d_r.at[to], dp=to).wait_recv()
        return carry

    lax.fori_loop(1, 8, others, 0)

    @pl.when(main)
    def _():
        away.wait_send()

    @pl.when(jnp.logical_not(main))
    def _():
        away.wait_recv()

    spread(ns_x, ohome_h, oh_s, oh_r, wait_block_sent)
    for i in range(4):
        for k in range(3):
            wait_block_received(ohome_h.at[i, k], oh_s.at[0, 0], oh_r.at[i, k])


def run_update(choice_rows, hid, gain, bwd):
    dw, gres, gna, gnap, msum, mom, omain, oleft = bwd
    vmem = pl.BlockSpec(memory_space=pltpu.VMEM)
    hbm = pl.BlockSpec(memory_space=pl.ANY)
    S = jax.ShapeDtypeStruct
    V = pltpu.VMEM
    return pl.pallas_call(
        update_kernel,
        out_shape=[
            S((8, ROWS, 256), BF16),
            S((TOK, D), F32),
            S((TOK, FF), BF16),
            S((4, 3, ROWS, HALF), BF16),
            S((4, 3, ROWS, HALF), BF16),
        ],
        in_specs=[vmem] * 7 + [hbm] * 3,
        out_specs=[vmem, vmem, vmem, hbm, hbm],
        scratch_shapes=[
            V((8, 4, ROWS, 256), BF16),
            V((8, 4, ROWS, 256), BF16),
            V((8, 3, ROWS, 256), BF16),
            V((8, ROWS, 256), BF16),
            V((8, ROWS, 256), BF16),
            V((D, 256), BF16),
            V((1024, D), BF16),
            V((512, HALF), BF16),
            V((TOK, 1024), BF16),
            V((TOK, 512), BF16),
            V((TOK, FF), BF16),
            V((D, FF), BF16),
            V((FF, FF), BF16),
            V((D, FF), F32),
            sems(31),
            sems(8, 4),
            sems(8, 4),
            sems(8, 3),
            sems(8, 3),
            sems(8),
            sems(8),
            sems(8),
            sems(8),
            pltpu.SemaphoreType.DMA,
            pltpu.SemaphoreType.DMA,
            sems(8, 2),
            sems(4, 3),
            sems(8, 2),
            sems(4, 3),
        ],
        compiler_params=pltpu.CompilerParams(
            collective_id=2, has_side_effects=True, vmem_limit_bytes=60 * MiB
        ),
        name="update",
    )(choice_rows, hid, gain, gna, gnap, msum, mom, dw, omain, oleft)


def adam_update(weight, first, second, grad, rate, decay):
    first_new = 0.9 * first + 0.1 * grad
    second_new = 0.95 * second + 0.05 * grad * grad
    corrected = first_new / (1.0 - 0.9**10)
    denominator = jnp.sqrt(second_new / (1.0 - 0.95**10)) + 1e-08
    return (first_new, second_new, weight * (1.0 - rate * decay) - rate * corrected / denominator)


def shards(
    hidden_in,
    out_grad,
    expert_choice,
    segments,
    expert_weights,
    expert_moment,
    attention_weights,
    attention_first,
    attention_second,
    router_weights,
    router_first,
    router_second,
    norm_gains,
    gains_first,
    gains_second,
):
    tensor = lax.axis_index("tensor")
    choice_rows = expert_choice.T
    elow = expert_weights.astype(BF16)
    fwd = run_forward(
        hidden_in,
        out_grad,
        choice_rows,
        segments,
        attention_weights,
        router_weights,
        norm_gains,
        elow,
    )
    resid, gain = fwd[5], fwd[9]
    mlow = (0.95 * expert_moment).astype(BF16)
    bwd = run_backward(choice_rows, segments, fwd, out_grad, mlow)
    gres = bwd[1]
    fin, term, moe, ghome, ohome = run_update(choice_rows, hidden_in, gain, bwd)

    layer_output = lax.dynamic_slice_in_dim(resid, tensor * FF, FF, 1) + moe.astype(F32)
    input_grad = gres + term
    moment_new = 0.95 * expert_moment + ghome.astype(F32)
    rates = jnp.array(MUON_RATES, F32)[None, :, None, None]
    expert_new = expert_weights * (1.0 - rates * 0.1) - rates * (0.2 * D**0.5) * ohome.astype(F32)
    slot_rates = jnp.where(jnp.arange(14) >= 8, 0.5, 0.05)[None, :, None, None]
    grads = fin.astype(F32)
    attention_grad = grads[0:7].reshape(7, ROWS, 2, 128).transpose(0, 2, 1, 3)
    attention_out = adam_update(
        attention_weights,
        attention_first,
        attention_second,
        attention_grad.reshape(1, 14, ROWS, 128),
        slot_rates,
        0.1,
    )
    router_out = adam_update(
        router_weights, router_first, router_second, grads[7, :, 0:32], 0.025, 0.1
    )
    gains_grad = jnp.stack([grads[7, :, 33], grads[7, :, 32]])
    gains_out = adam_update(norm_gains, gains_first, gains_second, gains_grad, 1.0, 0.0)
    return (
        layer_output,
        input_grad,
        moment_new,
        expert_new,
        *attention_out,
        *router_out,
        *gains_out,
    )


def solution(mesh):
    tokens = P(("dp", "ctx"), None)
    expert = P("dp", None, "ctx", "tensor")
    attention = P("tensor", None, "ctx", None)
    router = P("ctx", None)
    gains = P(None, "ctx")
    return jax.shard_map(
        shards,
        mesh=mesh,
        in_specs=(
            (tokens,) * 3
            + (P("dp", None),)
            + (expert,) * 2
            + (attention,) * 3
            + (router,) * 3
            + (gains,) * 3
        ),
        out_specs=(
            (P(("dp", "ctx"), "tensor"), tokens)
            + (expert,) * 2
            + (attention,) * 3
            + (router,) * 3
            + (gains,) * 3
        ),
        check_vma=False,
    )
```

```python
import functools

import jax
import jax.numpy as jnp
from jax import lax
from jax.experimental import pallas as pl
from jax.experimental.pallas import tpu as pltpu
from jax.sharding import PartitionSpec as P

MESH = pl.DeviceIdType.MESH
F32 = jnp.float32
BF16 = jnp.bfloat16
EPS = 1e-06
TOK = 256
D = 1536
FF = 768
ROWS = 192
HALF = 384
SCALE = 128.0 ** (-0.5)
MiB = 2**20


def dot(a, b):
    return jnp.dot(a, b, preferred_element_type=F32)


def dot_nt(a, b):
    return lax.dot_general(a, b, (((1,), (1,)), ((), ())), preferred_element_type=F32)


def dot_tn(a, b):
    return lax.dot_general(a, b, (((0,), (0,)), ((), ())), preferred_element_type=F32)


def iota(shape, axis):
    return lax.broadcasted_iota(jnp.int32, shape, axis)


def remote(src, dst, send_sem, recv_sem, **device):
    return pltpu.make_async_remote_copy(
        src_ref=src,
        dst_ref=dst,
        send_sem=send_sem,
        recv_sem=recv_sem,
        device_id=device,
        device_id_type=MESH,
    )


def local(src, dst, sem):
    return pltpu.make_async_copy(src, dst, sem)


def place():
    ctx = lax.axis_index("ctx")
    return lax.axis_index("dp"), ctx, lax.axis_index("tensor"), lax.div(ctx, 2), lax.rem(ctx, 2)


def row_to_column(row):
    n = row.shape[1]
    same = iota((n, n), 0) == iota((n, n), 1)
    return jnp.sum(jnp.where(same, row, jnp.zeros_like(row)), axis=1, keepdims=True)


def codes_by_expert(choice_rows):
    expert = iota((32, TOK), 0)
    hit = jnp.zeros((32, TOK), F32)
    for k in range(4):
        hit = hit + jnp.where(choice_rows[k : k + 1, :] == expert, 1.0, 0.0)
    before = jnp.where(iota((TOK, TOK), 0) < iota((TOK, TOK), 1), 1.0, 0.0).astype(BF16)
    slot = dot(hit.astype(BF16), before)
    return jnp.where(hit > 0.5, slot, -1.0)


def codes_by_token(choice_rows):
    expert = iota((TOK, 128), 1)
    hit = jnp.zeros((TOK, 128), F32)
    for k in range(4):
        hit = hit + jnp.where(row_to_column(choice_rows[k : k + 1, :]) == expert, 1.0, 0.0)
    before = jnp.where(iota((TOK, TOK), 0) > iota((TOK, TOK), 1), 1.0, 0.0).astype(BF16)
    slot = dot(before, hit.astype(BF16))
    return hit, jnp.where(hit > 0.5, slot, -1.0)


def fill_onehot(code_ref, main_ref, left_ref):
    def one(e, carry):
        code = code_ref[pl.ds(e, 1), :]
        main_ref[pl.ds(pl.multiple_of(e * 32, 32), 32), :] = jnp.where(
            iota((32, TOK), 0).astype(F32) == code, 1.0, 0.0
        ).astype(BF16)
        left_ref[pl.ds(pl.multiple_of(e * 16, 16), 16), :] = jnp.where(
            (32 + lax.rem(iota((16, TOK), 0), 4)).astype(F32) == code, 1.0, 0.0
        ).astype(BF16)
        return carry

    lax.fori_loop(0, 32, one, 0)


def pack_rows(onehot_main, onehot_left, rows_ref, out_main, out_left):
    width = rows_ref.shape[1]

    def main_block(b, carry):
        at = pl.ds(pl.multiple_of(b * 256, 256), 256)
        out_main[at, :] = dot(onehot_main[at, :], rows_ref[...]).astype(BF16)
        return carry

    lax.fori_loop(0, 4, main_block, 0)

    def left_block(b, carry):
        at = pl.ds(pl.multiple_of(b * 256, 256), 256)
        quarter = lax.rem(lax.div(iota((256, HALF), 0), 4), 4)
        total = jnp.zeros((256, HALF), F32)
        for q in range(4):
            piece = dot(onehot_left[at, :], rows_ref[:, q * HALF : (q + 1) * HALF])
            total = total + jnp.where(quarter == q, piece, 0.0)
        out_left[at, 0:HALF] = total.astype(BF16)
        if width > D:
            out_left[at, HALF:] = dot(onehot_left[at, :], rows_ref[:, D:]).astype(BF16)
        return carry

    lax.fori_loop(0, 2, left_block, 0)


def plane_for(dp, to_dp, ten):
    return jnp.where(lax.div(dp, 4) == lax.div(to_dp, 4), ten, 1 - ten)


def send_rows(src_main, src_left, dst_main, dst_left, send_sem, recv_sem):
    dp, ctx, ten, z, c = place()
    core = lax.rem(z, 2)
    source = dp * 2 + lax.div(z, 2)

    def one(e, carry):
        to_dp, to_z = lax.div(e, 4), lax.rem(e, 4)
        here = (to_dp == dp) & (to_z == z) & (c == core)
        for i, (src, dst, n) in enumerate(((src_main, dst_main, 32), (src_left, dst_left, 16))):
            src_at = src.at[pl.ds(pl.multiple_of(e * n, n), n)]
            dst_at = dst.at[pl.ds(pl.multiple_of(source * n, n), n)]

            @pl.when(here)
            def _(i=i, src_at=src_at, dst_at=dst_at):
                local(src_at, dst_at, recv_sem.at[i, source]).start()

            @pl.when(jnp.logical_not(here))
            def _(i=i, src_at=src_at, dst_at=dst_at):
                remote(
                    src_at,
                    dst_at,
                    send_sem.at[i, e],
                    recv_sem.at[i, source],
                    dp=to_dp,
                    ctx=to_z * 2 + core,
                    tensor=plane_for(dp, to_dp, ten),
                ).start()

        return carry

    lax.fori_loop(0, 32, one, 0)


def wait_sent_rows(src_main, src_left, dst_main, dst_left, send_sem, recv_sem):
    dp, ctx, ten, z, c = place()

    def one(e, carry):
        here = (lax.div(e, 4) == dp) & (lax.rem(e, 4) == z) & (c == lax.rem(z, 2))

        @pl.when(jnp.logical_not(here))
        def _():
            for i, (src, dst, n) in enumerate(((src_main, dst_main, 32), (src_left, dst_left, 16))):
                remote(
                    src.at[pl.ds(pl.multiple_of(e * n, n), n)],
                    dst.at[pl.ds(0, n)],
                    send_sem.at[i, e],
                    recv_sem.at[i, 0],
                    dp=dp,
                    ctx=ctx,
                    tensor=1 - ten,
                ).wait_send()

        return carry

    lax.fori_loop(0, 32, one, 0)


def wait_received_rows(src_main, src_left, dst_main, dst_left, send_sem, recv_sem):
    dp, ctx, ten, z, c = place()

    def one(s, carry):
        for i, (src, dst, n) in enumerate(((src_main, dst_main, 32), (src_left, dst_left, 16))):
            remote(
                src.at[pl.ds(0, n)],
                dst.at[pl.ds(pl.multiple_of(s * n, n), n)],
                send_sem.at[i, 0],
                recv_sem.at[i, s],
                dp=dp,
                ctx=ctx,
                tensor=1 - ten,
            ).wait_recv()
        return carry

    lax.fori_loop(0, 16, one, 0)


def greet_row_senders(barrier):
    dp, ctx, ten, z, c = place()
    main = c == ten

    def one(s, carry):
        from_dp, from_z = lax.div(s, 2), lax.rem(s, 2) * 2 + c
        plane = plane_for(dp, from_dp, ten)
        here = main & (from_dp == dp) & (from_z == z)

        @pl.when(jnp.logical_not(here))
        def _():
            pl.semaphore_signal(
                barrier,
                inc=1,
                device_id={"dp": from_dp, "ctx": from_z * 2 + plane, "tensor": plane},
                device_id_type=MESH,
            )

        return carry

    lax.fori_loop(0, 16, one, 0)
    self_in = (c == lax.rem(z, 2)).astype(jnp.int32)
    return jnp.where(main, 32 - self_in, 0)


def forward_kernel(
    choice_ref,
    seg_ref,
    rw_ref,
    gains_ref,
    hid_h,
    og_h,
    aw_h,
    ew_h,
    lse_ref,
    gate_ref,
    gain_ref,
    router_ref,
    q_h,
    kv_h,
    heads_h,
    w_h,
    resid_h,
    nba_h,
    nbb_h,
    wexp_ref,
    xmain_ref,
    xleft_ref,
    ogmain_ref,
    ogleft_ref,
    hid_ref,
    og_ref,
    aw_ref,
    ew_ref,
    elow_ref,
    q_ref,
    kv_ref,
    heads_ref,
    w_ref,
    resid_ref,
    nba_ref,
    nbb_ref,
    ld,
    st,
    ws,
    rs,
    gs,
    grecv,
    bias,
    code_ref,
    onehot_main,
    onehot_left,
    nbx,
    ogl,
    send_main,
    send_left,
    send_ogmain,
    send_ogleft,
    part,
    prec,
    za_s,
    za_r,
    xa_s,
    xa_r,
    ca_s,
    ca_r,
    sm_s,
    sm_r,
    kv_s,
    kv_r,
    kvf_s,
    kvf_r,
    pe_s,
    pe_r,
    og_s,
    og_r,
    x_s,
    x_r,
    wz_s,
    wz_r,
    wy_s,
    wy_r,
    wc_s,
    wc_r,
):
    dp, ctx, ten, z, c = place()
    main = c == ten
    core_peer = z * 2 + 1 - c

    def z_peer(d):
        return lax.rem(z + d, 4) * 2 + c

    loads = [
        pltpu.make_async_copy(src, dst, ld.at[i])
        for i, (src, dst) in enumerate(
            ((aw_h, aw_ref), (hid_h, hid_ref), (og_h, og_ref), (ew_h, ew_ref))
        )
    ]
    for copy in loads:
        copy.start()
    stores = []

    def store(src, dst):
        copy = pltpu.make_async_copy(src, dst, st.at[len(stores)])
        copy.start()
        stores.append(copy)

    barrier = pltpu.get_barrier_semaphore()
    for j in range(1, 8):
        pl.semaphore_signal(
            barrier, inc=1, device_id={"ctx": lax.rem(ctx + j, 8)}, device_id_type=MESH
        )
    pl.semaphore_signal(barrier, inc=1, device_id={"tensor": 1 - ten}, device_id_type=MESH)
    for j in range(1, 4):
        pl.semaphore_signal(
            barrier,
            inc=1,
            device_id={"dp": dp - lax.rem(dp, 4) + lax.rem(dp + j, 4)},
            device_id_type=MESH,
        )
    extra = greet_row_senders(barrier)

    loads[0].wait()
    for p in range(7):
        ws[p, :, 0:128] = aw_ref[0, 2 * p].astype(BF16)
        ws[p, :, 128:256] = aw_ref[0, 2 * p + 1].astype(BF16)
    spots = jnp.where(iota((32, 128), 0) == iota((32, 128), 1), 1.0, 0.0).astype(BF16)
    rs[...] = dot_tn(rw_ref[...].astype(BF16), spots).astype(BF16)
    shift = jnp.where(iota((ROWS, D), 1) == iota((ROWS, D), 0) + ctx * ROWS, 1.0, 0.0).astype(BF16)
    gs[...] = jnp.zeros_like(gs)
    gs[0:2, :] = dot(gains_ref[...].astype(BF16), shift)

    pl.semaphore_wait(barrier, 11 + extra)

    def rows_at(index):
        return pl.ds(pl.multiple_of(index * ROWS, 64), ROWS)

    small = []
    for j in range(1, 8):
        to = lax.rem(ctx + j, 8)
        for i, (src, dst) in enumerate(
            ((gs, grecv.at[j - 1]), (rs, router_ref.at[rows_at(ctx)]))
        ):
            copy = remote(src, dst, sm_s.at[i, j - 1], sm_r.at[i, j - 1], ctx=to)
            copy.start()
            small.append(copy)
    router_ref[rows_at(ctx), :] = rs[...]

    groups = ((3, 1), (0, 3), (4, 3))
    xx = lax.rem(dp, 4)
    weight_copies = {}

    def x_peer(j):
        return dp - xx + lax.rem(xx + j, 4)

    def quarter(index):
        return pl.ds(pl.multiple_of(index * ROWS + xx * 48, 16), 48)

    def start_group(g):
        first, count = groups[g]
        pairs = pl.ds(first, count)
        for d in (1, 3, 2):
            copy = remote(
                ws.at[pairs, quarter(0)],
                w_ref.at[pairs, quarter(ctx)],
                za_s.at[g, d - 1],
                za_r.at[g, d - 1],
                ctx=z_peer(d),
            )
            copy.start()
            weight_copies[g, "z", d] = copy
        copy = remote(
            ws.at[pairs], w_ref.at[pairs, rows_at(ctx)], ca_s.at[g, 0], ca_r.at[g, 0], ctx=core_peer
        )
        copy.start()
        weight_copies[g, "c", 0] = copy
        w_ref[first : first + count, rows_at(ctx), :] = ws[first : first + count]

    def spread_group(g):
        pairs = pl.ds(*groups[g])
        for d in (1, 3, 2):
            weight_copies[g, "z", d].wait_recv()
            block = w_ref.at[pairs, quarter(lax.rem(z + 4 - d, 4) * 2 + c)]
            for j in (1, 3, 2):
                copy = remote(
                    block, block, xa_s.at[g, d - 1, j - 1], xa_r.at[g, d - 1, j - 1], dp=x_peer(j)
                )
                copy.start()
                weight_copies[g, "x", d, j] = copy

    def join_group(g):
        first, count = groups[g]
        pairs = pl.ds(first, count)
        for d in (1, 3, 2):
            for j in (1, 3, 2):
                weight_copies[g, "x", d, j].wait_recv()
            share = w_ref.at[pairs, rows_at(lax.rem(z + 4 - d, 4) * 2 + c)]
            copy = remote(share, share, ca_s.at[g, d], ca_r.at[g, d], ctx=core_peer)
            copy.start()
            weight_copies[g, "c", d] = copy
        for d in (0, 1, 3, 2):
            weight_copies[g, "c", d].wait_recv()
        store(w_ref.at[pairs], w_h.at[pairs])

    for g in range(3):
        start_group(g)

    seg_here = seg_ref[:, pl.ds(pl.multiple_of(ctx * TOK, TOK), TOK)]
    seg_col = row_to_column(seg_here)
    for b in range(8):
        at = slice(b * 256, (b + 1) * 256)
        key_pos = b * 256 + iota((TOK, 256), 1)
        query_pos = ctx * TOK + iota((TOK, 256), 0)
        allowed = (key_pos <= query_pos) & (seg_ref[:, at] == seg_col)
        bias[:, at] = jnp.where(allowed, 0.0, -1e30)
    spread_group(0)
    spread_group(1)

    for copy in small:
        copy.wait_recv()
    gain_ref[...] = gs[...]
    for j in range(7):
        gain_ref[...] += grecv[j]
    loads[1].wait()
    hid = hid_ref[...]
    inverse = lax.rsqrt(jnp.mean(hid * hid, axis=1, keepdims=True) + EPS)
    nba_ref[...] = (hid * inverse * gain_ref[0:1, :]).astype(BF16)
    store(nba_ref, nba_h)

    loads[3].wait()
    cols = pl.ds(pl.multiple_of(ten * HALF, 128), HALF)
    spread = {}

    def lower(i, carry):
        elow_ref[i] = ew_ref[i].astype(BF16)
        return carry

    lax.fori_loop(0, 4, lower, 0)

    def send_kind(k):
        for d in range(4):
            to_z = lax.rem(z + d, 4)
            src, dst = elow_ref.at[to_z, k], wexp_ref.at[k, z, c, :, cols]
            if d == 0:
                copy = pltpu.make_async_copy(src, dst, wz_r.at[k, 0])
            else:
                copy = remote(src, dst, wz_s.at[k, d], wz_r.at[k, d], ctx=z_peer(d))
            copy.start()
            spread[k, d] = copy

    def pass_kind(k):
        for d in range(4):
            if d == 0:
                spread[k, d].wait()
            else:
                spread[k, d].wait_recv()
        own = wexp_ref.at[k, :, c, :, cols]
        spread[k, "y"] = remote(own, own, wy_s.at[k], wy_r.at[k], tensor=1 - ten)
        spread[k, "c"] = remote(own, own, wc_s.at[k, 0], wc_r.at[k, 0], ctx=core_peer)
        spread[k, "y"].start()
        spread[k, "c"].start()

    send_kind(0)

    forwards = {}

    def kv_rows(index):
        return kv_ref.at[pl.ds(pl.multiple_of(index * TOK, TOK), TOK)]

    join_group(0)
    kv_ref[pl.ds(pl.multiple_of(ctx * TOK, TOK), TOK), :] = dot(nba_ref[...], w_ref[3]).astype(BF16)
    kv_copies = {}
    for d in (1, 3, 2, 0):
        to = core_peer if d == 0 else z_peer(d)
        copy = remote(kv_rows(ctx), kv_rows(ctx), kv_s.at[d], kv_r.at[d], ctx=to)
        copy.start()
        kv_copies[d] = copy
    spread_group(2)

    choice = choice_ref[...]
    hit, _ = codes_by_token(choice)
    loads[2].wait()

    @pl.when(main)
    def _():
        code_ref[...] = codes_by_expert(choice)
        fill_onehot(code_ref, onehot_main, onehot_left)
        ogl[...] = og_ref[...].astype(BF16)
        pack_rows(onehot_main, onehot_left, ogl, send_ogmain, send_ogleft)

    join_group(1)
    for p in range(3):
        q_ref[p] = dot(nba_ref[...], w_ref[p]).astype(BF16)
    store(q_ref, q_h)

    for d in (1, 3, 2):
        kv_copies[d].wait_recv()
        rows = kv_rows(lax.rem(z + 4 - d, 4) * 2 + c)
        fcopy = remote(rows, rows, kvf_s.at[d - 1], kvf_r.at[d - 1], ctx=core_peer)
        fcopy.start()
        forwards["kv", d] = fcopy
    kv_copies[0].wait_recv()
    for d in (1, 3, 2):
        forwards["kv", d].wait_recv()
    store(kv_ref, kv_h)

    og_args = (send_ogmain, send_ogleft, ogmain_ref, ogleft_ref, og_s, og_r)
    x_args = (send_main, send_left, xmain_ref, xleft_ref, x_s, x_r)

    @pl.when(main)
    def _():
        send_rows(*og_args)

    pass_kind(0)
    send_kind(1)
    send_kind(2)

    lse_ref[...] = jnp.zeros_like(lse_ref)
    outgoing = []
    for half in range(2):
        at = slice(half * 128, (half + 1) * 128)
        for j in range(6):
            lanes = slice((j % 2) * 128, (j % 2) * 128 + 128)
            scores = dot_nt(q_ref[j // 2, at, lanes], kv_ref[:, 0:128]) * SCALE + bias[at, :]
            top = jnp.max(scores, axis=1, keepdims=True)
            terms = jnp.exp(scores - top)
            total = jnp.sum(terms, axis=1, keepdims=True)
            mixed = dot(terms.astype(BF16), kv_ref[:, 128:256]) / total
            heads_ref[j // 2, at, lanes] = mixed.astype(BF16)
            lse_ref[at, :] = jnp.where(
                iota((128, 128), 1) == j, top + jnp.log(total), lse_ref[at, :]
            )
        if half == 0:
            join_group(2)
        total = dot_nt(heads_ref[0, at, :], w_ref[4])
        total = total + dot_nt(heads_ref[1, at, :], w_ref[5])
        total = total + dot_nt(heads_ref[2, at, :], w_ref[6])
        part[at, :] = total.astype(BF16)
        copy = remote(part.at[at], prec.at[at], pe_s.at[half], pe_r.at[half], tensor=1 - ten)
        outgoing.append(copy)

        @pl.when(jnp.logical_not(main))
        def _(copy=copy):
            copy.start()

    pass_kind(1)
    pass_kind(2)

    for copy in outgoing:

        @pl.when(main)
        def _(copy=copy):
            copy.wait_recv()
            copy.start()

        @pl.when(jnp.logical_not(main))
        def _(copy=copy):
            copy.wait_recv()

    resid = hid_ref[...] + (part[...].astype(F32) + prec[...].astype(F32))
    resid_ref[...] = resid
    store(resid_ref, resid_h)
    store(heads_ref, heads_h)
    inverse = lax.rsqrt(jnp.mean(resid * resid, axis=1, keepdims=True) + EPS)
    nbb = (resid * inverse * gain_ref[1:2, :]).astype(BF16)
    nbb_ref[...] = nbb
    store(nbb_ref, nbb_h)
    logits = jnp.where(hit > 0.5, dot(nbb, router_ref[...]), -1e30)
    top = jnp.max(logits, axis=1, keepdims=True)
    terms = jnp.where(hit > 0.5, jnp.exp(logits - top), 0.0)
    gates = terms / jnp.sum(terms, axis=1, keepdims=True)
    gate_ref[...] = gates

    @pl.when(main)
    def _():
        nbx[:, 0:D] = nbb
        high = gates.astype(BF16).astype(F32)
        nbx[:, D:] = (high + pltpu.roll(gates - high, 32, 1)).astype(BF16)
        pack_rows(onehot_main, onehot_left, nbx, send_main, send_left)
        send_rows(*x_args)

    for k in range(3):
        spread[k, "y"].wait_recv()
        there = wexp_ref.at[k, :, c, :, pl.ds(pl.multiple_of((1 - ten) * HALF, 128), HALF)]
        spread[k, "cy"] = remote(there, there, wc_s.at[k, 1], wc_r.at[k, 1], ctx=core_peer)
        spread[k, "cy"].start()
    for k in range(3):
        spread[k, "c"].wait_recv()
        spread[k, "cy"].wait_recv()
        for d in (1, 2, 3):
            spread[k, d].wait_send()
        for name in ("y", "c", "cy"):
            spread[k, name].wait_send()
    wait_received_rows(*og_args)
    wait_received_rows(*x_args)

    @pl.when(main)
    def _():
        wait_sent_rows(*og_args)
        wait_sent_rows(*x_args)

    for copy in small + list(weight_copies.values()) + list(forwards.values()) + list(kv_copies.values()):
        copy.wait_send()
    for copy in outgoing:
        copy.wait_send()
    for copy in stores:
        copy.wait()


def sems(*shape):
    return pltpu.SemaphoreType.DMA(shape)


def run_forward(hid, og, choice_rows, seg, aw, rw, gains, ew):
    vmem = pl.BlockSpec(memory_space=pltpu.VMEM)
    hbm = pl.BlockSpec(memory_space=pl.ANY)
    S = jax.ShapeDtypeStruct
    V = pltpu.VMEM
    kept = [
        ((3, TOK, 256), BF16),
        ((2048, 256), BF16),
        ((3, TOK, 256), BF16),
        ((7, D, 256), BF16),
        ((TOK, D), F32),
        ((TOK, D), BF16),
        ((TOK, D), BF16),
    ]
    outs = [
        S((TOK, 128), F32),
        S((TOK, 128), F32),
        S((8, D), F32),
        S((D, 128), BF16),
        *(S(*shape) for shape in kept),
        S((3, 4, 2, ROWS, FF), BF16),
        S((512, D + 128), BF16),
        S((256, HALF + 128), BF16),
        S((512, D), BF16),
        S((256, HALF), BF16),
    ]
    lse, gate, gain, router, *rest = pl.pallas_call(
        forward_kernel,
        out_shape=outs,
        in_specs=[vmem] * 4 + [hbm] * 4,
        out_specs=[vmem] * 4 + [hbm] * 12,
        scratch_shapes=[
            V((TOK, D), F32),
            V((TOK, D), F32),
            V((1, 14, ROWS, 128), F32),
            V((4, 3, ROWS, HALF), F32),
            V((4, 3, ROWS, HALF), BF16),
            *(V(*shape) for shape in kept),
            sems(4),
            sems(16),
            V((7, ROWS, 256), BF16),
            V((ROWS, 128), BF16),
            V((8, D), F32),
            V((7, 8, D), F32),
            V((TOK, 2048), F32),
            V((32, TOK), F32),
            V((1024, TOK), BF16),
            V((512, TOK), BF16),
            V((TOK, D + 128), BF16),
            V((TOK, D), BF16),
            V((1024, D + 128), BF16),
            V((512, HALF + 128), BF16),
            V((1024, D), BF16),
            V((512, HALF), BF16),
            V((TOK, D), BF16),
            V((TOK, D), BF16),
            sems(3, 3),
            sems(3, 3),
            sems(3, 3, 3),
            sems(3, 3, 3),
            sems(3, 4),
            sems(3, 4),
            sems(2, 7),
            sems(2, 7),
            sems(4),
            sems(4),
            sems(3),
            sems(3),
            sems(2),
            sems(2),
            sems(2, 32),
            sems(2, 16),
            sems(2, 32),
            sems(2, 16),
            sems(3, 4),
            sems(3, 4),
            sems(3),
            sems(3),
            sems(3, 2),
            sems(3, 2),
        ],
        compiler_params=pltpu.CompilerParams(
            collective_id=0, has_side_effects=True, vmem_limit_bytes=56 * MiB
        ),
        name="attention_forward",
    )(choice_rows, seg, rw.T, gains, hid, og, aw, ew)
    q, kv, heads, w, resid, nba, nbb, *sent = rest
    return (q, kv, heads, lse, w, resid, nba, nbb, gate, gain, router, *sent)


GATE, UP, DOWN = 0, 1, 2
OWNER_PLANE = (0, 1, 0)
OWNER_CORE = (0, 1, 1)
CORE_SLOT = (0, 0, 1)
GELU_A = 0.7978845608028654
GELU_B = 0.044715


def is_owner(c, ten):
    return jnp.logical_not((c == 0) & (ten == 1))


def half_columns(index):
    return pl.ds(pl.multiple_of(index * HALF, 128), HALF)


def greet_group(barrier):
    _, ctx, ten, _, _ = place()
    for j in range(8):
        for t in range(2):
            if j or t:
                pl.semaphore_signal(
                    barrier,
                    inc=1,
                    device_id={"ctx": lax.rem(ctx + j, 8), "tensor": lax.rem(ten + t, 2)},
                    device_id_type=MESH,
                )


def send_block(src, dst, send_sem, recv_sem, to_ctx, to_ten):
    _, ctx, ten, _, _ = place()
    here = (ctx == to_ctx) & (ten == to_ten)

    @pl.when(here)
    def _():
        local(src, dst, recv_sem).start()

    @pl.when(jnp.logical_not(here))
    def _():
        remote(src, dst, send_sem, recv_sem, ctx=to_ctx, tensor=to_ten).start()


def wait_block_sent(src, dst, send_sem, recv_sem, to_ctx, to_ten):
    _, ctx, ten, _, _ = place()
    here = (ctx == to_ctx) & (ten == to_ten)

    @pl.when(jnp.logical_not(here))
    def _():
        remote(src, dst, send_sem, recv_sem, ctx=to_ctx, tensor=to_ten).wait_send()


def wait_block_received(block, send_sem, recv_sem):
    _, ctx, ten, _, _ = place()
    remote(block, block, send_sem, recv_sem, ctx=ctx, tensor=1 - ten).wait_recv()


def return_rows(src_main, src_left, dst_main, dst_left, send_sem, recv_sem):
    dp, ctx, ten, z, c = place()
    expert = dp * 4 + z

    def one(s, carry):
        to_dp, to_z = lax.div(s, 2), lax.rem(s, 2) * 2 + c
        plane = plane_for(dp, to_dp, ten)
        here = (to_dp == dp) & (to_z == z) & (c == ten)
        for i, (src, dst, n) in enumerate(((src_main, dst_main, 32), (src_left, dst_left, 16))):
            src_at = src.at[pl.ds(pl.multiple_of(s * n, n), n)]
            dst_at = dst.at[pl.ds(pl.multiple_of(expert * n, n), n)]

            @pl.when(here)
            def _(i=i, src_at=src_at, dst_at=dst_at):
                local(src_at, dst_at, recv_sem.at[i, expert]).start()

            @pl.when(jnp.logical_not(here))
            def _(i=i, src_at=src_at, dst_at=dst_at):
                remote(
                    src_at,
                    dst_at,
                    send_sem.at[i, s],
                    recv_sem.at[i, expert],
                    dp=to_dp,
                    ctx=to_z * 2 + plane,
                    tensor=plane,
                ).start()

        return carry

    lax.fori_loop(0, 16, one, 0)


def wait_returned(src_main, src_left, dst_main, dst_left, send_sem, recv_sem):
    dp, ctx, ten, z, c = place()

    def one(e, carry):
        for i, (src, dst, n) in enumerate(((src_main, dst_main, 32), (src_left, dst_left, 16))):
            remote(
                src.at[pl.ds(0, n)],
                dst.at[pl.ds(pl.multiple_of(e * n, n), n)],
                send_sem.at[i, 0],
                recv_sem.at[i, e],
                dp=dp,
                ctx=ctx,
                tensor=1 - ten,
            ).wait_recv()
        return carry

    lax.fori_loop(0, 32, one, 0)


def wait_return_sent(src_main, src_left, dst_main, dst_left, send_sem, recv_sem):
    dp, ctx, ten, z, c = place()

    def one(s, carry):
        here = (lax.div(s, 2) == dp) & (lax.rem(s, 2) * 2 + c == z) & (c == ten)

        @pl.when(jnp.logical_not(here))
        def _():
            for i, (src, dst, n) in enumerate(((src_main, dst_main, 32), (src_left, dst_left, 16))):
                remote(
                    src.at[pl.ds(pl.multiple_of(s * n, n), n)],
                    dst.at[pl.ds(0, n)],
                    send_sem.at[i, s],
                    recv_sem.at[i, 0],
                    dp=dp,
                    ctx=ctx,
                    tensor=1 - ten,
                ).wait_send()

        return carry

    lax.fori_loop(0, 16, one, 0)


def greet_expert_devices(barrier):
    dp, ctx, ten, z, c = place()
    core = lax.rem(z, 2)

    def one(e, carry):
        to_dp, to_z = lax.div(e, 4), lax.rem(e, 4)
        here = (to_dp == dp) & (to_z == z) & (c == core)

        @pl.when(jnp.logical_not(here))
        def _():
            pl.semaphore_signal(
                barrier,
                inc=1,
                device_id={
                    "dp": to_dp,
                    "ctx": to_z * 2 + core,
                    "tensor": plane_for(dp, to_dp, ten),
                },
                device_id_type=MESH,
            )

        return carry

    @pl.when(c == ten)
    def _():
        lax.fori_loop(0, 32, one, 0)

    return 16 - ((c == ten) & (core == c)).astype(jnp.int32)


def left_picker(quarter):
    row, col = iota((64, 256), 0), iota((64, 256), 1)
    return jnp.where(col == lax.div(row, 4) * 16 + quarter * 4 + lax.rem(row, 4), 1.0, 0.0).astype(
        BF16
    )


def left_packer(quarter):
    row, col = iota((256, 64), 0), iota((256, 64), 1)
    return jnp.where(row == lax.div(col, 4) * 16 + quarter * 4 + lax.rem(col, 4), 1.0, 0.0).astype(
        BF16
    )


def fill_token_onehot(code, main_ref, left_ref):
    code = code.astype(BF16)
    for b in range(4):
        expert, col = iota((128, 256), 0), iota((128, 256), 1) + b * 256
        spread = dot(code, jnp.where(lax.div(col, 32) == expert, 1.0, 0.0).astype(BF16))
        slot = lax.rem(iota((TOK, 256), 1), 32).astype(F32)
        main_ref[:, b * 256 : (b + 1) * 256] = jnp.where(spread == slot, 1.0, 0.0).astype(BF16)
    for b in range(2):
        expert, col = iota((128, 256), 0), iota((128, 256), 1) + b * 256
        spread = dot(code, jnp.where(lax.div(col, 16) == expert, 1.0, 0.0).astype(BF16))
        slot = (32 + lax.rem(iota((TOK, 256), 1), 4)).astype(F32)
        left_ref[:, b * 256 : (b + 1) * 256] = jnp.where(spread == slot, 1.0, 0.0).astype(BF16)


def left_quarter(left_ref, quarter):
    keep = lax.rem(lax.div(iota((TOK, 512), 1), 4), 4) == quarter
    return jnp.where(keep, left_ref[...].astype(F32), 0.0).astype(BF16)


def backward_kernel(
    choice_ref,
    seg_ref,
    gate_ref,
    lse_ref,
    gain_ref,
    router_ref,
    xmain_h,
    xleft_h,
    ogmain_h,
    ogleft_h,
    wexp_h,
    w_h,
    q_h,
    kv_h,
    heads_h,
    nba_h,
    nbb_h,
    resid_h,
    og_h,
    mlow_h,
    dw_h,
    gres_ref,
    gna_ref,
    msum_ref,
    mom_h,
    omain_h,
    oleft_h,
    xall,
    gx,
    xleft,
    ogall,
    ogleft,
    w9,
    ggp,
    gup,
    hidden,
    ghid,
    gmain,
    gleft,
    oleft,
    dw9,
    rcore,
    cmain,
    cleft,
    ptm,
    ptl,
    ext,
    kv,
    q,
    heads,
    nba,
    nbb,
    resid,
    gheads,
    gatt,
    dslab,
    dq,
    dkv,
    rkv,
    skv,
    r2kv,
    stage,
    ld,
    lw,
    dw_s,
    g_s,
    g_r,
    o_s,
    o_r,
    mc_s,
    mc_r,
    my_s,
    my_r,
    e_s,
    e_r,
    k1_s,
    k1_r,
    k2_s,
    k2_r,
    mo_s,
    mo_r,
):
    dp, ctx, ten, z, c = place()
    main = c == ten
    core_peer = z * 2 + 1 - c
    expert = dp * 4 + z

    def z_peer(d):
        return lax.rem(z + d, 4) * 2 + c

    barrier = pltpu.get_barrier_semaphore()
    greet_group(barrier)
    extra = greet_expert_devices(barrier)

    loads = [
        pltpu.make_async_copy(xmain_h.at[:, 0:D], xall.at[0:512], ld.at[0]),
        pltpu.make_async_copy(xmain_h.at[:, D:], gx.at[0:512], ld.at[1]),
        pltpu.make_async_copy(xleft_h, xleft, ld.at[2]),
        pltpu.make_async_copy(ogmain_h, ogall.at[0:512], ld.at[3]),
        pltpu.make_async_copy(ogleft_h, ogleft, ld.at[4]),
    ]
    expert_loads = []
    for n in range(3):
        for k in range(3):
            expert_loads.append(
                pltpu.make_async_copy(
                    wexp_h.at[k, :, n * 256 : (n + 1) * 256], w9.at[3 * k + n], lw.at[3 * k + n]
                )
            )
    later = [
        pltpu.make_async_copy(src, dst, ld.at[5 + i])
        for i, (src, dst) in enumerate(
            (
                (kv_h, kv),
                (q_h, q),
                (heads_h, heads),
                (nba_h, nba),
                (nbb_h, nbb),
                (resid_h, resid),
                (og_h, gres_ref),
            )
        )
    ]
    for copy in loads + expert_loads + later:
        copy.start()

    @pl.when(main)
    def _():
        _, code = codes_by_token(choice_ref[...])
        fill_token_onehot(code, ptm, ptl)

    for copy in loads:
        copy.wait()
    for n in range(4):
        at = slice(n * HALF, (n + 1) * HALF)
        pick = left_picker(n)
        xall[512:576, at] = dot(pick, xleft[:, 0:HALF]).astype(BF16)
        ogall[512:576, at] = dot(pick, ogleft[...]).astype(BF16)
    gx[512:576, :] = dot(left_picker(0), xleft[:, HALF:]).astype(BF16)
    lane = iota((576, 128), 1)
    mine = (lane == expert) | (lane == expert + 32)
    gate = jnp.sum(jnp.where(mine, gx[...].astype(F32), 0.0), axis=1, keepdims=True)

    pl.semaphore_wait(barrier, 15 + extra)
    for i in range(4):
        for k in range(3):
            send_block(
                mlow_h.at[i, k],
                mom_h.at[z, c, :, half_columns(ten)],
                mo_s.at[i, k],
                mo_r.at[ctx * 2 + ten],
                2 * i + OWNER_CORE[k],
                OWNER_PLANE[k],
            )

    grad_gate = jnp.zeros((576, 1), F32)
    for n in range(3):
        for k in range(3):
            expert_loads[3 * n + k].wait()
        at = slice(n * 256, (n + 1) * 256)
        pre = dot(xall[...], w9[n])
        up = dot(xall[...], w9[3 + n])
        back = dot(ogall[...], w9[6 + n])
        bent = jnp.tanh(GELU_A * (pre + GELU_B * pre * pre * pre))
        value = 0.5 * pre * (1.0 + bent)
        slope = 0.5 * (1.0 + bent) + 0.5 * pre * (1.0 - bent * bent) * GELU_A * (
            1.0 + 3.0 * GELU_B * pre * pre
        )
        hid = (value * up).astype(BF16).astype(F32)
        grad_gate = grad_gate + jnp.sum(hid * back, axis=1, keepdims=True)
        scaled = back * gate
        ghid[:, at] = (hid * gate).astype(BF16)
        ggp[:, at] = (scaled * up * slope).astype(BF16)
        gup[:, at] = (scaled * value).astype(BF16)

    high = grad_gate.astype(BF16).astype(F32)
    marks = jnp.where(lane == expert, high, jnp.where(lane == expert + 32, grad_gate - high, 0.0))
    marks = marks.astype(BF16)
    gmain[:, D:] = marks[0:512]
    gleft[:, HALF:] = dot(left_packer(0), marks[512:576]).astype(BF16)
    packed = jnp.zeros((256, HALF), F32)
    for m in range(4):
        at = slice(m * HALF, (m + 1) * HALF)
        total = jnp.zeros((576, HALF), F32)
        for n in range(3):
            cols = slice(n * 256, (n + 1) * 256)
            total = total + dot_nt(ggp[:, cols], w9[n, at, :])
            total = total + dot_nt(gup[:, cols], w9[3 + n, at, :])
        gmain[:, at] = total[0:512].astype(BF16)
        packed = packed + dot(left_packer(m), total[512:576].astype(BF16))
    gleft[:, 0:HALF] = packed.astype(BF16)
    g_args = (gmain, gleft, cmain, cleft, g_s, g_r)
    o_args = (xall, oleft, omain_h, oleft_h, o_s, o_r)
    return_rows(*g_args)

    core_copies, plane_copies = {}, {}
    order = [(k, n) for k in (GATE, DOWN, UP) for n in range(3)]
    for k, n in order:
        at = slice(n * 256, (n + 1) * 256)
        rows, right = (ogall, ghid) if k == DOWN else (xall, ggp if k == GATE else gup)
        dw9[3 * k + n] = dot_tn(rows[...], right[:, at]).astype(BF16)
        copy = remote(
            dw9.at[3 * k + n],
            rcore.at[CORE_SLOT[k], n],
            mc_s.at[k, n],
            mc_r.at[k, n],
            ctx=core_peer,
        )
        core_copies[k, n] = copy

        @pl.when(c != OWNER_CORE[k])
        def _(copy=copy):
            copy.start()

    packed = jnp.zeros((256, HALF), F32)
    for m in range(4):
        at = slice(m * HALF, (m + 1) * HALF)
        total = jnp.zeros((576, HALF), F32)
        for n in range(3):
            total = total + dot_nt(ghid[:, n * 256 : (n + 1) * 256], w9[6 + n, at, :])
        xall[0:512, at] = total[0:512].astype(BF16)
        packed = packed + dot(left_packer(m), total[512:576].astype(BF16))
    oleft[...] = packed.astype(BF16)

    for k, n in order:
        copy = remote(
            dw9.at[3 * k + n], msum_ref.at[:, n * 256 : (n + 1) * 256], my_s.at[k, n], my_r.at[k, n], tensor=1 - ten
        )
        plane_copies[k, n] = copy

        @pl.when(c == OWNER_CORE[k])
        def _(k=k, n=n, copy=copy):
            core_copies[k, n].wait_recv()
            dw9[3 * k + n] = (
                dw9[3 * k + n].astype(F32) + rcore[CORE_SLOT[k], n].astype(F32)
            ).astype(BF16)

            @pl.when(ten != OWNER_PLANE[k])
            def _():
                copy.start()

    weight_loads = [pltpu.make_async_copy(w_h.at[p], w9.at[p], lw.at[p]) for p in range(7)]
    for copy in weight_loads:
        copy.start()

    @pl.when(main)
    def _():
        wait_returned(*g_args)
        extras = dot(ptm[...], cmain[:, D:]) + dot(left_quarter(ptl, 0), cleft[:, HALF:])
        grads = jnp.where(iota((TOK, 128), 1) < 32, extras + pltpu.roll(extras, 96, 1), 0.0)
        gates = gate_ref[...]
        grad_logits = gates * (grads - jnp.sum(gates * grads, axis=1, keepdims=True))
        high = grad_logits.astype(BF16)
        low = (grad_logits - high.astype(F32)).astype(BF16)
        ext[:, D:] = (high.astype(F32) + pltpu.roll(low.astype(F32), 32, 1)).astype(BF16)
        for m in range(4):
            at = slice(m * HALF, (m + 1) * HALF)
            total = dot(ptm[...], cmain[:, at]) + dot(left_quarter(ptl, m), cleft[:, 0:HALF])
            total = total + dot_nt(high, router_ref[at, :]) + dot_nt(low, router_ref[at, :])
            ext[:, at] = total.astype(BF16)

    share = remote(ext, ext, e_s, e_r, tensor=1 - ten)

    @pl.when(main)
    def _():
        share.start()
        share.wait_send()

    @pl.when(jnp.logical_not(main))
    def _():
        share.wait_recv()

    return_rows(*o_args)

    for copy in later:
        copy.wait()
    dslab[...] = jnp.zeros_like(dslab)

    def norm_rows(r, carry):
        at = pl.ds(pl.multiple_of(r * 64, 64), 64)
        gnb = ext[at, 0:D].astype(F32)
        value = resid[at, :]
        inverse = lax.rsqrt(jnp.mean(value * value, axis=1, keepdims=True) + EPS)
        scaled = gnb * gain_ref[1:2, :]
        inner = jnp.mean(scaled * value, axis=1, keepdims=True)
        gres = gres_ref[at, :] + inverse * scaled - value * (inverse * inverse * inverse) * inner
        gres_ref[at, :] = gres
        gatt[at, :] = gres.astype(BF16)
        flat = gnb * value * inverse
        high = flat.astype(BF16)
        low = (flat - high.astype(F32)).astype(BF16)
        lane = iota((64, 128), 1)
        ones = jnp.where(lane == 32, 1.0, 0.0).astype(BF16)
        both = ext[at, D:].astype(F32)
        logit_high = jnp.where(lane < 32, both, 0.0).astype(BF16)
        logit_low = jnp.where(lane < 32, pltpu.roll(both, 96, 1), 0.0).astype(BF16)
        rows = nbb[at, :]
        dslab[...] += (
            dot_tn(rows, logit_high) + dot_tn(rows, logit_low) + dot_tn(high, ones) + dot_tn(low, ones)
        )
        return carry

    lax.fori_loop(0, 4, norm_rows, 0)

    stores = {}

    def store(p, value):
        if p < 4:
            stores[p + 4].wait()
        stage[p % 4] = value
        stores[p] = pltpu.make_async_copy(stage.at[p % 4], dw_h.at[p], dw_s.at[p])
        stores[p].start()

    for copy in weight_loads:
        copy.wait()
    store(7, jnp.concatenate([dslab[...], jnp.zeros((D, 128), F32)], axis=1).astype(BF16))
    terms = jnp.zeros((TOK, 128), F32)
    for p in range(3):
        gheads[p] = dot(gatt[...], w9[4 + p]).astype(BF16)
        store(4 + p, dot_tn(gatt[...], heads[p]).astype(BF16))
        prod = gheads[p].astype(F32) * heads[p].astype(F32)
        for i in range(2):
            term = jnp.sum(prod[:, i * 128 : (i + 1) * 128], axis=1, keepdims=True)
            terms = jnp.where(iota((TOK, 128), 1) == 2 * p + i, term, terms)
    lse_rows = jnp.transpose(lse_ref[...])
    term_rows = jnp.transpose(terms)
    dkv[...] = jnp.zeros_like(dkv)
    dq[...] = jnp.zeros_like(dq)
    seg_here = seg_ref[:, pl.ds(pl.multiple_of(ctx * TOK, TOK), TOK)]

    def key_block(b, carry):
        at = pl.ds(pl.multiple_of(b * TOK, TOK), TOK)
        seg_col = row_to_column(seg_ref[:, at])
        key_pos = b * TOK + iota((TOK, TOK), 0)
        query_pos = ctx * TOK + iota((TOK, TOK), 1)
        allowed = (key_pos <= query_pos) & (seg_here == seg_col)
        keys, values = kv[at, 0:128], kv[at, 128:256]
        dk = jnp.zeros((TOK, 128), F32)
        dv = jnp.zeros((TOK, 128), F32)
        for j in range(6):
            lanes = slice((j % 2) * 128, (j % 2) * 128 + 128)
            qj, gj = q[j // 2, :, lanes], gheads[j // 2, :, lanes]
            scores = dot_nt(keys, qj) * SCALE
            probs = jnp.where(allowed, jnp.exp(scores - lse_rows[j : j + 1, :]), 0.0)
            grad = dot_nt(values, gj)
            grad_scores = (probs * (grad - term_rows[j : j + 1, :]) * SCALE).astype(BF16)
            dv = dv + dot(probs.astype(BF16), gj)
            dk = dk + dot(grad_scores, qj)
            dq[j // 2, :, lanes] += dot_tn(grad_scores, keys)
        dkv[at, 0:128] = dk.astype(BF16)
        dkv[at, 128:256] = dv.astype(BF16)
        return carry

    lax.fori_loop(0, ctx + 1, key_block, 0)

    pair = []
    for to_z in range(4):
        src = dkv.at[pl.ds(pl.multiple_of((to_z * 2 + 1 - c) * TOK, TOK), TOK)]
        copy = remote(src, rkv.at[to_z], k1_s.at[to_z], k1_r.at[to_z], ctx=core_peer)
        copy.start()
        pair.append(copy)
    for p in range(3):
        store(p, dot_tn(nba[...], dq[p].astype(BF16)).astype(BF16))
    total = dot_nt(dq[0].astype(BF16), w9[0])
    total = total + dot_nt(dq[1].astype(BF16), w9[1])
    total = total + dot_nt(dq[2].astype(BF16), w9[2])
    for to_z in range(4):
        pair[to_z].wait_recv()
        own = dkv[pl.ds(pl.multiple_of((to_z * 2 + c) * TOK, TOK), TOK), :]
        skv[to_z] = (own.astype(F32) + rkv[to_z].astype(F32)).astype(BF16)
    ring = []
    for d in (1, 3, 2):
        copy = remote(
            skv.at[lax.rem(z + d, 4)], r2kv.at[d - 1], k2_s.at[d - 1], k2_r.at[d - 1], ctx=z_peer(d)
        )
        copy.start()
        ring.append(copy)
    for copy in ring:
        copy.wait_recv()
    gkv = skv[z].astype(F32) + r2kv[0].astype(F32) + r2kv[1].astype(F32) + r2kv[2].astype(F32)
    gkv = gkv.astype(BF16)
    store(3, dot_tn(nba[...], gkv).astype(BF16))
    total = total + dot_nt(gkv, w9[3])
    gna_ref[...] = total.astype(BF16)

    for k in range(3):
        for n in range(3):
            plane = plane_copies[k, n]

            @pl.when((c == OWNER_CORE[k]) & (ten == OWNER_PLANE[k]))
            def _(k=k, n=n, plane=plane):
                plane.wait_recv()
                at = slice(n * 256, (n + 1) * 256)
                msum_ref[:, at] = (
                    dw9[3 * k + n].astype(F32) + msum_ref[:, at].astype(F32)
                ).astype(BF16)

            @pl.when((c == OWNER_CORE[k]) & (ten != OWNER_PLANE[k]))
            def _(plane=plane):
                plane.wait_send()

            @pl.when(c != OWNER_CORE[k])
            def _(k=k, n=n):
                core_copies[k, n].wait_send()

    @pl.when((c == 0) & (ten == 1))
    def _():
        msum_ref[...] = jnp.zeros_like(msum_ref)

    for i in range(4):
        for k in range(3):
            wait_block_sent(
                mlow_h.at[i, k],
                mom_h.at[z, c, :, half_columns(ten)],
                mo_s.at[i, k],
                mo_r.at[ctx * 2 + ten],
                2 * i + OWNER_CORE[k],
                OWNER_PLANE[k],
            )

    @pl.when(is_owner(c, ten))
    def _():
        for index in range(16):
            wait_block_received(mlow_h.at[0, 0], mo_s.at[0, 0], mo_r.at[index])

    for copy in pair + ring:
        copy.wait_send()
    wait_return_sent(*g_args)
    wait_return_sent(*o_args)

    @pl.when(main)
    def _():
        wait_returned(*o_args)

    for p in range(4):
        stores[p].wait()


def run_backward(choice_rows, seg, fwd, og, mlow):
    (q, kv, heads, lse, w, resid, nba, nbb, gate, gain, router, wexp, xm, xl, om, ol) = fwd
    vmem = pl.BlockSpec(memory_space=pltpu.VMEM)
    hbm = pl.BlockSpec(memory_space=pl.ANY)
    S = jax.ShapeDtypeStruct
    V = pltpu.VMEM
    return pl.pallas_call(
        backward_kernel,
        out_shape=[
            S((8, D, 256), BF16),
            S((TOK, D), F32),
            S((TOK, D), BF16),
            S((D, FF), BF16),
            S((4, 2, ROWS, FF), BF16),
            S((1024, D), BF16),
            S((512, HALF), BF16),
        ],
        in_specs=[vmem] * 6 + [hbm] * 14,
        out_specs=[hbm, vmem, vmem, vmem, hbm, hbm, hbm],
        scratch_shapes=[
            V((576, D), BF16),
            V((576, 128), BF16),
            V((256, HALF + 128), BF16),
            V((576, D), BF16),
            V((256, HALF), BF16),
            V((9, D, 256), BF16),
            V((576, FF), BF16),
            V((576, FF), BF16),
            V((8, 128), BF16),
            V((576, FF), BF16),
            V((512, D + 128), BF16),
            V((256, HALF + 128), BF16),
            V((256, HALF), BF16),
            V((9, D, 256), BF16),
            V((2, 3, D, 256), BF16),
            V((1024, D + 128), BF16),
            V((512, HALF + 128), BF16),
            V((TOK, 1024), BF16),
            V((TOK, 512), BF16),
            V((TOK, D + 128), BF16),
            V((2048, 256), BF16),
            V((3, TOK, 256), BF16),
            V((3, TOK, 256), BF16),
            V((TOK, D), BF16),
            V((TOK, D), BF16),
            V((TOK, D), F32),
            V((3, TOK, 256), BF16),
            V((TOK, D), BF16),
            V((D, 128), F32),
            V((3, TOK, 256), F32),
            V((2048, 256), BF16),
            V((4, TOK, 256), BF16),
            V((4, TOK, 256), BF16),
            V((3, TOK, 256), BF16),
            V((4, D, 256), BF16),
            sems(12),
            sems(9),
            sems(8),
            sems(2, 16),
            sems(2, 32),
            sems(2, 16),
            sems(2, 32),
            sems(3, 3),
            sems(3, 3),
            sems(3, 3),
            sems(3, 3),
            pltpu.SemaphoreType.DMA,
            pltpu.SemaphoreType.DMA,
            sems(4),
            sems(4),
            sems(3),
            sems(3),
            sems(4, 3),
            sems(16),
        ],
        compiler_params=pltpu.CompilerParams(
            collective_id=1, has_side_effects=True, vmem_limit_bytes=58 * MiB
        ),
        name="backward",
    )(
        choice_rows, seg, gate, lse, gain, router, xm, xl, om, ol, wexp.reshape(3, D, FF),
        w, q, kv, heads, nba, nbb, resid, og, mlow,
    )
NS_A = 3.4445
NS_B = -4.775
NS_C = 2.0315
MUON_RATES = (0.15, 0.15, 0.6)


def update_kernel(
    choice_ref,
    gain_ref,
    hid_h,
    gna_h,
    msum_h,
    mom_h,
    dw_h,
    omain_h,
    oleft_h,
    fin_ref,
    term_ref,
    moe_ref,
    ghome_h,
    ohome_h,
    hid_ref,
    gna_ref,
    msum_ref,
    mom_ref,
    own,
    r1,
    r2,
    r3,
    s2,
    slab,
    omain,
    oleft,
    ptm,
    ptl,
    moe_send,
    gnap,
    ns_x,
    ns_b,
    ns_m,
    ld,
    a_s,
    a_r,
    b_s,
    b_r,
    c_s,
    c_r,
    d_s,
    d_r,
    l_s,
    l_r,
    gn_s,
    gn_r,
    gh_s,
    gh_r,
    oh_s,
    oh_r,
):
    dp, ctx, ten, z, c = place()
    main = c == ten
    core_peer = z * 2 + 1 - c

    def z_peer(d):
        return lax.rem(z + d, 4) * 2 + c

    barrier = pltpu.get_barrier_semaphore()
    greet_group(barrier)
    for j in range(1, 8):
        pl.semaphore_signal(
            barrier, inc=1, device_id={"dp": lax.rem(dp + j, 8)}, device_id_type=MESH
        )

    loads = [
        pltpu.make_async_copy(dw_h.at[7], slab, ld.at[0]),
        pltpu.make_async_copy(omain_h, omain, ld.at[1]),
        pltpu.make_async_copy(oleft_h, oleft, ld.at[2]),
        pltpu.make_async_copy(gna_h, gna_ref, ld.at[31]),
        pltpu.make_async_copy(msum_h, msum_ref, ld.at[32]),
        pltpu.make_async_copy(mom_h, mom_ref, ld.at[33]),
        pltpu.make_async_copy(hid_h, hid_ref, ld.at[34]),
    ]
    own_loads = []
    for p in range(7):
        for to_z in range(4):
            rows = pl.ds(pl.multiple_of((to_z * 2 + c) * ROWS, 64), ROWS)
            own_loads.append(
                pltpu.make_async_copy(dw_h.at[p, rows], own.at[p, to_z], ld.at[3 + p * 4 + to_z])
            )
    for copy in loads + own_loads:
        copy.start()

    owner = is_owner(c, ten)

    pl.semaphore_wait(barrier, 22)

    swap = remote(gna_ref, gnap, gn_s, gn_r, tensor=1 - ten)
    loads[3].wait()
    swap.start()

    first = {}

    def send_first(p):
        for to_z in range(4):
            rows = pl.ds(pl.multiple_of((to_z * 2 + 1 - c) * ROWS, 64), ROWS)
            src = slab.at[rows] if p == 7 else dw_h.at[p, rows]
            first[p, to_z] = remote(
                src, r1.at[p, to_z], a_s.at[p, to_z], a_r.at[p, to_z], ctx=core_peer
            )
            first[p, to_z].start()

    for p in (4, 5, 6, 0, 1, 2, 3):
        send_first(p)

    def spread(src, dst_h, send_sem, recv_sem, act):
        for k in range(3):

            @pl.when((c == OWNER_CORE[k]) & (ten == OWNER_PLANE[k]))
            def _(k=k):
                for to in range(8):
                    for t in range(2):
                        act(
                            src.at[to * ROWS : (to + 1) * ROWS, t * HALF : (t + 1) * HALF],
                            dst_h.at[z, k],
                            send_sem.at[to, t],
                            recv_sem.at[z, k],
                            to,
                            t,
                        )

    for copy in own_loads + loads[4:]:
        copy.wait()
    second = {}

    def send_second(p):
        for to_z in range(4):
            first[p, to_z].wait_recv()
        own[p] = (own[p].astype(F32) + r1[p].astype(F32)).astype(BF16)
        for d in (1, 3, 2):
            second[p, d] = remote(
                own.at[p, lax.rem(z + d, 4)],
                r2.at[p, d - 1],
                b_s.at[p, d - 1],
                b_r.at[p, d - 1],
                ctx=z_peer(d),
            )
            second[p, d].start()

    for p in (4, 5, 6, 0, 1, 2, 3):
        send_second(p)

    spread(msum_ref, ghome_h, gh_s, gh_r, send_block)

    _, code = codes_by_token(choice_ref[...])
    loads[1].wait()
    loads[2].wait()
    away = remote(moe_send, moe_ref, l_s, l_r, tensor=1 - ten)

    @pl.when(main)
    def _():
        fill_token_onehot(code, ptm, ptl)
        for m in range(4):
            at = slice(m * HALF, (m + 1) * HALF)
            total = dot(ptm[...], omain[:, at]) + dot(left_quarter(ptl, m), oleft[...])
            to = slice((m % 2) * HALF, (m % 2 + 1) * HALF)

            @pl.when(ten == m // 2)
            def _(total=total, to=to):
                moe_ref[:, to] = total.astype(BF16)

            @pl.when(ten != m // 2)
            def _(total=total, to=to):
                moe_send[:, to] = total.astype(BF16)

        away.start()

    loads[0].wait()
    swap.wait_recv()
    gna = gna_ref[...].astype(F32) + gnap[...].astype(F32)
    hid = hid_ref[...]
    inverse = lax.rsqrt(jnp.mean(hid * hid, axis=1, keepdims=True) + EPS)
    scaled = gna * gain_ref[0:1, :]
    inner = jnp.mean(scaled * hid, axis=1, keepdims=True)
    term_ref[...] = inverse * scaled - hid * (inverse * inverse * inverse) * inner
    flat = gna * hid * inverse
    high = flat.astype(BF16)
    low = (flat - high.astype(F32)).astype(BF16)
    ones = jnp.where(iota((TOK, 128), 1) == 33, 1.0, 0.0).astype(BF16)
    slab[:, 0:128] = (slab[:, 0:128].astype(F32) + dot_tn(high, ones) + dot_tn(low, ones)).astype(BF16)

    send_first(7)
    for to_z in range(4):
        rows = pl.ds(pl.multiple_of((to_z * 2 + c) * ROWS, 64), ROWS)
        own[7, to_z] = slab[rows, :]
    send_second(7)

    @pl.when(owner)
    def _():
        ns_m[...] = mom_ref[...].reshape(D, FF).astype(F32) + msum_ref[...].astype(F32)
        norm = jnp.sqrt(jnp.sum(ns_m[...] * ns_m[...])) + 1e-07
        ns_x[...] = (ns_m[...] / norm).astype(BF16)

    def step(turn, carry):
        @pl.when(owner)
        def _():
            gram = dot_tn(ns_x[...], ns_x[...]).astype(BF16)
            ns_b[...] = gram
            square = dot(ns_b[...], ns_b[...])
            ns_b[...] = (NS_B * ns_b[...].astype(F32) + NS_C * square).astype(BF16)
            for r in range(6):
                at = slice(r * 256, (r + 1) * 256)
                ns_x[at, :] = (
                    NS_A * ns_x[at, :].astype(F32) + dot(ns_x[at, :], ns_b[...])
                ).astype(BF16)

        for when, pairs in ((3, (4, 5, 6, 0)), (4, (1, 2, 3, 7))):

            @pl.when(turn == when)
            def _(pairs=pairs):
                for p in pairs:
                    total = own[p, z].astype(F32)
                    for d in (1, 2, 3):
                        second[p, d].wait_recv()
                        total = total + r2[p, d - 1].astype(F32)
                    s2[p] = total.astype(BF16)

                    @pl.when(p != dp)
                    def _(p=p):
                        remote(s2.at[p], r3.at[dp], c_s.at[p], c_r.at[dp], dp=p).start()

                    @pl.when(p == dp)
                    def _(p=p):
                        r3[dp] = s2[p]

        return carry

    lax.fori_loop(0, 5, step, 0)

    spread(ns_x, ohome_h, oh_s, oh_r, send_block)

    def arrived(s, carry):
        @pl.when(s != dp)
        def _():
            remote(r3.at[s], r3.at[s], c_s.at[s], c_r.at[s], dp=s).wait_recv()

        return carry

    lax.fori_loop(0, 8, arrived, 0)
    total = r3[0].astype(F32)
    for index in range(1, 8):
        total = total + r3[index].astype(F32)
    fin_ref[dp] = total.astype(BF16)

    def give(j, carry):
        to = lax.rem(dp + j, 8)
        remote(fin_ref.at[dp], fin_ref.at[dp], d_s.at[to], d_r.at[dp], dp=to).start()
        return carry

    lax.fori_loop(1, 8, give, 0)

    spread(msum_ref, ghome_h, gh_s, gh_r, wait_block_sent)
    for i in range(4):
        for k in range(3):
            wait_block_received(ghome_h.at[i, k], gh_s.at[0, 0], gh_r.at[i, k])
    swap.wait_send()
    for copy in list(first.values()) + list(second.values()):
        copy.wait_send()

    def others(j, carry):
        to = lax.rem(dp + j, 8)
        remote(s2.at[to], r3.at[dp], c_s.at[to], c_r.at[dp], dp=to).wait_send()
        remote(fin_ref.at[dp], fin_ref.at[dp], d_s.at[to], d_r.at[dp], dp=to).wait_send()
        remote(fin_ref.at[to], fin_ref.at[to], d_s.at[to], d_r.at[to], dp=to).wait_recv()
        return carry

    lax.fori_loop(1, 8, others, 0)

    @pl.when(main)
    def _():
        away.wait_send()

    @pl.when(jnp.logical_not(main))
    def _():
        away.wait_recv()

    spread(ns_x, ohome_h, oh_s, oh_r, wait_block_sent)
    for i in range(4):
        for k in range(3):
            wait_block_received(ohome_h.at[i, k], oh_s.at[0, 0], oh_r.at[i, k])


def run_update(choice_rows, hid, gain, bwd):
    dw, gres, gna, msum, mom, omain, oleft = bwd
    vmem = pl.BlockSpec(memory_space=pltpu.VMEM)
    hbm = pl.BlockSpec(memory_space=pl.ANY)
    S = jax.ShapeDtypeStruct
    V = pltpu.VMEM
    return pl.pallas_call(
        update_kernel,
        out_shape=[
            S((8, ROWS, 256), BF16),
            S((TOK, D), F32),
            S((TOK, FF), BF16),
            S((4, 3, ROWS, HALF), BF16),
            S((4, 3, ROWS, HALF), BF16),
        ],
        in_specs=[vmem] * 2 + [hbm] * 7,
        out_specs=[vmem, vmem, vmem, hbm, hbm],
        scratch_shapes=[
            V((TOK, D), F32),
            V((TOK, D), BF16),
            V((D, FF), BF16),
            V((4, 2, ROWS, FF), BF16),
            V((8, 4, ROWS, 256), BF16),
            V((8, 4, ROWS, 256), BF16),
            V((8, 3, ROWS, 256), BF16),
            V((8, ROWS, 256), BF16),
            V((8, ROWS, 256), BF16),
            V((D, 256), BF16),
            V((1024, D), BF16),
            V((512, HALF), BF16),
            V((TOK, 1024), BF16),
            V((TOK, 512), BF16),
            V((TOK, FF), BF16),
            V((TOK, D), BF16),
            V((D, FF), BF16),
            V((FF, FF), BF16),
            V((D, FF), F32),
            sems(35),
            sems(8, 4),
            sems(8, 4),
            sems(8, 3),
            sems(8, 3),
            sems(8),
            sems(8),
            sems(8),
            sems(8),
            pltpu.SemaphoreType.DMA,
            pltpu.SemaphoreType.DMA,
            pltpu.SemaphoreType.DMA,
            pltpu.SemaphoreType.DMA,
            sems(8, 2),
            sems(4, 3),
            sems(8, 2),
            sems(4, 3),
        ],
        compiler_params=pltpu.CompilerParams(
            collective_id=2, has_side_effects=True, vmem_limit_bytes=60 * MiB
        ),
        name="update",
    )(choice_rows, gain, hid, gna, msum, mom, dw, omain, oleft)


def adam_update(weight, first, second, grad, rate, decay):
    first_new = 0.9 * first + 0.1 * grad
    second_new = 0.95 * second + 0.05 * grad * grad
    corrected = first_new / (1.0 - 0.9**10)
    denominator = jnp.sqrt(second_new / (1.0 - 0.95**10)) + 1e-08
    return (first_new, second_new, weight * (1.0 - rate * decay) - rate * corrected / denominator)


def shards(
    hidden_in,
    out_grad,
    expert_choice,
    segments,
    expert_weights,
    expert_moment,
    attention_weights,
    attention_first,
    attention_second,
    router_weights,
    router_first,
    router_second,
    norm_gains,
    gains_first,
    gains_second,
):
    tensor = lax.axis_index("tensor")
    choice_rows = expert_choice.T
    fwd = run_forward(
        hidden_in,
        out_grad,
        choice_rows,
        segments,
        attention_weights,
        router_weights,
        norm_gains,
        expert_weights,
    )
    resid, gain = fwd[5], fwd[9]
    mlow = (0.95 * expert_moment).astype(BF16)
    bwd = run_backward(choice_rows, segments, fwd, out_grad, mlow)
    gres = bwd[1]
    fin, term, moe, ghome, ohome = run_update(choice_rows, hidden_in, gain, bwd)

    layer_output = lax.dynamic_slice_in_dim(resid, tensor * FF, FF, 1) + moe.astype(F32)
    input_grad = gres + term
    moment_new = 0.95 * expert_moment + ghome.astype(F32)
    rates = jnp.array(MUON_RATES, F32)[None, :, None, None]
    expert_new = expert_weights * (1.0 - rates * 0.1) - rates * (0.2 * D**0.5) * ohome.astype(F32)
    slot_rates = jnp.where(jnp.arange(14) >= 8, 0.5, 0.05)[None, :, None, None]
    grads = fin.astype(F32)
    attention_grad = grads[0:7].reshape(7, ROWS, 2, 128).transpose(0, 2, 1, 3)
    attention_out = adam_update(
        attention_weights,
        attention_first,
        attention_second,
        attention_grad.reshape(1, 14, ROWS, 128),
        slot_rates,
        0.1,
    )
    router_out = adam_update(
        router_weights, router_first, router_second, grads[7, :, 0:32], 0.025, 0.1
    )
    gains_grad = jnp.stack([grads[7, :, 33], grads[7, :, 32]])
    gains_out = adam_update(norm_gains, gains_first, gains_second, gains_grad, 1.0, 0.0)
    return (
        layer_output,
        input_grad,
        moment_new,
        expert_new,
        *attention_out,
        *router_out,
        *gains_out,
    )


def solution(mesh):
    tokens = P(("dp", "ctx"), None)
    expert = P("dp", None, "ctx", "tensor")
    attention = P("tensor", None, "ctx", None)
    router = P("ctx", None)
    gains = P(None, "ctx")
    return jax.shard_map(
        shards,
        mesh=mesh,
        in_specs=(
            (tokens,) * 3
            + (P("dp", None),)
            + (expert,) * 2
            + (attention,) * 3
            + (router,) * 3
            + (gains,) * 3
        ),
        out_specs=(
            (P(("dp", "ctx"), "tensor"), tokens)
            + (expert,) * 2
            + (attention,) * 3
            + (router,) * 3
            + (gains,) * 3
        ),
        check_vma=False,
    )
```

```python
import functools

import jax
import jax.numpy as jnp
from jax import lax
from jax.experimental import pallas as pl
from jax.experimental.pallas import tpu as pltpu
from jax.sharding import PartitionSpec as P

MESH = pl.DeviceIdType.MESH
F32 = jnp.float32
BF16 = jnp.bfloat16
EPS = 1e-06
TOK = 256
D = 1536
FF = 768
ROWS = 192
HALF = 384
SCALE = 128.0 ** (-0.5)
MiB = 2**20


def dot(a, b):
    return jnp.dot(a, b, preferred_element_type=F32)


def dot_nt(a, b):
    return lax.dot_general(a, b, (((1,), (1,)), ((), ())), preferred_element_type=F32)


def dot_tn(a, b):
    return lax.dot_general(a, b, (((0,), (0,)), ((), ())), preferred_element_type=F32)


def iota(shape, axis):
    return lax.broadcasted_iota(jnp.int32, shape, axis)


def remote(src, dst, send_sem, recv_sem, **device):
    return pltpu.make_async_remote_copy(
        src_ref=src,
        dst_ref=dst,
        send_sem=send_sem,
        recv_sem=recv_sem,
        device_id=device,
        device_id_type=MESH,
    )


def local(src, dst, sem):
    return pltpu.make_async_copy(src, dst, sem)


def place():
    ctx = lax.axis_index("ctx")
    return lax.axis_index("dp"), ctx, lax.axis_index("tensor"), lax.div(ctx, 2), lax.rem(ctx, 2)


def row_to_column(row):
    n = row.shape[1]
    same = iota((n, n), 0) == iota((n, n), 1)
    return jnp.sum(jnp.where(same, row, jnp.zeros_like(row)), axis=1, keepdims=True)


def codes_by_expert(choice_rows):
    expert = iota((32, TOK), 0)
    hit = jnp.zeros((32, TOK), F32)
    for k in range(4):
        hit = hit + jnp.where(choice_rows[k : k + 1, :] == expert, 1.0, 0.0)
    before = jnp.where(iota((TOK, TOK), 0) < iota((TOK, TOK), 1), 1.0, 0.0).astype(BF16)
    slot = dot(hit.astype(BF16), before)
    return jnp.where(hit > 0.5, slot, -1.0)


def codes_by_token(choice_rows):
    expert = iota((TOK, 128), 1)
    hit = jnp.zeros((TOK, 128), F32)
    for k in range(4):
        hit = hit + jnp.where(row_to_column(choice_rows[k : k + 1, :]) == expert, 1.0, 0.0)
    before = jnp.where(iota((TOK, TOK), 0) > iota((TOK, TOK), 1), 1.0, 0.0).astype(BF16)
    slot = dot(before, hit.astype(BF16))
    return hit, jnp.where(hit > 0.5, slot, -1.0)


def fill_onehot(code_ref, main_ref, left_ref):
    def one(e, carry):
        code = code_ref[pl.ds(e, 1), :]
        main_ref[pl.ds(pl.multiple_of(e * 32, 32), 32), :] = jnp.where(
            iota((32, TOK), 0).astype(F32) == code, 1.0, 0.0
        ).astype(BF16)
        left_ref[pl.ds(pl.multiple_of(e * 16, 16), 16), :] = jnp.where(
            (32 + lax.rem(iota((16, TOK), 0), 4)).astype(F32) == code, 1.0, 0.0
        ).astype(BF16)
        return carry

    lax.fori_loop(0, 32, one, 0)


def pack_rows(onehot_main, onehot_left, rows_ref, out_main, out_left):
    width = rows_ref.shape[1]

    def main_block(b, carry):
        at = pl.ds(pl.multiple_of(b * 256, 256), 256)
        out_main[at, :] = dot(onehot_main[at, :], rows_ref[...]).astype(BF16)
        return carry

    lax.fori_loop(0, 4, main_block, 0)

    def left_block(b, carry):
        at = pl.ds(pl.multiple_of(b * 256, 256), 256)
        quarter = lax.rem(lax.div(iota((256, HALF), 0), 4), 4)
        total = jnp.zeros((256, HALF), F32)
        for q in range(4):
            piece = dot(onehot_left[at, :], rows_ref[:, q * HALF : (q + 1) * HALF])
            total = total + jnp.where(quarter == q, piece, 0.0)
        out_left[at, 0:HALF] = total.astype(BF16)
        if width > D:
            out_left[at, HALF:] = dot(onehot_left[at, :], rows_ref[:, D:]).astype(BF16)
        return carry

    lax.fori_loop(0, 2, left_block, 0)


def plane_for(dp, to_dp, ten):
    return jnp.where(lax.div(dp, 4) == lax.div(to_dp, 4), ten, 1 - ten)


def send_rows(src_main, src_left, dst_main, dst_left, send_sem, recv_sem):
    dp, ctx, ten, z, c = place()
    core = lax.rem(z, 2)
    source = dp * 2 + lax.div(z, 2)

    def one(e, carry):
        to_dp, to_z = lax.div(e, 4), lax.rem(e, 4)
        here = (to_dp == dp) & (to_z == z) & (c == core)
        for i, (src, dst, n) in enumerate(((src_main, dst_main, 32), (src_left, dst_left, 16))):
            src_at = src.at[pl.ds(pl.multiple_of(e * n, n), n)]
            dst_at = dst.at[pl.ds(pl.multiple_of(source * n, n), n)]

            @pl.when(here)
            def _(i=i, src_at=src_at, dst_at=dst_at):
                local(src_at, dst_at, recv_sem.at[i, source]).start()

            @pl.when(jnp.logical_not(here))
            def _(i=i, src_at=src_at, dst_at=dst_at):
                remote(
                    src_at,
                    dst_at,
                    send_sem.at[i, e],
                    recv_sem.at[i, source],
                    dp=to_dp,
                    ctx=to_z * 2 + core,
                    tensor=plane_for(dp, to_dp, ten),
                ).start()

        return carry

    lax.fori_loop(0, 32, one, 0)


def wait_sent_rows(src_main, src_left, dst_main, dst_left, send_sem, recv_sem):
    dp, ctx, ten, z, c = place()

    def one(e, carry):
        here = (lax.div(e, 4) == dp) & (lax.rem(e, 4) == z) & (c == lax.rem(z, 2))

        @pl.when(jnp.logical_not(here))
        def _():
            for i, (src, dst, n) in enumerate(((src_main, dst_main, 32), (src_left, dst_left, 16))):
                remote(
                    src.at[pl.ds(pl.multiple_of(e * n, n), n)],
                    dst.at[pl.ds(0, n)],
                    send_sem.at[i, e],
                    recv_sem.at[i, 0],
                    dp=dp,
                    ctx=ctx,
                    tensor=1 - ten,
                ).wait_send()

        return carry

    lax.fori_loop(0, 32, one, 0)


def wait_received_rows(src_main, src_left, dst_main, dst_left, send_sem, recv_sem):
    dp, ctx, ten, z, c = place()

    def one(s, carry):
        for i, (src, dst, n) in enumerate(((src_main, dst_main, 32), (src_left, dst_left, 16))):
            remote(
                src.at[pl.ds(0, n)],
                dst.at[pl.ds(pl.multiple_of(s * n, n), n)],
                send_sem.at[i, 0],
                recv_sem.at[i, s],
                dp=dp,
                ctx=ctx,
                tensor=1 - ten,
            ).wait_recv()
        return carry

    lax.fori_loop(0, 16, one, 0)


def greet_row_senders(barrier):
    dp, ctx, ten, z, c = place()
    main = c == ten

    def one(s, carry):
        from_dp, from_z = lax.div(s, 2), lax.rem(s, 2) * 2 + c
        plane = plane_for(dp, from_dp, ten)
        here = main & (from_dp == dp) & (from_z == z)

        @pl.when(jnp.logical_not(here))
        def _():
            pl.semaphore_signal(
                barrier,
                inc=1,
                device_id={"dp": from_dp, "ctx": from_z * 2 + plane, "tensor": plane},
                device_id_type=MESH,
            )

        return carry

    lax.fori_loop(0, 16, one, 0)
    self_in = (c == lax.rem(z, 2)).astype(jnp.int32)
    return jnp.where(main, 32 - self_in, 0)


def forward_kernel(
    choice_ref,
    seg_ref,
    rw_ref,
    gains_ref,
    hid_h,
    og_h,
    aw_h,
    ew_h,
    lse_ref,
    gate_ref,
    gain_ref,
    router_ref,
    q_h,
    kv_h,
    heads_h,
    w_h,
    resid_h,
    nba_h,
    nbb_h,
    wexp_ref,
    xmain_ref,
    xleft_ref,
    ogmain_ref,
    ogleft_ref,
    hid_ref,
    og_ref,
    aw_ref,
    ew_ref,
    elow_ref,
    q_ref,
    kv_ref,
    heads_ref,
    w_ref,
    resid_ref,
    nba_ref,
    nbb_ref,
    ld,
    st,
    ws,
    rs,
    gs,
    grecv,
    bias,
    code_ref,
    onehot_main,
    onehot_left,
    nbx,
    ogl,
    send_main,
    send_left,
    send_ogmain,
    send_ogleft,
    part,
    prec,
    za_s,
    za_r,
    xa_s,
    xa_r,
    ca_s,
    ca_r,
    sm_s,
    sm_r,
    kv_s,
    kv_r,
    kvf_s,
    kvf_r,
    pe_s,
    pe_r,
    og_s,
    og_r,
    x_s,
    x_r,
    wz_s,
    wz_r,
    wy_s,
    wy_r,
    wc_s,
    wc_r,
):
    dp, ctx, ten, z, c = place()
    main = c == ten
    core_peer = z * 2 + 1 - c

    def z_peer(d):
        return lax.rem(z + d, 4) * 2 + c

    loads = [
        pltpu.make_async_copy(src, dst, ld.at[i])
        for i, (src, dst) in enumerate(
            ((aw_h, aw_ref), (hid_h, hid_ref), (og_h, og_ref), (ew_h, ew_ref))
        )
    ]
    for copy in loads:
        copy.start()
    stores = []

    def store(src, dst):
        copy = pltpu.make_async_copy(src, dst, st.at[len(stores)])
        copy.start()
        stores.append(copy)

    barrier = pltpu.get_barrier_semaphore()
    for j in range(1, 8):
        pl.semaphore_signal(
            barrier, inc=1, device_id={"ctx": lax.rem(ctx + j, 8)}, device_id_type=MESH
        )
    pl.semaphore_signal(barrier, inc=1, device_id={"tensor": 1 - ten}, device_id_type=MESH)
    for j in range(1, 4):
        pl.semaphore_signal(
            barrier,
            inc=1,
            device_id={"dp": dp - lax.rem(dp, 4) + lax.rem(dp + j, 4)},
            device_id_type=MESH,
        )
    extra = greet_row_senders(barrier)

    loads[0].wait()
    for p in range(7):
        ws[p, :, 0:128] = aw_ref[0, 2 * p].astype(BF16)
        ws[p, :, 128:256] = aw_ref[0, 2 * p + 1].astype(BF16)
    spots = jnp.where(iota((32, 128), 0) == iota((32, 128), 1), 1.0, 0.0).astype(BF16)
    rs[...] = dot_tn(rw_ref[...].astype(BF16), spots).astype(BF16)
    shift = jnp.where(iota((ROWS, D), 1) == iota((ROWS, D), 0) + ctx * ROWS, 1.0, 0.0).astype(BF16)
    gs[...] = jnp.zeros_like(gs)
    gs[0:2, :] = dot(gains_ref[...].astype(BF16), shift)

    pl.semaphore_wait(barrier, 11 + extra)

    def rows_at(index):
        return pl.ds(pl.multiple_of(index * ROWS, 64), ROWS)

    small = []
    for j in range(1, 8):
        to = lax.rem(ctx + j, 8)
        for i, (src, dst) in enumerate(
            ((gs, grecv.at[j - 1]), (rs, router_ref.at[rows_at(ctx)]))
        ):
            copy = remote(src, dst, sm_s.at[i, j - 1], sm_r.at[i, j - 1], ctx=to)
            copy.start()
            small.append(copy)
    router_ref[rows_at(ctx), :] = rs[...]

    groups = ((3, 1), (0, 3), (4, 3))
    xx = lax.rem(dp, 4)
    weight_copies = {}

    def x_peer(j):
        return dp - xx + lax.rem(xx + j, 4)

    def quarter(index):
        return pl.ds(pl.multiple_of(index * ROWS + xx * 48, 16), 48)

    def start_group(g):
        first, count = groups[g]
        pairs = pl.ds(first, count)
        for d in (1, 3, 2):
            copy = remote(
                ws.at[pairs, quarter(0)],
                w_ref.at[pairs, quarter(ctx)],
                za_s.at[g, d - 1],
                za_r.at[g, d - 1],
                ctx=z_peer(d),
            )
            copy.start()
            weight_copies[g, "z", d] = copy
        copy = remote(
            ws.at[pairs], w_ref.at[pairs, rows_at(ctx)], ca_s.at[g, 0], ca_r.at[g, 0], ctx=core_peer
        )
        copy.start()
        weight_copies[g, "c", 0] = copy
        w_ref[first : first + count, rows_at(ctx), :] = ws[first : first + count]

    def spread_group(g):
        pairs = pl.ds(*groups[g])
        for d in (1, 3, 2):
            weight_copies[g, "z", d].wait_recv()
            block = w_ref.at[pairs, quarter(lax.rem(z + 4 - d, 4) * 2 + c)]
            for j in (1, 3, 2):
                copy = remote(
                    block, block, xa_s.at[g, d - 1, j - 1], xa_r.at[g, d - 1, j - 1], dp=x_peer(j)
                )
                copy.start()
                weight_copies[g, "x", d, j] = copy

    def join_group(g):
        first, count = groups[g]
        pairs = pl.ds(first, count)
        for d in (1, 3, 2):
            for j in (1, 3, 2):
                weight_copies[g, "x", d, j].wait_recv()
            share = w_ref.at[pairs, rows_at(lax.rem(z + 4 - d, 4) * 2 + c)]
            copy = remote(share, share, ca_s.at[g, d], ca_r.at[g, d], ctx=core_peer)
            copy.start()
            weight_copies[g, "c", d] = copy
        for d in (0, 1, 3, 2):
            weight_copies[g, "c", d].wait_recv()
        store(w_ref.at[pairs], w_h.at[pairs])

    for g in range(3):
        start_group(g)

    seg_here = seg_ref[:, pl.ds(pl.multiple_of(ctx * TOK, TOK), TOK)]
    seg_col = row_to_column(seg_here)
    for b in range(8):
        at = slice(b * 256, (b + 1) * 256)
        key_pos = b * 256 + iota((TOK, 256), 1)
        query_pos = ctx * TOK + iota((TOK, 256), 0)
        allowed = (key_pos <= query_pos) & (seg_ref[:, at] == seg_col)
        bias[:, at] = jnp.where(allowed, 0.0, -1e30)
    spread_group(0)
    spread_group(1)

    for copy in small:
        copy.wait_recv()
    gain_ref[...] = gs[...]
    for j in range(7):
        gain_ref[...] += grecv[j]
    loads[1].wait()
    hid = hid_ref[...]
    inverse = lax.rsqrt(jnp.mean(hid * hid, axis=1, keepdims=True) + EPS)
    nba_ref[...] = (hid * inverse * gain_ref[0:1, :]).astype(BF16)
    store(nba_ref, nba_h)

    loads[3].wait()
    cols = pl.ds(pl.multiple_of(ten * HALF, 128), HALF)
    spread = {}

    def lower(i, carry):
        elow_ref[i] = ew_ref[i].astype(BF16)
        return carry

    lax.fori_loop(0, 4, lower, 0)

    def send_kind(k):
        for d in range(4):
            to_z = lax.rem(z + d, 4)
            src, dst = elow_ref.at[to_z, k], wexp_ref.at[k, z, c, :, cols]
            if d == 0:
                copy = pltpu.make_async_copy(src, dst, wz_r.at[k, 0])
            else:
                copy = remote(src, dst, wz_s.at[k, d], wz_r.at[k, d], ctx=z_peer(d))
            copy.start()
            spread[k, d] = copy

    def pass_kind(k):
        for d in range(4):
            if d == 0:
                spread[k, d].wait()
            else:
                spread[k, d].wait_recv()
        own = wexp_ref.at[k, :, c, :, cols]
        spread[k, "y"] = remote(own, own, wy_s.at[k], wy_r.at[k], tensor=1 - ten)
        spread[k, "c"] = remote(own, own, wc_s.at[k, 0], wc_r.at[k, 0], ctx=core_peer)
        spread[k, "y"].start()
        spread[k, "c"].start()

    send_kind(0)

    forwards = {}

    def kv_rows(index):
        return kv_ref.at[pl.ds(pl.multiple_of(index * TOK, TOK), TOK)]

    join_group(0)
    kv_ref[pl.ds(pl.multiple_of(ctx * TOK, TOK), TOK), :] = dot(nba_ref[...], w_ref[3]).astype(BF16)
    kv_copies = {}
    for d in (1, 3, 2, 0):
        to = core_peer if d == 0 else z_peer(d)
        copy = remote(kv_rows(ctx), kv_rows(ctx), kv_s.at[d], kv_r.at[d], ctx=to)
        copy.start()
        kv_copies[d] = copy
    spread_group(2)
    pass_kind(0)

    choice = choice_ref[...]
    hit, _ = codes_by_token(choice)
    loads[2].wait()

    @pl.when(main)
    def _():
        code_ref[...] = codes_by_expert(choice)
        fill_onehot(code_ref, onehot_main, onehot_left)
        ogl[...] = og_ref[...].astype(BF16)
        pack_rows(onehot_main, onehot_left, ogl, send_ogmain, send_ogleft)

    join_group(1)
    for p in range(3):
        q_ref[p] = dot(nba_ref[...], w_ref[p]).astype(BF16)
    store(q_ref, q_h)

    for d in (1, 3, 2):
        kv_copies[d].wait_recv()
        rows = kv_rows(lax.rem(z + 4 - d, 4) * 2 + c)
        fcopy = remote(rows, rows, kvf_s.at[d - 1], kvf_r.at[d - 1], ctx=core_peer)
        fcopy.start()
        forwards["kv", d] = fcopy
    kv_copies[0].wait_recv()
    for d in (1, 3, 2):
        forwards["kv", d].wait_recv()
    store(kv_ref, kv_h)

    og_args = (send_ogmain, send_ogleft, ogmain_ref, ogleft_ref, og_s, og_r)
    x_args = (send_main, send_left, xmain_ref, xleft_ref, x_s, x_r)

    @pl.when(main)
    def _():
        send_rows(*og_args)

    send_kind(1)
    send_kind(2)

    lse_ref[...] = jnp.zeros_like(lse_ref)
    outgoing = []
    for half in range(2):
        at = slice(half * 128, (half + 1) * 128)
        for j in range(6):
            lanes = slice((j % 2) * 128, (j % 2) * 128 + 128)
            scores = dot_nt(q_ref[j // 2, at, lanes], kv_ref[:, 0:128]) * SCALE + bias[at, :]
            top = jnp.max(scores, axis=1, keepdims=True)
            terms = jnp.exp(scores - top)
            total = jnp.sum(terms, axis=1, keepdims=True)
            mixed = dot(terms.astype(BF16), kv_ref[:, 128:256]) / total
            heads_ref[j // 2, at, lanes] = mixed.astype(BF16)
            lse_ref[at, :] = jnp.where(
                iota((128, 128), 1) == j, top + jnp.log(total), lse_ref[at, :]
            )
        if half == 0:
            join_group(2)
        total = dot_nt(heads_ref[0, at, :], w_ref[4])
        total = total + dot_nt(heads_ref[1, at, :], w_ref[5])
        total = total + dot_nt(heads_ref[2, at, :], w_ref[6])
        part[at, :] = total.astype(BF16)
        copy = remote(part.at[at], prec.at[at], pe_s.at[half], pe_r.at[half], tensor=1 - ten)
        outgoing.append(copy)

        @pl.when(jnp.logical_not(main))
        def _(copy=copy):
            copy.start()

    for copy in outgoing:

        @pl.when(main)
        def _(copy=copy):
            copy.wait_recv()
            copy.start()

        @pl.when(jnp.logical_not(main))
        def _(copy=copy):
            copy.wait_recv()

    pass_kind(1)
    pass_kind(2)
    resid = hid_ref[...] + (part[...].astype(F32) + prec[...].astype(F32))
    resid_ref[...] = resid
    store(resid_ref, resid_h)
    store(heads_ref, heads_h)
    inverse = lax.rsqrt(jnp.mean(resid * resid, axis=1, keepdims=True) + EPS)
    nbb = (resid * inverse * gain_ref[1:2, :]).astype(BF16)
    nbb_ref[...] = nbb
    store(nbb_ref, nbb_h)
    logits = jnp.where(hit > 0.5, dot(nbb, router_ref[...]), -1e30)
    top = jnp.max(logits, axis=1, keepdims=True)
    terms = jnp.where(hit > 0.5, jnp.exp(logits - top), 0.0)
    gates = terms / jnp.sum(terms, axis=1, keepdims=True)
    gate_ref[...] = gates

    @pl.when(main)
    def _():
        nbx[:, 0:D] = nbb
        high = gates.astype(BF16).astype(F32)
        nbx[:, D:] = (high + pltpu.roll(gates - high, 32, 1)).astype(BF16)
        pack_rows(onehot_main, onehot_left, nbx, send_main, send_left)
        send_rows(*x_args)

    for k in range(3):
        spread[k, "y"].wait_recv()
        there = wexp_ref.at[k, :, c, :, pl.ds(pl.multiple_of((1 - ten) * HALF, 128), HALF)]
        spread[k, "cy"] = remote(there, there, wc_s.at[k, 1], wc_r.at[k, 1], ctx=core_peer)
        spread[k, "cy"].start()
    for k in range(3):
        spread[k, "c"].wait_recv()
        spread[k, "cy"].wait_recv()
        for d in (1, 2, 3):
            spread[k, d].wait_send()
        for name in ("y", "c", "cy"):
            spread[k, name].wait_send()
    wait_received_rows(*og_args)
    wait_received_rows(*x_args)

    @pl.when(main)
    def _():
        wait_sent_rows(*og_args)
        wait_sent_rows(*x_args)

    for copy in small + list(weight_copies.values()) + list(forwards.values()) + list(kv_copies.values()):
        copy.wait_send()
    for copy in outgoing:
        copy.wait_send()
    for copy in stores:
        copy.wait()


def sems(*shape):
    return pltpu.SemaphoreType.DMA(shape)


def run_forward(hid, og, choice_rows, seg, aw, rw, gains, ew):
    vmem = pl.BlockSpec(memory_space=pltpu.VMEM)
    hbm = pl.BlockSpec(memory_space=pl.ANY)
    S = jax.ShapeDtypeStruct
    V = pltpu.VMEM
    kept = [
        ((3, TOK, 256), BF16),
        ((2048, 256), BF16),
        ((3, TOK, 256), BF16),
        ((7, D, 256), BF16),
        ((TOK, D), F32),
        ((TOK, D), BF16),
        ((TOK, D), BF16),
    ]
    outs = [
        S((TOK, 128), F32),
        S((TOK, 128), F32),
        S((8, D), F32),
        S((D, 128), BF16),
        *(S(*shape) for shape in kept),
        S((3, 4, 2, ROWS, FF), BF16),
        S((512, D + 128), BF16),
        S((256, HALF + 128), BF16),
        S((512, D), BF16),
        S((256, HALF), BF16),
    ]
    lse, gate, gain, router, *rest = pl.pallas_call(
        forward_kernel,
        out_shape=outs,
        in_specs=[vmem] * 4 + [hbm] * 4,
        out_specs=[vmem] * 4 + [hbm] * 12,
        scratch_shapes=[
            V((TOK, D), F32),
            V((TOK, D), F32),
            V((1, 14, ROWS, 128), F32),
            V((4, 3, ROWS, HALF), F32),
            V((4, 3, ROWS, HALF), BF16),
            *(V(*shape) for shape in kept),
            sems(4),
            sems(16),
            V((7, ROWS, 256), BF16),
            V((ROWS, 128), BF16),
            V((8, D), F32),
            V((7, 8, D), F32),
            V((TOK, 2048), F32),
            V((32, TOK), F32),
            V((1024, TOK), BF16),
            V((512, TOK), BF16),
            V((TOK, D + 128), BF16),
            V((TOK, D), BF16),
            V((1024, D + 128), BF16),
            V((512, HALF + 128), BF16),
            V((1024, D), BF16),
            V((512, HALF), BF16),
            V((TOK, D), BF16),
            V((TOK, D), BF16),
            sems(3, 3),
            sems(3, 3),
            sems(3, 3, 3),
            sems(3, 3, 3),
            sems(3, 4),
            sems(3, 4),
            sems(2, 7),
            sems(2, 7),
            sems(4),
            sems(4),
            sems(3),
            sems(3),
            sems(2),
            sems(2),
            sems(2, 32),
            sems(2, 16),
            sems(2, 32),
            sems(2, 16),
            sems(3, 4),
            sems(3, 4),
            sems(3),
            sems(3),
            sems(3, 2),
            sems(3, 2),
        ],
        compiler_params=pltpu.CompilerParams(
            collective_id=0, has_side_effects=True, vmem_limit_bytes=56 * MiB
        ),
        name="attention_forward",
    )(choice_rows, seg, rw.T, gains, hid, og, aw, ew)
    q, kv, heads, w, resid, nba, nbb, *sent = rest
    return (q, kv, heads, lse, w, resid, nba, nbb, gate, gain, router, *sent)


GATE, UP, DOWN = 0, 1, 2
OWNER_CORE = (0, 1, 1)
CORE_SLOT = (0, 0, 1)
GELU_A = 0.7978845608028654
GELU_B = 0.044715


def owner_plane(k):
    _, _, _, z, _ = place()
    return lax.rem(z, 2) if k != UP else 1 - lax.rem(z, 2)


def is_owner(c, ten):
    return jnp.logical_not((c == 0) & (ten != owner_plane(GATE)))


def half_columns(index):
    return pl.ds(pl.multiple_of(index * HALF, 128), HALF)


def greet_group(barrier):
    _, ctx, ten, _, _ = place()
    for j in range(8):
        for t in range(2):
            if j or t:
                pl.semaphore_signal(
                    barrier,
                    inc=1,
                    device_id={"ctx": lax.rem(ctx + j, 8), "tensor": lax.rem(ten + t, 2)},
                    device_id_type=MESH,
                )


def send_block(src, dst, send_sem, recv_sem, to_ctx, to_ten):
    _, ctx, ten, _, _ = place()
    here = (ctx == to_ctx) & (ten == to_ten)

    @pl.when(here)
    def _():
        local(src, dst, recv_sem).start()

    @pl.when(jnp.logical_not(here))
    def _():
        remote(src, dst, send_sem, recv_sem, ctx=to_ctx, tensor=to_ten).start()


def wait_block_sent(src, dst, send_sem, recv_sem, to_ctx, to_ten):
    _, ctx, ten, _, _ = place()
    here = (ctx == to_ctx) & (ten == to_ten)

    @pl.when(jnp.logical_not(here))
    def _():
        remote(src, dst, send_sem, recv_sem, ctx=to_ctx, tensor=to_ten).wait_send()


def wait_block_received(block, send_sem, recv_sem):
    _, ctx, ten, _, _ = place()
    remote(block, block, send_sem, recv_sem, ctx=ctx, tensor=1 - ten).wait_recv()


def return_rows(src_main, src_left, dst_main, dst_left, send_sem, recv_sem):
    dp, ctx, ten, z, c = place()
    expert = dp * 4 + z

    def one(s, carry):
        to_dp, to_z = lax.div(s, 2), lax.rem(s, 2) * 2 + c
        plane = plane_for(dp, to_dp, ten)
        here = (to_dp == dp) & (to_z == z) & (c == ten)
        for i, (src, dst, n) in enumerate(((src_main, dst_main, 32), (src_left, dst_left, 16))):
            src_at = src.at[pl.ds(pl.multiple_of(s * n, n), n)]
            dst_at = dst.at[pl.ds(pl.multiple_of(expert * n, n), n)]

            @pl.when(here)
            def _(i=i, src_at=src_at, dst_at=dst_at):
                local(src_at, dst_at, recv_sem.at[i, expert]).start()

            @pl.when(jnp.logical_not(here))
            def _(i=i, src_at=src_at, dst_at=dst_at):
                remote(
                    src_at,
                    dst_at,
                    send_sem.at[i, s],
                    recv_sem.at[i, expert],
                    dp=to_dp,
                    ctx=to_z * 2 + plane,
                    tensor=plane,
                ).start()

        return carry

    lax.fori_loop(0, 16, one, 0)


def wait_returned(src_main, src_left, dst_main, dst_left, send_sem, recv_sem):
    dp, ctx, ten, z, c = place()

    def one(e, carry):
        for i, (src, dst, n) in enumerate(((src_main, dst_main, 32), (src_left, dst_left, 16))):
            remote(
                src.at[pl.ds(0, n)],
                dst.at[pl.ds(pl.multiple_of(e * n, n), n)],
                send_sem.at[i, 0],
                recv_sem.at[i, e],
                dp=dp,
                ctx=ctx,
                tensor=1 - ten,
            ).wait_recv()
        return carry

    lax.fori_loop(0, 32, one, 0)


def wait_return_sent(src_main, src_left, dst_main, dst_left, send_sem, recv_sem):
    dp, ctx, ten, z, c = place()

    def one(s, carry):
        here = (lax.div(s, 2) == dp) & (lax.rem(s, 2) * 2 + c == z) & (c == ten)

        @pl.when(jnp.logical_not(here))
        def _():
            for i, (src, dst, n) in enumerate(((src_main, dst_main, 32), (src_left, dst_left, 16))):
                remote(
                    src.at[pl.ds(pl.multiple_of(s * n, n), n)],
                    dst.at[pl.ds(0, n)],
                    send_sem.at[i, s],
                    recv_sem.at[i, 0],
                    dp=dp,
                    ctx=ctx,
                    tensor=1 - ten,
                ).wait_send()

        return carry

    lax.fori_loop(0, 16, one, 0)


def greet_expert_devices(barrier):
    dp, ctx, ten, z, c = place()
    core = lax.rem(z, 2)

    def one(e, carry):
        to_dp, to_z = lax.div(e, 4), lax.rem(e, 4)
        here = (to_dp == dp) & (to_z == z) & (c == core)

        @pl.when(jnp.logical_not(here))
        def _():
            pl.semaphore_signal(
                barrier,
                inc=1,
                device_id={
                    "dp": to_dp,
                    "ctx": to_z * 2 + core,
                    "tensor": plane_for(dp, to_dp, ten),
                },
                device_id_type=MESH,
            )

        return carry

    @pl.when(c == ten)
    def _():
        lax.fori_loop(0, 32, one, 0)

    return 16 - ((c == ten) & (core == c)).astype(jnp.int32)


def left_picker(quarter):
    row, col = iota((64, 256), 0), iota((64, 256), 1)
    return jnp.where(col == lax.div(row, 4) * 16 + quarter * 4 + lax.rem(row, 4), 1.0, 0.0).astype(
        BF16
    )


def left_packer(quarter):
    row, col = iota((256, 64), 0), iota((256, 64), 1)
    return jnp.where(row == lax.div(col, 4) * 16 + quarter * 4 + lax.rem(col, 4), 1.0, 0.0).astype(
        BF16
    )


def fill_token_onehot(code, main_ref, left_ref):
    code = code.astype(BF16)
    for b in range(4):
        expert, col = iota((128, 256), 0), iota((128, 256), 1) + b * 256
        spread = dot(code, jnp.where(lax.div(col, 32) == expert, 1.0, 0.0).astype(BF16))
        slot = lax.rem(iota((TOK, 256), 1), 32).astype(F32)
        main_ref[:, b * 256 : (b + 1) * 256] = jnp.where(spread == slot, 1.0, 0.0).astype(BF16)
    for b in range(2):
        expert, col = iota((128, 256), 0), iota((128, 256), 1) + b * 256
        spread = dot(code, jnp.where(lax.div(col, 16) == expert, 1.0, 0.0).astype(BF16))
        slot = (32 + lax.rem(iota((TOK, 256), 1), 4)).astype(F32)
        left_ref[:, b * 256 : (b + 1) * 256] = jnp.where(spread == slot, 1.0, 0.0).astype(BF16)


def left_quarter(left_ref, quarter):
    keep = lax.rem(lax.div(iota((TOK, 512), 1), 4), 4) == quarter
    return jnp.where(keep, left_ref[...].astype(F32), 0.0).astype(BF16)


def backward_kernel(
    choice_ref,
    seg_ref,
    gate_ref,
    lse_ref,
    gain_ref,
    router_ref,
    xmain_h,
    xleft_h,
    ogmain_h,
    ogleft_h,
    wexp_h,
    w_h,
    q_h,
    kv_h,
    heads_h,
    nba_h,
    nbb_h,
    resid_h,
    og_h,
    mlow_h,
    dw_h,
    gres_ref,
    gna_ref,
    msum_ref,
    omain_h,
    oleft_h,
    xall,
    gx,
    xleft,
    ogall,
    ogleft,
    w9,
    ggp,
    gup,
    hidden,
    ghid,
    gmain,
    gleft,
    oleft,
    dw9,
    rcore,
    cmain,
    cleft,
    ptm,
    ptl,
    ext,
    kv,
    q,
    heads,
    nba,
    nbb,
    resid,
    gheads,
    gatt,
    dslab,
    dq,
    dkv,
    rkv,
    skv,
    r2kv,
    stage,
    ld,
    lw,
    dw_s,
    g_s,
    g_r,
    o_s,
    o_r,
    mc_s,
    mc_r,
    my_s,
    my_r,
    e_s,
    e_r,
    k1_s,
    k1_r,
    k2_s,
    k2_r,
    mo_s,
    mo_r,
):
    dp, ctx, ten, z, c = place()
    main = c == ten
    core_peer = z * 2 + 1 - c
    expert = dp * 4 + z

    def z_peer(d):
        return lax.rem(z + d, 4) * 2 + c

    barrier = pltpu.get_barrier_semaphore()
    greet_group(barrier)
    extra = greet_expert_devices(barrier)

    loads = [
        pltpu.make_async_copy(xmain_h.at[:, 0:D], xall.at[0:512], ld.at[0]),
        pltpu.make_async_copy(xmain_h.at[:, D:], gx.at[0:512], ld.at[1]),
        pltpu.make_async_copy(xleft_h, xleft, ld.at[2]),
        pltpu.make_async_copy(ogmain_h, ogall.at[0:512], ld.at[3]),
        pltpu.make_async_copy(ogleft_h, ogleft, ld.at[4]),
    ]
    expert_loads = []
    for n in range(3):
        for k in range(3):
            expert_loads.append(
                pltpu.make_async_copy(
                    wexp_h.at[k, :, n * 256 : (n + 1) * 256], w9.at[3 * k + n], lw.at[3 * k + n]
                )
            )
    later = [
        pltpu.make_async_copy(src, dst, ld.at[5 + i])
        for i, (src, dst) in enumerate(
            (
                (kv_h, kv),
                (q_h, q),
                (heads_h, heads),
                (nba_h, nba),
                (nbb_h, nbb),
                (resid_h, resid),
                (og_h, gres_ref),
            )
        )
    ]
    for copy in loads + expert_loads + later:
        copy.start()

    @pl.when(main)
    def _():
        _, code = codes_by_token(choice_ref[...])
        fill_token_onehot(code, ptm, ptl)

    for copy in loads:
        copy.wait()
    for n in range(4):
        at = slice(n * HALF, (n + 1) * HALF)
        pick = left_picker(n)
        xall[512:576, at] = dot(pick, xleft[:, 0:HALF]).astype(BF16)
        ogall[512:576, at] = dot(pick, ogleft[...]).astype(BF16)
    gx[512:576, :] = dot(left_picker(0), xleft[:, HALF:]).astype(BF16)
    lane = iota((576, 128), 1)
    mine = (lane == expert) | (lane == expert + 32)
    gate = jnp.sum(jnp.where(mine, gx[...].astype(F32), 0.0), axis=1, keepdims=True)

    pl.semaphore_wait(barrier, 15 + extra)
    wide = pl.ds(pl.multiple_of(ten * 128, 128), 256)
    narrow = pl.ds(pl.multiple_of((1 - ten) * 256, 128), 128)
    here_rows = pl.ds(pl.multiple_of(ctx * ROWS, 64), ROWS)

    def momentum(act):
        for k in range(3):
            for i in range(4):
                slot = 2 * CORE_SLOT[k]
                for part, (src, dst) in enumerate(
                    (
                        (mlow_h.at[i, k, :, wide], stage.at[slot, here_rows]),
                        (mlow_h.at[i, k, :, narrow], stage.at[slot + 1, here_rows, 0:128]),
                    )
                ):
                    act(
                        src,
                        dst,
                        mo_s.at[i, k, part],
                        mo_r.at[CORE_SLOT[k], ctx, part],
                        2 * i + OWNER_CORE[k],
                        ten,
                    )

    momentum(send_block)

    grad_gate = jnp.zeros((576, 1), F32)
    for n in range(3):
        for k in range(3):
            expert_loads[3 * n + k].wait()
        at = slice(n * 256, (n + 1) * 256)
        pre = dot(xall[...], w9[n])
        up = dot(xall[...], w9[3 + n])
        back = dot(ogall[...], w9[6 + n])
        bent = jnp.tanh(GELU_A * (pre + GELU_B * pre * pre * pre))
        value = 0.5 * pre * (1.0 + bent)
        slope = 0.5 * (1.0 + bent) + 0.5 * pre * (1.0 - bent * bent) * GELU_A * (
            1.0 + 3.0 * GELU_B * pre * pre
        )
        hid = (value * up).astype(BF16).astype(F32)
        grad_gate = grad_gate + jnp.sum(hid * back, axis=1, keepdims=True)
        scaled = back * gate
        ghid[:, at] = (hid * gate).astype(BF16)
        ggp[:, at] = (scaled * up * slope).astype(BF16)
        gup[:, at] = (scaled * value).astype(BF16)

    high = grad_gate.astype(BF16).astype(F32)
    marks = jnp.where(lane == expert, high, jnp.where(lane == expert + 32, grad_gate - high, 0.0))
    marks = marks.astype(BF16)
    gmain[:, D:] = marks[0:512]
    gleft[:, HALF:] = dot(left_packer(0), marks[512:576]).astype(BF16)
    packed = jnp.zeros((256, HALF), F32)
    for m in range(4):
        at = slice(m * HALF, (m + 1) * HALF)
        total = jnp.zeros((576, HALF), F32)
        for n in range(3):
            cols = slice(n * 256, (n + 1) * 256)
            total = total + dot_nt(ggp[:, cols], w9[n, at, :])
            total = total + dot_nt(gup[:, cols], w9[3 + n, at, :])
        gmain[:, at] = total[0:512].astype(BF16)
        packed = packed + dot(left_packer(m), total[512:576].astype(BF16))
    gleft[:, 0:HALF] = packed.astype(BF16)
    g_args = (gmain, gleft, cmain, cleft, g_s, g_r)
    o_args = (xall, oleft, omain_h, oleft_h, o_s, o_r)
    return_rows(*g_args)

    core_copies, plane_copies = {}, {}
    order = [(k, n) for k in (GATE, DOWN, UP) for n in range(3)]
    for k, n in order:
        at = slice(n * 256, (n + 1) * 256)
        rows, right = (ogall, ghid) if k == DOWN else (xall, ggp if k == GATE else gup)
        dw9[3 * k + n] = dot_tn(rows[...], right[:, at]).astype(BF16)
        copy = remote(
            dw9.at[3 * k + n],
            rcore.at[CORE_SLOT[k], n],
            mc_s.at[k, n],
            mc_r.at[k, n],
            ctx=core_peer,
        )
        core_copies[k, n] = copy

        @pl.when(c != OWNER_CORE[k])
        def _(copy=copy):
            copy.start()

    for k, n in order:
        plane_copies[k, n] = remote(
            dw9.at[3 * k + n],
            msum_ref.at[:, n * 256 : (n + 1) * 256],
            my_s.at[k, n],
            my_r.at[k, n],
            tensor=1 - ten,
        )

    def pass_on(k, n):
        @pl.when(ten != owner_plane(k))
        def _():
            plane_copies[k, n].start()

    for k in (GATE, DOWN, UP):
        for n in (0, 2):

            @pl.when((c == OWNER_CORE[k]) & (ten == 1 - n // 2))
            def _(k=k, n=n):
                core_copies[k, n].wait_recv()
                total = dw9[3 * k + n].astype(F32) + rcore[CORE_SLOT[k], n].astype(F32)
                dw9[3 * k + n] = total.astype(BF16)
                pass_on(k, n)

    for k in (GATE, DOWN, UP):

        @pl.when(c == OWNER_CORE[k])
        def _(k=k):
            slot = 2 * CORE_SLOT[k]
            for index in range(8):
                rows = pl.ds(index * ROWS, ROWS)
                for part, block in enumerate(
                    (stage.at[slot, rows], stage.at[slot + 1, rows, 0:128])
                ):
                    wait_block_received(
                        block, mo_s.at[0, 0, part], mo_r.at[CORE_SLOT[k], index, part]
                    )
            core_copies[k, 1].wait_recv()
            total = dw9[3 * k + 1].astype(F32) + rcore[CORE_SLOT[k], 1].astype(F32)
            low, high = total[:, 0:128], total[:, 128:256]
            more = stage[slot + 1, :, 0:128].astype(F32)
            dw9[3 * k + 1, :, 0:128] = jnp.where(ten == 0, low + more, low).astype(BF16)
            dw9[3 * k + 1, :, 128:256] = jnp.where(ten == 0, high, high + more).astype(BF16)
            pass_on(k, 1)
            for n in (0, 2):

                @pl.when(ten == n // 2)
                def _(n=n):
                    core_copies[k, n].wait_recv()
                    total = dw9[3 * k + n].astype(F32) + rcore[CORE_SLOT[k], n].astype(F32)
                    dw9[3 * k + n] = (total + stage[slot].astype(F32)).astype(BF16)

    packed = jnp.zeros((256, HALF), F32)
    for m in range(4):
        at = slice(m * HALF, (m + 1) * HALF)
        total = jnp.zeros((576, HALF), F32)
        for n in range(3):
            total = total + dot_nt(ghid[:, n * 256 : (n + 1) * 256], w9[6 + n, at, :])
        xall[0:512, at] = total[0:512].astype(BF16)
        packed = packed + dot(left_packer(m), total[512:576].astype(BF16))
    oleft[...] = packed.astype(BF16)

    weight_loads = [pltpu.make_async_copy(w_h.at[p], w9.at[p], lw.at[p]) for p in range(7)]
    for copy in weight_loads:
        copy.start()

    @pl.when(main)
    def _():
        wait_returned(*g_args)
        extras = dot(ptm[...], cmain[:, D:]) + dot(left_quarter(ptl, 0), cleft[:, HALF:])
        grads = jnp.where(iota((TOK, 128), 1) < 32, extras + pltpu.roll(extras, 96, 1), 0.0)
        gates = gate_ref[...]
        grad_logits = gates * (grads - jnp.sum(gates * grads, axis=1, keepdims=True))
        high = grad_logits.astype(BF16)
        low = (grad_logits - high.astype(F32)).astype(BF16)
        ext[:, D:] = (high.astype(F32) + pltpu.roll(low.astype(F32), 32, 1)).astype(BF16)
        for m in range(4):
            at = slice(m * HALF, (m + 1) * HALF)
            total = dot(ptm[...], cmain[:, at]) + dot(left_quarter(ptl, m), cleft[:, 0:HALF])
            total = total + dot_nt(high, router_ref[at, :]) + dot_nt(low, router_ref[at, :])
            ext[:, at] = total.astype(BF16)

    share = remote(ext, ext, e_s, e_r, tensor=1 - ten)

    @pl.when(main)
    def _():
        share.start()
        share.wait_send()

    @pl.when(jnp.logical_not(main))
    def _():
        share.wait_recv()

    for k in (GATE, DOWN, UP):
        for n in (0, 2):

            @pl.when((c == OWNER_CORE[k]) & (ten == n // 2))
            def _(k=k, n=n):
                pass_on(k, n)

    return_rows(*o_args)

    for copy in later:
        copy.wait()
    dslab[...] = jnp.zeros_like(dslab)

    def norm_rows(r, carry):
        at = pl.ds(pl.multiple_of(r * 64, 64), 64)
        gnb = ext[at, 0:D].astype(F32)
        value = resid[at, :]
        inverse = lax.rsqrt(jnp.mean(value * value, axis=1, keepdims=True) + EPS)
        scaled = gnb * gain_ref[1:2, :]
        inner = jnp.mean(scaled * value, axis=1, keepdims=True)
        gres = gres_ref[at, :] + inverse * scaled - value * (inverse * inverse * inverse) * inner
        gres_ref[at, :] = gres
        gatt[at, :] = gres.astype(BF16)
        flat = gnb * value * inverse
        high = flat.astype(BF16)
        low = (flat - high.astype(F32)).astype(BF16)
        lane = iota((64, 128), 1)
        ones = jnp.where(lane == 32, 1.0, 0.0).astype(BF16)
        both = ext[at, D:].astype(F32)
        logit_high = jnp.where(lane < 32, both, 0.0).astype(BF16)
        logit_low = jnp.where(lane < 32, pltpu.roll(both, 96, 1), 0.0).astype(BF16)
        rows = nbb[at, :]
        dslab[...] += (
            dot_tn(rows, logit_high) + dot_tn(rows, logit_low) + dot_tn(high, ones) + dot_tn(low, ones)
        )
        return carry

    lax.fori_loop(0, 4, norm_rows, 0)

    stores = {}

    def store(p, value):
        if p < 4:
            stores[p + 4].wait()
        stage[p % 4] = value
        stores[p] = pltpu.make_async_copy(stage.at[p % 4], dw_h.at[p], dw_s.at[p])
        stores[p].start()

    for copy in weight_loads:
        copy.wait()
    store(7, jnp.concatenate([dslab[...], jnp.zeros((D, 128), F32)], axis=1).astype(BF16))
    terms = jnp.zeros((TOK, 128), F32)
    for p in range(3):
        gheads[p] = dot(gatt[...], w9[4 + p]).astype(BF16)
        store(4 + p, dot_tn(gatt[...], heads[p]).astype(BF16))
        prod = gheads[p].astype(F32) * heads[p].astype(F32)
        for i in range(2):
            term = jnp.sum(prod[:, i * 128 : (i + 1) * 128], axis=1, keepdims=True)
            terms = jnp.where(iota((TOK, 128), 1) == 2 * p + i, term, terms)
    lse_rows = jnp.transpose(lse_ref[...])
    term_rows = jnp.transpose(terms)
    dkv[...] = jnp.zeros_like(dkv)
    dq[...] = jnp.zeros_like(dq)
    seg_here = seg_ref[:, pl.ds(pl.multiple_of(ctx * TOK, TOK), TOK)]

    def key_block(b, carry):
        at = pl.ds(pl.multiple_of(b * TOK, TOK), TOK)
        seg_col = row_to_column(seg_ref[:, at])
        key_pos = b * TOK + iota((TOK, TOK), 0)
        query_pos = ctx * TOK + iota((TOK, TOK), 1)
        allowed = (key_pos <= query_pos) & (seg_here == seg_col)
        keys, values = kv[at, 0:128], kv[at, 128:256]
        dk = jnp.zeros((TOK, 128), F32)
        dv = jnp.zeros((TOK, 128), F32)
        for j in range(6):
            lanes = slice((j % 2) * 128, (j % 2) * 128 + 128)
            qj, gj = q[j // 2, :, lanes], gheads[j // 2, :, lanes]
            scores = dot_nt(keys, qj) * SCALE
            probs = jnp.where(allowed, jnp.exp(scores - lse_rows[j : j + 1, :]), 0.0)
            grad = dot_nt(values, gj)
            grad_scores = (probs * (grad - term_rows[j : j + 1, :]) * SCALE).astype(BF16)
            dv = dv + dot(probs.astype(BF16), gj)
            dk = dk + dot(grad_scores, qj)
            dq[j // 2, :, lanes] += dot_tn(grad_scores, keys)
        dkv[at, 0:128] = dk.astype(BF16)
        dkv[at, 128:256] = dv.astype(BF16)
        return carry

    lax.fori_loop(0, ctx + 1, key_block, 0)

    pair = []
    for to_z in range(4):
        src = dkv.at[pl.ds(pl.multiple_of((to_z * 2 + 1 - c) * TOK, TOK), TOK)]
        copy = remote(src, rkv.at[to_z], k1_s.at[to_z], k1_r.at[to_z], ctx=core_peer)
        copy.start()
        pair.append(copy)
    for p in range(3):
        store(p, dot_tn(nba[...], dq[p].astype(BF16)).astype(BF16))
    total = dot_nt(dq[0].astype(BF16), w9[0])
    total = total + dot_nt(dq[1].astype(BF16), w9[1])
    total = total + dot_nt(dq[2].astype(BF16), w9[2])
    for to_z in range(4):
        pair[to_z].wait_recv()
        own = dkv[pl.ds(pl.multiple_of((to_z * 2 + c) * TOK, TOK), TOK), :]
        skv[to_z] = (own.astype(F32) + rkv[to_z].astype(F32)).astype(BF16)
    ring = []
    for d in (1, 3, 2):
        copy = remote(
            skv.at[lax.rem(z + d, 4)], r2kv.at[d - 1], k2_s.at[d - 1], k2_r.at[d - 1], ctx=z_peer(d)
        )
        copy.start()
        ring.append(copy)
    for copy in ring:
        copy.wait_recv()
    gkv = skv[z].astype(F32) + r2kv[0].astype(F32) + r2kv[1].astype(F32) + r2kv[2].astype(F32)
    gkv = gkv.astype(BF16)
    store(3, dot_tn(nba[...], gkv).astype(BF16))
    total = total + dot_nt(gkv, w9[3])
    gna_ref[...] = total.astype(BF16)

    for k in range(3):
        for n in range(3):
            plane = plane_copies[k, n]

            @pl.when((c == OWNER_CORE[k]) & (ten == owner_plane(k)))
            def _(k=k, n=n, plane=plane):
                plane.wait_recv()
                at = slice(n * 256, (n + 1) * 256)
                msum_ref[:, at] = (
                    dw9[3 * k + n].astype(F32) + msum_ref[:, at].astype(F32)
                ).astype(BF16)

            @pl.when((c == OWNER_CORE[k]) & (ten != owner_plane(k)))
            def _(plane=plane):
                plane.wait_send()

            @pl.when(c != OWNER_CORE[k])
            def _(k=k, n=n):
                core_copies[k, n].wait_send()

    @pl.when(jnp.logical_not(is_owner(c, ten)))
    def _():
        msum_ref[...] = jnp.zeros_like(msum_ref)

    momentum(wait_block_sent)
    for copy in pair + ring:
        copy.wait_send()
    wait_return_sent(*g_args)
    wait_return_sent(*o_args)

    @pl.when(main)
    def _():
        wait_returned(*o_args)

    for p in range(4):
        stores[p].wait()


def run_backward(choice_rows, seg, fwd, og, mlow):
    (q, kv, heads, lse, w, resid, nba, nbb, gate, gain, router, wexp, xm, xl, om, ol) = fwd
    vmem = pl.BlockSpec(memory_space=pltpu.VMEM)
    hbm = pl.BlockSpec(memory_space=pl.ANY)
    S = jax.ShapeDtypeStruct
    V = pltpu.VMEM
    return pl.pallas_call(
        backward_kernel,
        out_shape=[
            S((8, D, 256), BF16),
            S((TOK, D), F32),
            S((TOK, D), BF16),
            S((D, FF), BF16),
            S((1024, D), BF16),
            S((512, HALF), BF16),
        ],
        in_specs=[vmem] * 6 + [hbm] * 14,
        out_specs=[hbm, vmem, vmem, vmem, hbm, hbm],
        scratch_shapes=[
            V((576, D), BF16),
            V((576, 128), BF16),
            V((256, HALF + 128), BF16),
            V((576, D), BF16),
            V((256, HALF), BF16),
            V((9, D, 256), BF16),
            V((576, FF), BF16),
            V((576, FF), BF16),
            V((8, 128), BF16),
            V((576, FF), BF16),
            V((512, D + 128), BF16),
            V((256, HALF + 128), BF16),
            V((256, HALF), BF16),
            V((9, D, 256), BF16),
            V((2, 3, D, 256), BF16),
            V((1024, D + 128), BF16),
            V((512, HALF + 128), BF16),
            V((TOK, 1024), BF16),
            V((TOK, 512), BF16),
            V((TOK, D + 128), BF16),
            V((2048, 256), BF16),
            V((3, TOK, 256), BF16),
            V((3, TOK, 256), BF16),
            V((TOK, D), BF16),
            V((TOK, D), BF16),
            V((TOK, D), F32),
            V((3, TOK, 256), BF16),
            V((TOK, D), BF16),
            V((D, 128), F32),
            V((3, TOK, 256), F32),
            V((2048, 256), BF16),
            V((4, TOK, 256), BF16),
            V((4, TOK, 256), BF16),
            V((3, TOK, 256), BF16),
            V((4, D, 256), BF16),
            sems(12),
            sems(9),
            sems(8),
            sems(2, 16),
            sems(2, 32),
            sems(2, 16),
            sems(2, 32),
            sems(3, 3),
            sems(3, 3),
            sems(3, 3),
            sems(3, 3),
            pltpu.SemaphoreType.DMA,
            pltpu.SemaphoreType.DMA,
            sems(4),
            sems(4),
            sems(3),
            sems(3),
            sems(4, 3, 2),
            sems(2, 8, 2),
        ],
        compiler_params=pltpu.CompilerParams(
            collective_id=1, has_side_effects=True, vmem_limit_bytes=58 * MiB
        ),
        name="backward",
    )(
        choice_rows, seg, gate, lse, gain, router, xm, xl, om, ol, wexp.reshape(3, D, FF),
        w, q, kv, heads, nba, nbb, resid, og, mlow,
    )
NS_A = 3.4445
NS_B = -4.775
NS_C = 2.0315
MUON_RATES = (0.15, 0.15, 0.6)


def update_kernel(
    choice_ref,
    gain_ref,
    hid_h,
    gna_h,
    msum_h,
    dw_h,
    omain_h,
    oleft_h,
    fin_ref,
    term_ref,
    moe_ref,
    ghome_h,
    ohome_h,
    hid_ref,
    gna_ref,
    msum_ref,
    own,
    r1,
    r2,
    r3,
    s2,
    slab,
    omain,
    oleft,
    ptm,
    ptl,
    moe_send,
    gnap,
    ns_x,
    ns_b,
    ld,
    a_s,
    a_r,
    b_s,
    b_r,
    c_s,
    c_r,
    d_s,
    d_r,
    l_s,
    l_r,
    gn_s,
    gn_r,
    gh_s,
    gh_r,
    oh_s,
    oh_r,
):
    dp, ctx, ten, z, c = place()
    main = c == ten
    core_peer = z * 2 + 1 - c

    def z_peer(d):
        return lax.rem(z + d, 4) * 2 + c

    barrier = pltpu.get_barrier_semaphore()
    greet_group(barrier)
    for j in range(1, 8):
        pl.semaphore_signal(
            barrier, inc=1, device_id={"dp": lax.rem(dp + j, 8)}, device_id_type=MESH
        )

    loads = [
        pltpu.make_async_copy(dw_h.at[7], slab, ld.at[0]),
        pltpu.make_async_copy(omain_h, omain, ld.at[1]),
        pltpu.make_async_copy(oleft_h, oleft, ld.at[2]),
        pltpu.make_async_copy(gna_h, gna_ref, ld.at[31]),
        pltpu.make_async_copy(msum_h, msum_ref, ld.at[32]),
        pltpu.make_async_copy(hid_h, hid_ref, ld.at[33]),
    ]
    own_loads = []
    for p in range(7):
        for to_z in range(4):
            rows = pl.ds(pl.multiple_of((to_z * 2 + c) * ROWS, 64), ROWS)
            own_loads.append(
                pltpu.make_async_copy(dw_h.at[p, rows], own.at[p, to_z], ld.at[3 + p * 4 + to_z])
            )
    for copy in loads + own_loads:
        copy.start()

    owner = is_owner(c, ten)

    pl.semaphore_wait(barrier, 22)

    swap = remote(gna_ref, gnap, gn_s, gn_r, tensor=1 - ten)
    loads[3].wait()
    swap.start()

    def first(p, to_z):
        rows = pl.ds(pl.multiple_of((to_z * 2 + 1 - c) * ROWS, 64), ROWS)
        src = slab.at[rows] if p == 7 else dw_h.at[p, rows]
        return remote(src, r1.at[p, to_z], a_s.at[p, to_z], a_r.at[p, to_z], ctx=core_peer)

    def send_first(p):
        for to_z in range(4):
            first(p, to_z).start()

    for p in (4, 5, 6, 0, 1, 2, 3):
        send_first(p)

    def spread(src, dst_h, send_sem, recv_sem, act):
        for k in range(3):

            @pl.when((c == OWNER_CORE[k]) & (ten == owner_plane(k)))
            def _(k=k):
                for to in range(8):
                    for t in range(2):
                        act(
                            src.at[to * ROWS : (to + 1) * ROWS, t * HALF : (t + 1) * HALF],
                            dst_h.at[z, k],
                            send_sem.at[to, t],
                            recv_sem.at[z, k],
                            to,
                            t,
                        )

    def second(p, d):
        return remote(
            own.at[p, lax.rem(z + d, 4)],
            r2.at[p, d - 1],
            b_s.at[p, d - 1],
            b_r.at[p, d - 1],
            ctx=z_peer(d),
        )

    def send_second(p):
        for to_z in range(4):
            first(p, to_z).wait_recv()
        own[p] = (own[p].astype(F32) + r1[p].astype(F32)).astype(BF16)
        for d in (1, 3, 2):
            second(p, d).start()

    for copy in loads[4:]:
        copy.wait()

    @pl.when(owner)
    def _():
        whole = msum_ref[...].astype(F32)
        norm = jnp.sqrt(jnp.sum(whole * whole)) + 1e-07
        ns_x[...] = (whole / norm).astype(BF16)

    def norm_and_first():
        loads[0].wait()
        swap.wait_recv()
        gna = gna_ref[...].astype(F32) + gnap[...].astype(F32)
        hid = hid_ref[...]
        inverse = lax.rsqrt(jnp.mean(hid * hid, axis=1, keepdims=True) + EPS)
        scaled = gna * gain_ref[0:1, :]
        inner = jnp.mean(scaled * hid, axis=1, keepdims=True)
        term_ref[...] = inverse * scaled - hid * (inverse * inverse * inverse) * inner
        flat = gna * hid * inverse
        high = flat.astype(BF16)
        low = (flat - high.astype(F32)).astype(BF16)
        ones = jnp.where(iota((TOK, 128), 1) == 33, 1.0, 0.0).astype(BF16)
        slab[:, 0:128] = (slab[:, 0:128].astype(F32) + dot_tn(high, ones) + dot_tn(low, ones)).astype(BF16)

        send_first(7)
        for to_z in range(4):
            rows = pl.ds(pl.multiple_of((to_z * 2 + c) * ROWS, 64), ROWS)
            own[7, to_z] = slab[rows, :]

    def finish(pairs):
        for p in pairs:
            total = own[p, z].astype(F32)
            for d in (1, 2, 3):
                second(p, d).wait_recv()
                total = total + r2[p, d - 1].astype(F32)
            s2[p] = total.astype(BF16)

            @pl.when(p != dp)
            def _(p=p):
                remote(s2.at[p], r3.at[dp], c_s.at[p], c_r.at[dp], dp=p).start()

            @pl.when(p == dp)
            def _(p=p):
                r3[dp] = s2[p]

    def step(turn, carry):
        @pl.when(owner)
        def _():
            gram = dot_tn(ns_x[...], ns_x[...]).astype(BF16)
            ns_b[...] = gram
            square = dot(ns_b[...], ns_b[...])
            ns_b[...] = (NS_B * ns_b[...].astype(F32) + NS_C * square).astype(BF16)
            for r in range(6):
                at = slice(r * 256, (r + 1) * 256)
                ns_x[at, :] = (
                    NS_A * ns_x[at, :].astype(F32) + dot(ns_x[at, :], ns_b[...])
                ).astype(BF16)

        @pl.when(turn == 0)
        def _():
            for copy in own_loads:
                copy.wait()
            for p in (4, 5, 6, 0, 1, 2, 3):
                send_second(p)

        @pl.when(turn == 1)
        def _():
            norm_and_first()

        @pl.when(turn == 2)
        def _():
            send_second(7)
            spread(msum_ref, ghome_h, gh_s, gh_r, send_block)

        @pl.when(turn == 3)
        def _():
            finish((4, 5, 6))

        return carry

    lax.fori_loop(0, 5, step, 0)

    spread(ns_x, ohome_h, oh_s, oh_r, send_block)

    finish((0, 1, 2, 3, 7))

    def arrived(s, carry):
        @pl.when(s != dp)
        def _():
            remote(r3.at[s], r3.at[s], c_s.at[s], c_r.at[s], dp=s).wait_recv()

        return carry

    lax.fori_loop(0, 8, arrived, 0)
    total = r3[0].astype(F32)
    for index in range(1, 8):
        total = total + r3[index].astype(F32)
    fin_ref[dp] = total.astype(BF16)

    def give(j, carry):
        to = lax.rem(dp + j, 8)
        remote(fin_ref.at[dp], fin_ref.at[dp], d_s.at[to], d_r.at[dp], dp=to).start()
        return carry

    lax.fori_loop(1, 8, give, 0)

    _, code = codes_by_token(choice_ref[...])
    loads[1].wait()
    loads[2].wait()
    away = remote(moe_send, moe_ref, l_s, l_r, tensor=1 - ten)

    @pl.when(main)
    def _():
        fill_token_onehot(code, ptm, ptl)
        for m in range(4):
            at = slice(m * HALF, (m + 1) * HALF)
            total = dot(ptm[...], omain[:, at]) + dot(left_quarter(ptl, m), oleft[...])
            to = slice((m % 2) * HALF, (m % 2 + 1) * HALF)

            @pl.when(ten == m // 2)
            def _(total=total, to=to):
                moe_ref[:, to] = total.astype(BF16)

            @pl.when(ten != m // 2)
            def _(total=total, to=to):
                moe_send[:, to] = total.astype(BF16)

        away.start()

    spread(msum_ref, ghome_h, gh_s, gh_r, wait_block_sent)
    for i in range(4):
        for k in range(3):
            wait_block_received(ghome_h.at[i, k], gh_s.at[0, 0], gh_r.at[i, k])
    swap.wait_send()
    for p in range(8):
        for to_z in range(4):
            first(p, to_z).wait_send()
        for d in (1, 2, 3):
            second(p, d).wait_send()

    def others(j, carry):
        to = lax.rem(dp + j, 8)
        remote(s2.at[to], r3.at[dp], c_s.at[to], c_r.at[dp], dp=to).wait_send()
        remote(fin_ref.at[dp], fin_ref.at[dp], d_s.at[to], d_r.at[dp], dp=to).wait_send()
        remote(fin_ref.at[to], fin_ref.at[to], d_s.at[to], d_r.at[to], dp=to).wait_recv()
        return carry

    lax.fori_loop(1, 8, others, 0)

    @pl.when(main)
    def _():
        away.wait_send()

    @pl.when(jnp.logical_not(main))
    def _():
        away.wait_recv()

    spread(ns_x, ohome_h, oh_s, oh_r, wait_block_sent)
    for i in range(4):
        for k in range(3):
            wait_block_received(ohome_h.at[i, k], oh_s.at[0, 0], oh_r.at[i, k])


def run_update(choice_rows, hid, gain, bwd):
    dw, gres, gna, msum, omain, oleft = bwd
    vmem = pl.BlockSpec(memory_space=pltpu.VMEM)
    hbm = pl.BlockSpec(memory_space=pl.ANY)
    S = jax.ShapeDtypeStruct
    V = pltpu.VMEM
    return pl.pallas_call(
        update_kernel,
        out_shape=[
            S((8, ROWS, 256), BF16),
            S((TOK, D), F32),
            S((TOK, FF), BF16),
            S((4, 3, ROWS, HALF), BF16),
            S((4, 3, ROWS, HALF), BF16),
        ],
        in_specs=[vmem] * 2 + [hbm] * 6,
        out_specs=[vmem, vmem, vmem, hbm, hbm],
        scratch_shapes=[
            V((TOK, D), F32),
            V((TOK, D), BF16),
            V((D, FF), BF16),
            V((8, 4, ROWS, 256), BF16),
            V((8, 4, ROWS, 256), BF16),
            V((8, 3, ROWS, 256), BF16),
            V((8, ROWS, 256), BF16),
            V((8, ROWS, 256), BF16),
            V((D, 256), BF16),
            V((1024, D), BF16),
            V((512, HALF), BF16),
            V((TOK, 1024), BF16),
            V((TOK, 512), BF16),
            V((TOK, FF), BF16),
            V((TOK, D), BF16),
            V((D, FF), BF16),
            V((FF, FF), BF16),
            sems(34),
            sems(8, 4),
            sems(8, 4),
            sems(8, 3),
            sems(8, 3),
            sems(8),
            sems(8),
            sems(8),
            sems(8),
            pltpu.SemaphoreType.DMA,
            pltpu.SemaphoreType.DMA,
            pltpu.SemaphoreType.DMA,
            pltpu.SemaphoreType.DMA,
            sems(8, 2),
            sems(4, 3),
            sems(8, 2),
            sems(4, 3),
        ],
        compiler_params=pltpu.CompilerParams(
            collective_id=2, has_side_effects=True, vmem_limit_bytes=60 * MiB
        ),
        name="update",
    )(choice_rows, gain, hid, gna, msum, dw, omain, oleft)


def adam_update(weight, first, second, grad, rate, decay):
    first_new = 0.9 * first + 0.1 * grad
    second_new = 0.95 * second + 0.05 * grad * grad
    corrected = first_new / (1.0 - 0.9**10)
    denominator = jnp.sqrt(second_new / (1.0 - 0.95**10)) + 1e-08
    return (first_new, second_new, weight * (1.0 - rate * decay) - rate * corrected / denominator)


def shards(
    hidden_in,
    out_grad,
    expert_choice,
    segments,
    expert_weights,
    expert_moment,
    attention_weights,
    attention_first,
    attention_second,
    router_weights,
    router_first,
    router_second,
    norm_gains,
    gains_first,
    gains_second,
):
    tensor = lax.axis_index("tensor")
    choice_rows = expert_choice.T
    fwd = run_forward(
        hidden_in,
        out_grad,
        choice_rows,
        segments,
        attention_weights,
        router_weights,
        norm_gains,
        expert_weights,
    )
    resid, gain = fwd[5], fwd[9]
    mlow = (0.95 * expert_moment).astype(BF16)
    bwd = run_backward(choice_rows, segments, fwd, out_grad, mlow)
    gres = bwd[1]
    fin, term, moe, ghome, ohome = run_update(choice_rows, hidden_in, gain, bwd)

    layer_output = lax.dynamic_slice_in_dim(resid, tensor * FF, FF, 1) + moe.astype(F32)
    input_grad = gres + term
    moment_new = ghome.astype(F32)
    rates = jnp.array(MUON_RATES, F32)[None, :, None, None]
    expert_new = expert_weights * (1.0 - rates * 0.1) - rates * (0.2 * D**0.5) * ohome.astype(F32)
    slot_rates = jnp.where(jnp.arange(14) >= 8, 0.5, 0.05)[None, :, None, None]
    grads = fin.astype(F32)
    attention_grad = grads[0:7].reshape(7, ROWS, 2, 128).transpose(0, 2, 1, 3)
    attention_out = adam_update(
        attention_weights,
        attention_first,
        attention_second,
        attention_grad.reshape(1, 14, ROWS, 128),
        slot_rates,
        0.1,
    )
    router_out = adam_update(
        router_weights, router_first, router_second, grads[7, :, 0:32], 0.025, 0.1
    )
    gains_grad = jnp.stack([grads[7, :, 33], grads[7, :, 32]])
    gains_out = adam_update(norm_gains, gains_first, gains_second, gains_grad, 1.0, 0.0)
    return (
        layer_output,
        input_grad,
        moment_new,
        expert_new,
        *attention_out,
        *router_out,
        *gains_out,
    )


def solution(mesh):
    tokens = P(("dp", "ctx"), None)
    expert = P("dp", None, "ctx", "tensor")
    attention = P("tensor", None, "ctx", None)
    router = P("ctx", None)
    gains = P(None, "ctx")
    return jax.shard_map(
        shards,
        mesh=mesh,
        in_specs=(
            (tokens,) * 3
            + (P("dp", None),)
            + (expert,) * 2
            + (attention,) * 3
            + (router,) * 3
            + (gains,) * 3
        ),
        out_specs=(
            (P(("dp", "ctx"), "tensor"), tokens)
            + (expert,) * 2
            + (attention,) * 3
            + (router,) * 3
            + (gains,) * 3
        ),
        check_vma=False,
    )
```

```python
import functools

import jax
import jax.numpy as jnp
from jax import lax
from jax.experimental import pallas as pl
from jax.experimental.pallas import tpu as pltpu
from jax.sharding import PartitionSpec as P

MESH = pl.DeviceIdType.MESH
F32 = jnp.float32
BF16 = jnp.bfloat16
EPS = 1e-06
TOK = 256
D = 1536
FF = 768
ROWS = 192
HALF = 384
SCALE = 128.0 ** (-0.5)
MiB = 2**20


def dot(a, b):
    return jnp.dot(a, b, preferred_element_type=F32)


def dot_nt(a, b):
    return lax.dot_general(a, b, (((1,), (1,)), ((), ())), preferred_element_type=F32)


def dot_tn(a, b):
    return lax.dot_general(a, b, (((0,), (0,)), ((), ())), preferred_element_type=F32)


def iota(shape, axis):
    return lax.broadcasted_iota(jnp.int32, shape, axis)


def remote(src, dst, send_sem, recv_sem, **device):
    return pltpu.make_async_remote_copy(
        src_ref=src,
        dst_ref=dst,
        send_sem=send_sem,
        recv_sem=recv_sem,
        device_id=device,
        device_id_type=MESH,
    )


def local(src, dst, sem):
    return pltpu.make_async_copy(src, dst, sem)


def place():
    ctx = lax.axis_index("ctx")
    return lax.axis_index("dp"), ctx, lax.axis_index("tensor"), lax.div(ctx, 2), lax.rem(ctx, 2)


def row_to_column(row):
    n = row.shape[1]
    same = iota((n, n), 0) == iota((n, n), 1)
    return jnp.sum(jnp.where(same, row, jnp.zeros_like(row)), axis=1, keepdims=True)


def codes_by_expert(choice_rows):
    expert = iota((32, TOK), 0)
    hit = jnp.zeros((32, TOK), F32)
    for k in range(4):
        hit = hit + jnp.where(choice_rows[k : k + 1, :] == expert, 1.0, 0.0)
    before = jnp.where(iota((TOK, TOK), 0) < iota((TOK, TOK), 1), 1.0, 0.0).astype(BF16)
    slot = dot(hit.astype(BF16), before)
    return jnp.where(hit > 0.5, slot, -1.0)


def codes_by_token(choice_rows):
    expert = iota((TOK, 128), 1)
    hit = jnp.zeros((TOK, 128), F32)
    for k in range(4):
        hit = hit + jnp.where(row_to_column(choice_rows[k : k + 1, :]) == expert, 1.0, 0.0)
    before = jnp.where(iota((TOK, TOK), 0) > iota((TOK, TOK), 1), 1.0, 0.0).astype(BF16)
    slot = dot(before, hit.astype(BF16))
    return hit, jnp.where(hit > 0.5, slot, -1.0)


def fill_onehot(code_ref, main_ref, left_ref):
    def one(e, carry):
        code = code_ref[pl.ds(e, 1), :]
        main_ref[pl.ds(pl.multiple_of(e * 32, 32), 32), :] = jnp.where(
            iota((32, TOK), 0).astype(F32) == code, 1.0, 0.0
        ).astype(BF16)
        left_ref[pl.ds(pl.multiple_of(e * 16, 16), 16), :] = jnp.where(
            (32 + lax.rem(iota((16, TOK), 0), 4)).astype(F32) == code, 1.0, 0.0
        ).astype(BF16)
        return carry

    lax.fori_loop(0, 32, one, 0)


def pack_rows(onehot_main, onehot_left, rows_ref, out_main, out_left):
    width = rows_ref.shape[1]

    def main_block(b, carry):
        at = pl.ds(pl.multiple_of(b * 256, 256), 256)
        out_main[at, :] = dot(onehot_main[at, :], rows_ref[...]).astype(BF16)
        return carry

    lax.fori_loop(0, 4, main_block, 0)

    def left_block(b, carry):
        at = pl.ds(pl.multiple_of(b * 256, 256), 256)
        quarter = lax.rem(lax.div(iota((256, HALF), 0), 4), 4)
        total = jnp.zeros((256, HALF), F32)
        for q in range(4):
            piece = dot(onehot_left[at, :], rows_ref[:, q * HALF : (q + 1) * HALF])
            total = total + jnp.where(quarter == q, piece, 0.0)
        out_left[at, 0:HALF] = total.astype(BF16)
        if width > D:
            out_left[at, HALF:] = dot(onehot_left[at, :], rows_ref[:, D:]).astype(BF16)
        return carry

    lax.fori_loop(0, 2, left_block, 0)


def plane_for(dp, to_dp, ten):
    return jnp.where(lax.div(dp, 4) == lax.div(to_dp, 4), ten, 1 - ten)


def send_rows(src_main, src_left, dst_main, dst_left, send_sem, recv_sem):
    dp, ctx, ten, z, c = place()
    core = lax.rem(z, 2)
    source = dp * 2 + lax.div(z, 2)

    def one(turn, carry):
        to_dp, to_z = lax.rem(dp + lax.div(turn, 4), 8), lax.rem(z + turn, 4)
        e = to_dp * 4 + to_z
        here = (to_dp == dp) & (to_z == z) & (c == core)
        for i, (src, dst, n) in enumerate(((src_main, dst_main, 32), (src_left, dst_left, 16))):
            src_at = src.at[pl.ds(pl.multiple_of(e * n, n), n)]
            dst_at = dst.at[pl.ds(pl.multiple_of(source * n, n), n)]

            @pl.when(here)
            def _(i=i, src_at=src_at, dst_at=dst_at):
                local(src_at, dst_at, recv_sem.at[i, source]).start()

            @pl.when(jnp.logical_not(here))
            def _(i=i, src_at=src_at, dst_at=dst_at):
                remote(
                    src_at,
                    dst_at,
                    send_sem.at[i, e],
                    recv_sem.at[i, source],
                    dp=to_dp,
                    ctx=to_z * 2 + core,
                    tensor=plane_for(dp, to_dp, ten),
                ).start()

        return carry

    lax.fori_loop(0, 32, one, 0)


def wait_sent_rows(src_main, src_left, dst_main, dst_left, send_sem, recv_sem):
    dp, ctx, ten, z, c = place()

    def one(e, carry):
        here = (lax.div(e, 4) == dp) & (lax.rem(e, 4) == z) & (c == lax.rem(z, 2))

        @pl.when(jnp.logical_not(here))
        def _():
            for i, (src, dst, n) in enumerate(((src_main, dst_main, 32), (src_left, dst_left, 16))):
                remote(
                    src.at[pl.ds(pl.multiple_of(e * n, n), n)],
                    dst.at[pl.ds(0, n)],
                    send_sem.at[i, e],
                    recv_sem.at[i, 0],
                    dp=dp,
                    ctx=ctx,
                    tensor=1 - ten,
                ).wait_send()

        return carry

    lax.fori_loop(0, 32, one, 0)


def wait_received_rows(src_main, src_left, dst_main, dst_left, send_sem, recv_sem):
    dp, ctx, ten, z, c = place()

    def one(s, carry):
        for i, (src, dst, n) in enumerate(((src_main, dst_main, 32), (src_left, dst_left, 16))):
            remote(
                src.at[pl.ds(0, n)],
                dst.at[pl.ds(pl.multiple_of(s * n, n), n)],
                send_sem.at[i, 0],
                recv_sem.at[i, s],
                dp=dp,
                ctx=ctx,
                tensor=1 - ten,
            ).wait_recv()
        return carry

    lax.fori_loop(0, 16, one, 0)


def greet_row_senders(barrier):
    dp, ctx, ten, z, c = place()
    main = c == ten

    def one(s, carry):
        from_dp, from_z = lax.div(s, 2), lax.rem(s, 2) * 2 + c
        plane = plane_for(dp, from_dp, ten)
        here = main & (from_dp == dp) & (from_z == z)

        @pl.when(jnp.logical_not(here))
        def _():
            pl.semaphore_signal(
                barrier,
                inc=1,
                device_id={"dp": from_dp, "ctx": from_z * 2 + plane, "tensor": plane},
                device_id_type=MESH,
            )

        return carry

    lax.fori_loop(0, 16, one, 0)
    self_in = (c == lax.rem(z, 2)).astype(jnp.int32)
    return jnp.where(main, 32 - self_in, 0)


def forward_kernel(
    choice_ref,
    seg_ref,
    rw_ref,
    gains_ref,
    hid_h,
    og_h,
    aw_h,
    ew_h,
    lse_ref,
    gate_ref,
    gain_ref,
    router_ref,
    q_h,
    kv_h,
    heads_h,
    w_h,
    resid_h,
    nba_h,
    nbb_h,
    wexp_ref,
    xmain_ref,
    xleft_ref,
    ogmain_ref,
    ogleft_ref,
    hid_ref,
    og_ref,
    aw_ref,
    ew_ref,
    elow_ref,
    q_ref,
    kv_ref,
    heads_ref,
    w_ref,
    resid_ref,
    nba_ref,
    nbb_ref,
    ld,
    st,
    ws,
    rs,
    gs,
    grecv,
    bias,
    code_ref,
    onehot_main,
    onehot_left,
    nbx,
    ogl,
    send_main,
    send_left,
    send_ogmain,
    send_ogleft,
    part,
    prec,
    za_s,
    za_r,
    xa_s,
    xa_r,
    ca_s,
    ca_r,
    sm_s,
    sm_r,
    kv_s,
    kv_r,
    kvf_s,
    kvf_r,
    pe_s,
    pe_r,
    og_s,
    og_r,
    x_s,
    x_r,
    wz_s,
    wz_r,
    wy_s,
    wy_r,
    wc_s,
    wc_r,
):
    dp, ctx, ten, z, c = place()
    main = c == ten
    core_peer = z * 2 + 1 - c

    def z_peer(d):
        return lax.rem(z + d, 4) * 2 + c

    loads = [
        pltpu.make_async_copy(src, dst, ld.at[i])
        for i, (src, dst) in enumerate(
            ((aw_h, aw_ref), (hid_h, hid_ref), (og_h, og_ref), (ew_h, ew_ref))
        )
    ]
    for copy in loads:
        copy.start()
    stores = []

    def store(src, dst):
        copy = pltpu.make_async_copy(src, dst, st.at[len(stores)])
        copy.start()
        stores.append(copy)

    barrier = pltpu.get_barrier_semaphore()
    for j in range(1, 8):
        pl.semaphore_signal(
            barrier, inc=1, device_id={"ctx": lax.rem(ctx + j, 8)}, device_id_type=MESH
        )
    pl.semaphore_signal(barrier, inc=1, device_id={"tensor": 1 - ten}, device_id_type=MESH)
    for j in range(1, 4):
        pl.semaphore_signal(
            barrier,
            inc=1,
            device_id={"dp": dp - lax.rem(dp, 4) + lax.rem(dp + j, 4)},
            device_id_type=MESH,
        )
    extra = greet_row_senders(barrier)

    loads[0].wait()
    for p in range(7):
        ws[p, :, 0:128] = aw_ref[0, 2 * p].astype(BF16)
        ws[p, :, 128:256] = aw_ref[0, 2 * p + 1].astype(BF16)
    spots = jnp.where(iota((32, 128), 0) == iota((32, 128), 1), 1.0, 0.0).astype(BF16)
    rs[...] = dot_tn(rw_ref[...].astype(BF16), spots).astype(BF16)
    shift = jnp.where(iota((ROWS, D), 1) == iota((ROWS, D), 0) + ctx * ROWS, 1.0, 0.0).astype(BF16)
    gs[...] = jnp.zeros_like(gs)
    gs[0:2, :] = dot(gains_ref[...].astype(BF16), shift)

    pl.semaphore_wait(barrier, 11 + extra)

    def rows_at(index):
        return pl.ds(pl.multiple_of(index * ROWS, 64), ROWS)

    small = []
    for j in range(1, 8):
        to = lax.rem(ctx + j, 8)
        for i, (src, dst) in enumerate(
            ((gs, grecv.at[j - 1]), (rs, router_ref.at[rows_at(ctx)]))
        ):
            copy = remote(src, dst, sm_s.at[i, j - 1], sm_r.at[i, j - 1], ctx=to)
            copy.start()
            small.append(copy)
    router_ref[rows_at(ctx), :] = rs[...]

    groups = ((3, 1), (0, 3), (4, 3))
    xx = lax.rem(dp, 4)
    weight_copies = {}

    def x_peer(j):
        return dp - xx + lax.rem(xx + j, 4)

    def quarter(index):
        return pl.ds(pl.multiple_of(index * ROWS + xx * 48, 16), 48)

    def start_group(g):
        first, count = groups[g]
        pairs = pl.ds(first, count)
        for d in (1, 3, 2):
            copy = remote(
                ws.at[pairs, quarter(0)],
                w_ref.at[pairs, quarter(ctx)],
                za_s.at[g, d - 1],
                za_r.at[g, d - 1],
                ctx=z_peer(d),
            )
            copy.start()
            weight_copies[g, "z", d] = copy
        copy = remote(
            ws.at[pairs], w_ref.at[pairs, rows_at(ctx)], ca_s.at[g, 0], ca_r.at[g, 0], ctx=core_peer
        )
        copy.start()
        weight_copies[g, "c", 0] = copy
        w_ref[first : first + count, rows_at(ctx), :] = ws[first : first + count]

    def spread_group(g):
        pairs = pl.ds(*groups[g])
        for d in (1, 3, 2):
            weight_copies[g, "z", d].wait_recv()
            block = w_ref.at[pairs, quarter(lax.rem(z + 4 - d, 4) * 2 + c)]
            for j in (1, 3, 2):
                copy = remote(
                    block, block, xa_s.at[g, d - 1, j - 1], xa_r.at[g, d - 1, j - 1], dp=x_peer(j)
                )
                copy.start()
                weight_copies[g, "x", d, j] = copy

    def join_group(g):
        first, count = groups[g]
        pairs = pl.ds(first, count)
        for d in (1, 3, 2):
            for j in (1, 3, 2):
                weight_copies[g, "x", d, j].wait_recv()
            share = w_ref.at[pairs, rows_at(lax.rem(z + 4 - d, 4) * 2 + c)]
            copy = remote(share, share, ca_s.at[g, d], ca_r.at[g, d], ctx=core_peer)
            copy.start()
            weight_copies[g, "c", d] = copy
        for d in (0, 1, 3, 2):
            weight_copies[g, "c", d].wait_recv()
        store(w_ref.at[pairs], w_h.at[pairs])

    for g in range(3):
        start_group(g)

    seg_here = seg_ref[:, pl.ds(pl.multiple_of(ctx * TOK, TOK), TOK)]
    seg_col = row_to_column(seg_here)
    for b in range(8):
        at = slice(b * 256, (b + 1) * 256)
        key_pos = b * 256 + iota((TOK, 256), 1)
        query_pos = ctx * TOK + iota((TOK, 256), 0)
        allowed = (key_pos <= query_pos) & (seg_ref[:, at] == seg_col)
        bias[:, at] = jnp.where(allowed, 0.0, -1e30)
    spread_group(0)
    spread_group(1)

    for copy in small:
        copy.wait_recv()
    gain_ref[...] = gs[...]
    for j in range(7):
        gain_ref[...] += grecv[j]
    loads[1].wait()
    hid = hid_ref[...]
    inverse = lax.rsqrt(jnp.mean(hid * hid, axis=1, keepdims=True) + EPS)
    nba_ref[...] = (hid * inverse * gain_ref[0:1, :]).astype(BF16)
    store(nba_ref, nba_h)

    loads[3].wait()
    cols = pl.ds(pl.multiple_of(ten * HALF, 128), HALF)
    spread = {}

    def lower(i, carry):
        elow_ref[i] = ew_ref[i].astype(BF16)
        return carry

    lax.fori_loop(0, 4, lower, 0)

    def send_kind(k):
        for d in range(4):
            to_z = lax.rem(z + d, 4)
            src, dst = elow_ref.at[to_z, k], wexp_ref.at[k, z, c, :, cols]
            if d == 0:
                copy = pltpu.make_async_copy(src, dst, wz_r.at[k, 0])
            else:
                copy = remote(src, dst, wz_s.at[k, d], wz_r.at[k, d], ctx=z_peer(d))
            copy.start()
            spread[k, d] = copy

    def pass_kind(k):
        for d in range(4):
            if d == 0:
                spread[k, d].wait()
            else:
                spread[k, d].wait_recv()
        own = wexp_ref.at[k, :, c, :, cols]
        spread[k, "y"] = remote(own, own, wy_s.at[k], wy_r.at[k], tensor=1 - ten)
        spread[k, "c"] = remote(own, own, wc_s.at[k, 0], wc_r.at[k, 0], ctx=core_peer)
        spread[k, "y"].start()
        spread[k, "c"].start()

    send_kind(0)

    forwards = {}

    def kv_rows(index):
        return kv_ref.at[pl.ds(pl.multiple_of(index * TOK, TOK), TOK)]

    join_group(0)
    kv_ref[pl.ds(pl.multiple_of(ctx * TOK, TOK), TOK), :] = dot(nba_ref[...], w_ref[3]).astype(BF16)
    kv_copies = {}
    for d in (1, 3, 2, 0):
        to = core_peer if d == 0 else z_peer(d)
        copy = remote(kv_rows(ctx), kv_rows(ctx), kv_s.at[d], kv_r.at[d], ctx=to)
        copy.start()
        kv_copies[d] = copy
    spread_group(2)
    pass_kind(0)

    choice = choice_ref[...]
    hit, _ = codes_by_token(choice)
    loads[2].wait()

    @pl.when(main)
    def _():
        code_ref[...] = codes_by_expert(choice)
        fill_onehot(code_ref, onehot_main, onehot_left)
        ogl[...] = og_ref[...].astype(BF16)
        pack_rows(onehot_main, onehot_left, ogl, send_ogmain, send_ogleft)

    join_group(1)
    for p in range(3):
        q_ref[p] = dot(nba_ref[...], w_ref[p]).astype(BF16)
    store(q_ref, q_h)

    for d in (1, 3, 2):
        kv_copies[d].wait_recv()
        rows = kv_rows(lax.rem(z + 4 - d, 4) * 2 + c)
        fcopy = remote(rows, rows, kvf_s.at[d - 1], kvf_r.at[d - 1], ctx=core_peer)
        fcopy.start()
        forwards["kv", d] = fcopy
    kv_copies[0].wait_recv()
    for d in (1, 3, 2):
        forwards["kv", d].wait_recv()
    store(kv_ref, kv_h)

    og_args = (send_ogmain, send_ogleft, ogmain_ref, ogleft_ref, og_s, og_r)
    x_args = (send_main, send_left, xmain_ref, xleft_ref, x_s, x_r)

    @pl.when(main)
    def _():
        send_rows(*og_args)

    send_kind(1)
    send_kind(2)

    lse_ref[...] = jnp.zeros_like(lse_ref)
    outgoing = []
    for half in range(2):
        at = slice(half * 128, (half + 1) * 128)
        for j in range(6):
            lanes = slice((j % 2) * 128, (j % 2) * 128 + 128)
            scores = dot_nt(q_ref[j // 2, at, lanes], kv_ref[:, 0:128]) * SCALE + bias[at, :]
            top = jnp.max(scores, axis=1, keepdims=True)
            terms = jnp.exp(scores - top)
            total = jnp.sum(terms, axis=1, keepdims=True)
            mixed = dot(terms.astype(BF16), kv_ref[:, 128:256]) / total
            heads_ref[j // 2, at, lanes] = mixed.astype(BF16)
            lse_ref[at, :] = jnp.where(
                iota((128, 128), 1) == j, top + jnp.log(total), lse_ref[at, :]
            )
        if half == 0:
            join_group(2)
        total = dot_nt(heads_ref[0, at, :], w_ref[4])
        total = total + dot_nt(heads_ref[1, at, :], w_ref[5])
        total = total + dot_nt(heads_ref[2, at, :], w_ref[6])
        part[at, :] = total.astype(BF16)
        copy = remote(part.at[at], prec.at[at], pe_s.at[half], pe_r.at[half], tensor=1 - ten)
        outgoing.append(copy)

        @pl.when(jnp.logical_not(main))
        def _(copy=copy):
            copy.start()

    for copy in outgoing:

        @pl.when(main)
        def _(copy=copy):
            copy.wait_recv()
            copy.start()

        @pl.when(jnp.logical_not(main))
        def _(copy=copy):
            copy.wait_recv()

    pass_kind(1)
    pass_kind(2)
    resid = hid_ref[...] + (part[...].astype(F32) + prec[...].astype(F32))
    resid_ref[...] = resid
    store(resid_ref, resid_h)
    store(heads_ref, heads_h)
    inverse = lax.rsqrt(jnp.mean(resid * resid, axis=1, keepdims=True) + EPS)
    nbb = (resid * inverse * gain_ref[1:2, :]).astype(BF16)
    nbb_ref[...] = nbb
    store(nbb_ref, nbb_h)
    logits = jnp.where(hit > 0.5, dot(nbb, router_ref[...]), -1e30)
    top = jnp.max(logits, axis=1, keepdims=True)
    terms = jnp.where(hit > 0.5, jnp.exp(logits - top), 0.0)
    gates = terms / jnp.sum(terms, axis=1, keepdims=True)
    gate_ref[...] = gates

    @pl.when(main)
    def _():
        nbx[:, 0:D] = nbb
        high = gates.astype(BF16).astype(F32)
        nbx[:, D:] = (high + pltpu.roll(gates - high, 32, 1)).astype(BF16)
        pack_rows(onehot_main, onehot_left, nbx, send_main, send_left)
        send_rows(*x_args)

    for k in range(3):
        spread[k, "y"].wait_recv()
        there = wexp_ref.at[k, :, c, :, pl.ds(pl.multiple_of((1 - ten) * HALF, 128), HALF)]
        spread[k, "cy"] = remote(there, there, wc_s.at[k, 1], wc_r.at[k, 1], ctx=core_peer)
        spread[k, "cy"].start()
    for k in range(3):
        spread[k, "c"].wait_recv()
        spread[k, "cy"].wait_recv()
        for d in (1, 2, 3):
            spread[k, d].wait_send()
        for name in ("y", "c", "cy"):
            spread[k, name].wait_send()
    wait_received_rows(*og_args)
    wait_received_rows(*x_args)

    @pl.when(main)
    def _():
        wait_sent_rows(*og_args)
        wait_sent_rows(*x_args)

    for copy in small + list(weight_copies.values()) + list(forwards.values()) + list(kv_copies.values()):
        copy.wait_send()
    for copy in outgoing:
        copy.wait_send()
    for copy in stores:
        copy.wait()


def sems(*shape):
    return pltpu.SemaphoreType.DMA(shape)


def run_forward(hid, og, choice_rows, seg, aw, rw, gains, ew):
    vmem = pl.BlockSpec(memory_space=pltpu.VMEM)
    hbm = pl.BlockSpec(memory_space=pl.ANY)
    S = jax.ShapeDtypeStruct
    V = pltpu.VMEM
    kept = [
        ((3, TOK, 256), BF16),
        ((2048, 256), BF16),
        ((3, TOK, 256), BF16),
        ((7, D, 256), BF16),
        ((TOK, D), F32),
        ((TOK, D), BF16),
        ((TOK, D), BF16),
    ]
    outs = [
        S((TOK, 128), F32),
        S((TOK, 128), F32),
        S((8, D), F32),
        S((D, 128), BF16),
        *(S(*shape) for shape in kept),
        S((3, 4, 2, ROWS, FF), BF16),
        S((512, D + 128), BF16),
        S((256, HALF + 128), BF16),
        S((512, D), BF16),
        S((256, HALF), BF16),
    ]
    lse, gate, gain, router, *rest = pl.pallas_call(
        forward_kernel,
        out_shape=outs,
        in_specs=[vmem] * 4 + [hbm] * 4,
        out_specs=[vmem] * 4 + [hbm] * 12,
        scratch_shapes=[
            V((TOK, D), F32),
            V((TOK, D), F32),
            V((1, 14, ROWS, 128), F32),
            V((4, 3, ROWS, HALF), F32),
            V((4, 3, ROWS, HALF), BF16),
            *(V(*shape) for shape in kept),
            sems(4),
            sems(16),
            V((7, ROWS, 256), BF16),
            V((ROWS, 128), BF16),
            V((8, D), F32),
            V((7, 8, D), F32),
            V((TOK, 2048), F32),
            V((32, TOK), F32),
            V((1024, TOK), BF16),
            V((512, TOK), BF16),
            V((TOK, D + 128), BF16),
            V((TOK, D), BF16),
            V((1024, D + 128), BF16),
            V((512, HALF + 128), BF16),
            V((1024, D), BF16),
            V((512, HALF), BF16),
            V((TOK, D), BF16),
            V((TOK, D), BF16),
            sems(3, 3),
            sems(3, 3),
            sems(3, 3, 3),
            sems(3, 3, 3),
            sems(3, 4),
            sems(3, 4),
            sems(2, 7),
            sems(2, 7),
            sems(4),
            sems(4),
            sems(3),
            sems(3),
            sems(2),
            sems(2),
            sems(2, 32),
            sems(2, 16),
            sems(2, 32),
            sems(2, 16),
            sems(3, 4),
            sems(3, 4),
            sems(3),
            sems(3),
            sems(3, 2),
            sems(3, 2),
        ],
        compiler_params=pltpu.CompilerParams(
            collective_id=0, has_side_effects=True, vmem_limit_bytes=56 * MiB
        ),
        name="attention_forward",
    )(choice_rows, seg, rw.T, gains, hid, og, aw, ew)
    q, kv, heads, w, resid, nba, nbb, *sent = rest
    return (q, kv, heads, lse, w, resid, nba, nbb, gate, gain, router, *sent)


GATE, UP, DOWN = 0, 1, 2
OWNER_CORE = (0, 1, 1)
CORE_SLOT = (0, 0, 1)
GELU_A = 0.7978845608028654
GELU_B = 0.044715


def owner_plane(k):
    _, _, _, z, _ = place()
    return lax.rem(z, 2) if k != UP else 1 - lax.rem(z, 2)


def is_owner(c, ten):
    return jnp.logical_not((c == 0) & (ten != owner_plane(GATE)))


def half_columns(index):
    return pl.ds(pl.multiple_of(index * HALF, 128), HALF)


def greet_group(barrier):
    _, ctx, ten, _, _ = place()
    for j in range(8):
        for t in range(2):
            if j or t:
                pl.semaphore_signal(
                    barrier,
                    inc=1,
                    device_id={"ctx": lax.rem(ctx + j, 8), "tensor": lax.rem(ten + t, 2)},
                    device_id_type=MESH,
                )


def send_block(src, dst, send_sem, recv_sem, to_ctx, to_ten):
    _, ctx, ten, _, _ = place()
    here = (ctx == to_ctx) & (ten == to_ten)

    @pl.when(here)
    def _():
        local(src, dst, recv_sem).start()

    @pl.when(jnp.logical_not(here))
    def _():
        remote(src, dst, send_sem, recv_sem, ctx=to_ctx, tensor=to_ten).start()


def wait_block_sent(src, dst, send_sem, recv_sem, to_ctx, to_ten):
    _, ctx, ten, _, _ = place()
    here = (ctx == to_ctx) & (ten == to_ten)

    @pl.when(jnp.logical_not(here))
    def _():
        remote(src, dst, send_sem, recv_sem, ctx=to_ctx, tensor=to_ten).wait_send()


def wait_block_received(block, send_sem, recv_sem):
    _, ctx, ten, _, _ = place()
    remote(block, block, send_sem, recv_sem, ctx=ctx, tensor=1 - ten).wait_recv()


def return_rows(src_main, src_left, dst_main, dst_left, send_sem, recv_sem):
    dp, ctx, ten, z, c = place()
    expert = dp * 4 + z

    def one(turn, carry):
        to_dp, half = lax.rem(dp + lax.div(turn, 2), 8), lax.rem(lax.div(z, 2) + turn, 2)
        s, to_z = to_dp * 2 + half, half * 2 + c
        plane = plane_for(dp, to_dp, ten)
        here = (to_dp == dp) & (to_z == z) & (c == ten)
        for i, (src, dst, n) in enumerate(((src_main, dst_main, 32), (src_left, dst_left, 16))):
            src_at = src.at[pl.ds(pl.multiple_of(s * n, n), n)]
            dst_at = dst.at[pl.ds(pl.multiple_of(expert * n, n), n)]

            @pl.when(here)
            def _(i=i, src_at=src_at, dst_at=dst_at):
                local(src_at, dst_at, recv_sem.at[i, expert]).start()

            @pl.when(jnp.logical_not(here))
            def _(i=i, src_at=src_at, dst_at=dst_at):
                remote(
                    src_at,
                    dst_at,
                    send_sem.at[i, s],
                    recv_sem.at[i, expert],
                    dp=to_dp,
                    ctx=to_z * 2 + plane,
                    tensor=plane,
                ).start()

        return carry

    lax.fori_loop(0, 16, one, 0)


def wait_returned(src_main, src_left, dst_main, dst_left, send_sem, recv_sem):
    dp, ctx, ten, z, c = place()

    def one(e, carry):
        for i, (src, dst, n) in enumerate(((src_main, dst_main, 32), (src_left, dst_left, 16))):
            remote(
                src.at[pl.ds(0, n)],
                dst.at[pl.ds(pl.multiple_of(e * n, n), n)],
                send_sem.at[i, 0],
                recv_sem.at[i, e],
                dp=dp,
                ctx=ctx,
                tensor=1 - ten,
            ).wait_recv()
        return carry

    lax.fori_loop(0, 32, one, 0)


def wait_return_sent(src_main, src_left, dst_main, dst_left, send_sem, recv_sem):
    dp, ctx, ten, z, c = place()

    def one(s, carry):
        here = (lax.div(s, 2) == dp) & (lax.rem(s, 2) * 2 + c == z) & (c == ten)

        @pl.when(jnp.logical_not(here))
        def _():
            for i, (src, dst, n) in enumerate(((src_main, dst_main, 32), (src_left, dst_left, 16))):
                remote(
                    src.at[pl.ds(pl.multiple_of(s * n, n), n)],
                    dst.at[pl.ds(0, n)],
                    send_sem.at[i, s],
                    recv_sem.at[i, 0],
                    dp=dp,
                    ctx=ctx,
                    tensor=1 - ten,
                ).wait_send()

        return carry

    lax.fori_loop(0, 16, one, 0)


def greet_expert_devices(barrier):
    dp, ctx, ten, z, c = place()
    core = lax.rem(z, 2)

    def one(e, carry):
        to_dp, to_z = lax.div(e, 4), lax.rem(e, 4)
        here = (to_dp == dp) & (to_z == z) & (c == core)

        @pl.when(jnp.logical_not(here))
        def _():
            pl.semaphore_signal(
                barrier,
                inc=1,
                device_id={
                    "dp": to_dp,
                    "ctx": to_z * 2 + core,
                    "tensor": plane_for(dp, to_dp, ten),
                },
                device_id_type=MESH,
            )

        return carry

    @pl.when(c == ten)
    def _():
        lax.fori_loop(0, 32, one, 0)

    return 16 - ((c == ten) & (core == c)).astype(jnp.int32)


def left_picker(quarter):
    row, col = iota((64, 256), 0), iota((64, 256), 1)
    return jnp.where(col == lax.div(row, 4) * 16 + quarter * 4 + lax.rem(row, 4), 1.0, 0.0).astype(
        BF16
    )


def left_packer(quarter):
    row, col = iota((256, 64), 0), iota((256, 64), 1)
    return jnp.where(row == lax.div(col, 4) * 16 + quarter * 4 + lax.rem(col, 4), 1.0, 0.0).astype(
        BF16
    )


def fill_token_onehot(code, main_ref, left_ref):
    code = code.astype(BF16)
    for b in range(4):
        expert, col = iota((128, 256), 0), iota((128, 256), 1) + b * 256
        spread = dot(code, jnp.where(lax.div(col, 32) == expert, 1.0, 0.0).astype(BF16))
        slot = lax.rem(iota((TOK, 256), 1), 32).astype(F32)
        main_ref[:, b * 256 : (b + 1) * 256] = jnp.where(spread == slot, 1.0, 0.0).astype(BF16)
    for b in range(2):
        expert, col = iota((128, 256), 0), iota((128, 256), 1) + b * 256
        spread = dot(code, jnp.where(lax.div(col, 16) == expert, 1.0, 0.0).astype(BF16))
        slot = (32 + lax.rem(iota((TOK, 256), 1), 4)).astype(F32)
        left_ref[:, b * 256 : (b + 1) * 256] = jnp.where(spread == slot, 1.0, 0.0).astype(BF16)


def left_quarter(left_ref, quarter):
    keep = lax.rem(lax.div(iota((TOK, 512), 1), 4), 4) == quarter
    return jnp.where(keep, left_ref[...].astype(F32), 0.0).astype(BF16)


def backward_kernel(
    choice_ref,
    seg_ref,
    gate_ref,
    lse_ref,
    gain_ref,
    router_ref,
    xmain_h,
    xleft_h,
    ogmain_h,
    ogleft_h,
    wexp_h,
    w_h,
    q_h,
    kv_h,
    heads_h,
    nba_h,
    nbb_h,
    resid_h,
    og_h,
    mlow_h,
    dw_h,
    sums_ref,
    gres_ref,
    gna_ref,
    msum_ref,
    omain_h,
    oleft_h,
    xall,
    gx,
    xleft,
    ogall,
    ogleft,
    w9,
    ggp,
    gup,
    hidden,
    ghid,
    gmain,
    gleft,
    oleft,
    dw9,
    rcore,
    cmain,
    cleft,
    ptm,
    ptl,
    ext,
    kv,
    q,
    heads,
    nba,
    nbb,
    resid,
    gheads,
    gatt,
    dslab,
    dq,
    dkv,
    rkv,
    skv,
    r2kv,
    stage,
    rhalf,
    rquarter,
    ld,
    lw,
    dw_s,
    ra_s,
    ra_r,
    rb_s,
    rb_r,
    g_s,
    g_r,
    o_s,
    o_r,
    mc_s,
    mc_r,
    my_s,
    my_r,
    e_s,
    e_r,
    k1_s,
    k1_r,
    k2_s,
    k2_r,
    mo_s,
    mo_r,
):
    dp, ctx, ten, z, c = place()
    main = c == ten
    core_peer = z * 2 + 1 - c
    expert = dp * 4 + z

    def z_peer(d):
        return lax.rem(z + d, 4) * 2 + c

    barrier = pltpu.get_barrier_semaphore()
    greet_group(barrier)
    extra = greet_expert_devices(barrier)

    loads = [
        pltpu.make_async_copy(xmain_h.at[:, 0:D], xall.at[0:512], ld.at[0]),
        pltpu.make_async_copy(xmain_h.at[:, D:], gx.at[0:512], ld.at[1]),
        pltpu.make_async_copy(xleft_h, xleft, ld.at[2]),
        pltpu.make_async_copy(ogmain_h, ogall.at[0:512], ld.at[3]),
        pltpu.make_async_copy(ogleft_h, ogleft, ld.at[4]),
    ]
    expert_loads = []
    for n in range(3):
        for k in range(3):
            expert_loads.append(
                pltpu.make_async_copy(
                    wexp_h.at[k, :, n * 256 : (n + 1) * 256], w9.at[3 * k + n], lw.at[3 * k + n]
                )
            )
    later = [
        pltpu.make_async_copy(src, dst, ld.at[5 + i])
        for i, (src, dst) in enumerate(
            (
                (kv_h, kv),
                (q_h, q),
                (heads_h, heads),
                (nba_h, nba),
                (nbb_h, nbb),
                (resid_h, resid),
                (og_h, gres_ref),
            )
        )
    ]
    for copy in loads + expert_loads + later:
        copy.start()

    @pl.when(main)
    def _():
        _, code = codes_by_token(choice_ref[...])
        fill_token_onehot(code, ptm, ptl)

    for copy in loads:
        copy.wait()
    for n in range(4):
        at = slice(n * HALF, (n + 1) * HALF)
        pick = left_picker(n)
        xall[512:576, at] = dot(pick, xleft[:, 0:HALF]).astype(BF16)
        ogall[512:576, at] = dot(pick, ogleft[...]).astype(BF16)
    gx[512:576, :] = dot(left_picker(0), xleft[:, HALF:]).astype(BF16)
    lane = iota((576, 128), 1)
    mine = (lane == expert) | (lane == expert + 32)
    gate = jnp.sum(jnp.where(mine, gx[...].astype(F32), 0.0), axis=1, keepdims=True)

    pl.semaphore_wait(barrier, 15 + extra)
    wide = pl.ds(pl.multiple_of(ten * 128, 128), 256)
    narrow = pl.ds(pl.multiple_of((1 - ten) * 256, 128), 128)
    here_rows = pl.ds(pl.multiple_of(ctx * ROWS, 64), ROWS)

    def momentum(act):
        for k in range(3):
            for turn in range(4):
                i = lax.rem(z + turn, 4)
                slot = 2 * CORE_SLOT[k]
                for part, (src, dst) in enumerate(
                    (
                        (mlow_h.at[i, k, :, wide], stage.at[slot, here_rows]),
                        (mlow_h.at[i, k, :, narrow], stage.at[slot + 1, here_rows, 0:128]),
                    )
                ):
                    act(
                        src,
                        dst,
                        mo_s.at[i, k, part],
                        mo_r.at[CORE_SLOT[k], ctx, part],
                        2 * i + OWNER_CORE[k],
                        ten,
                    )

    momentum(send_block)

    grad_gate = jnp.zeros((576, 1), F32)
    for n in range(3):
        for k in range(3):
            expert_loads[3 * n + k].wait()
        at = slice(n * 256, (n + 1) * 256)
        pre = dot(xall[...], w9[n])
        up = dot(xall[...], w9[3 + n])
        back = dot(ogall[...], w9[6 + n])
        bent = jnp.tanh(GELU_A * (pre + GELU_B * pre * pre * pre))
        value = 0.5 * pre * (1.0 + bent)
        slope = 0.5 * (1.0 + bent) + 0.5 * pre * (1.0 - bent * bent) * GELU_A * (
            1.0 + 3.0 * GELU_B * pre * pre
        )
        hid = (value * up).astype(BF16).astype(F32)
        grad_gate = grad_gate + jnp.sum(hid * back, axis=1, keepdims=True)
        scaled = back * gate
        ghid[:, at] = (hid * gate).astype(BF16)
        ggp[:, at] = (scaled * up * slope).astype(BF16)
        gup[:, at] = (scaled * value).astype(BF16)

    high = grad_gate.astype(BF16).astype(F32)
    marks = jnp.where(lane == expert, high, jnp.where(lane == expert + 32, grad_gate - high, 0.0))
    marks = marks.astype(BF16)
    gmain[:, D:] = marks[0:512]
    gleft[:, HALF:] = dot(left_packer(0), marks[512:576]).astype(BF16)
    packed = jnp.zeros((256, HALF), F32)
    for m in range(4):
        at = slice(m * HALF, (m + 1) * HALF)
        total = jnp.zeros((576, HALF), F32)
        for n in range(3):
            cols = slice(n * 256, (n + 1) * 256)
            total = total + dot_nt(ggp[:, cols], w9[n, at, :])
            total = total + dot_nt(gup[:, cols], w9[3 + n, at, :])
        gmain[:, at] = total[0:512].astype(BF16)
        packed = packed + dot(left_packer(m), total[512:576].astype(BF16))
    gleft[:, 0:HALF] = packed.astype(BF16)
    g_args = (gmain, gleft, cmain, cleft, g_s, g_r)
    o_args = (xall, oleft, omain_h, oleft_h, o_s, o_r)
    return_rows(*g_args)

    core_copies, plane_copies = {}, {}
    order = [(k, n) for k in (GATE, DOWN, UP) for n in range(3)]
    for k, n in order:
        at = slice(n * 256, (n + 1) * 256)
        rows, right = (ogall, ghid) if k == DOWN else (xall, ggp if k == GATE else gup)
        dw9[3 * k + n] = dot_tn(rows[...], right[:, at]).astype(BF16)
        copy = remote(
            dw9.at[3 * k + n],
            rcore.at[CORE_SLOT[k], n],
            mc_s.at[k, n],
            mc_r.at[k, n],
            ctx=core_peer,
        )
        core_copies[k, n] = copy

        @pl.when(c != OWNER_CORE[k])
        def _(copy=copy):
            copy.start()

    for k, n in order:
        plane_copies[k, n] = remote(
            dw9.at[3 * k + n],
            msum_ref.at[:, n * 256 : (n + 1) * 256],
            my_s.at[k, n],
            my_r.at[k, n],
            tensor=1 - ten,
        )

    def pass_on(k, n):
        @pl.when(ten != owner_plane(k))
        def _():
            plane_copies[k, n].start()

    for k in (GATE, DOWN, UP):
        for n in (0, 2):

            @pl.when((c == OWNER_CORE[k]) & (ten == 1 - n // 2))
            def _(k=k, n=n):
                core_copies[k, n].wait_recv()
                total = dw9[3 * k + n].astype(F32) + rcore[CORE_SLOT[k], n].astype(F32)
                dw9[3 * k + n] = total.astype(BF16)
                pass_on(k, n)

    for k in (GATE, DOWN, UP):

        @pl.when(c == OWNER_CORE[k])
        def _(k=k):
            slot = 2 * CORE_SLOT[k]
            for index in range(8):
                rows = pl.ds(index * ROWS, ROWS)
                for part, block in enumerate(
                    (stage.at[slot, rows], stage.at[slot + 1, rows, 0:128])
                ):
                    wait_block_received(
                        block, mo_s.at[0, 0, part], mo_r.at[CORE_SLOT[k], index, part]
                    )
            core_copies[k, 1].wait_recv()
            total = dw9[3 * k + 1].astype(F32) + rcore[CORE_SLOT[k], 1].astype(F32)
            low, high = total[:, 0:128], total[:, 128:256]
            more = stage[slot + 1, :, 0:128].astype(F32)
            dw9[3 * k + 1, :, 0:128] = jnp.where(ten == 0, low + more, low).astype(BF16)
            dw9[3 * k + 1, :, 128:256] = jnp.where(ten == 0, high, high + more).astype(BF16)
            pass_on(k, 1)
            for n in (0, 2):

                @pl.when(ten == n // 2)
                def _(n=n):
                    core_copies[k, n].wait_recv()
                    total = dw9[3 * k + n].astype(F32) + rcore[CORE_SLOT[k], n].astype(F32)
                    dw9[3 * k + n] = (total + stage[slot].astype(F32)).astype(BF16)

    packed = jnp.zeros((256, HALF), F32)
    for m in range(4):
        at = slice(m * HALF, (m + 1) * HALF)
        total = jnp.zeros((576, HALF), F32)
        for n in range(3):
            total = total + dot_nt(ghid[:, n * 256 : (n + 1) * 256], w9[6 + n, at, :])
        xall[0:512, at] = total[0:512].astype(BF16)
        packed = packed + dot(left_packer(m), total[512:576].astype(BF16))
    oleft[...] = packed.astype(BF16)

    weight_loads = [pltpu.make_async_copy(w_h.at[p], w9.at[p], lw.at[p]) for p in range(7)]
    for copy in weight_loads:
        copy.start()

    @pl.when(main)
    def _():
        wait_returned(*g_args)
        extras = dot(ptm[...], cmain[:, D:]) + dot(left_quarter(ptl, 0), cleft[:, HALF:])
        grads = jnp.where(iota((TOK, 128), 1) < 32, extras + pltpu.roll(extras, 96, 1), 0.0)
        gates = gate_ref[...]
        grad_logits = gates * (grads - jnp.sum(gates * grads, axis=1, keepdims=True))
        high = grad_logits.astype(BF16)
        low = (grad_logits - high.astype(F32)).astype(BF16)
        ext[:, D:] = (high.astype(F32) + pltpu.roll(low.astype(F32), 32, 1)).astype(BF16)
        for m in range(4):
            at = slice(m * HALF, (m + 1) * HALF)
            total = dot(ptm[...], cmain[:, at]) + dot(left_quarter(ptl, m), cleft[:, 0:HALF])
            total = total + dot_nt(high, router_ref[at, :]) + dot_nt(low, router_ref[at, :])
            ext[:, at] = total.astype(BF16)

    share = remote(ext, ext, e_s, e_r, tensor=1 - ten)

    @pl.when(main)
    def _():
        share.start()
        share.wait_send()

    @pl.when(jnp.logical_not(main))
    def _():
        share.wait_recv()

    for k in (GATE, DOWN, UP):
        for n in (0, 2):

            @pl.when((c == OWNER_CORE[k]) & (ten == n // 2))
            def _(k=k, n=n):
                pass_on(k, n)

    return_rows(*o_args)

    for copy in later:
        copy.wait()
    dslab[...] = jnp.zeros_like(dslab)

    def norm_rows(r, carry):
        at = pl.ds(pl.multiple_of(r * 64, 64), 64)
        gnb = ext[at, 0:D].astype(F32)
        value = resid[at, :]
        inverse = lax.rsqrt(jnp.mean(value * value, axis=1, keepdims=True) + EPS)
        scaled = gnb * gain_ref[1:2, :]
        inner = jnp.mean(scaled * value, axis=1, keepdims=True)
        gres = gres_ref[at, :] + inverse * scaled - value * (inverse * inverse * inverse) * inner
        gres_ref[at, :] = gres
        gatt[at, :] = gres.astype(BF16)
        flat = gnb * value * inverse
        high = flat.astype(BF16)
        low = (flat - high.astype(F32)).astype(BF16)
        lane = iota((64, 128), 1)
        ones = jnp.where(lane == 32, 1.0, 0.0).astype(BF16)
        both = ext[at, D:].astype(F32)
        logit_high = jnp.where(lane < 32, both, 0.0).astype(BF16)
        logit_low = jnp.where(lane < 32, pltpu.roll(both, 96, 1), 0.0).astype(BF16)
        rows = nbb[at, :]
        dslab[...] += (
            dot_tn(rows, logit_high) + dot_tn(rows, logit_low) + dot_tn(high, ones) + dot_tn(low, ones)
        )
        return carry

    lax.fori_loop(0, 4, norm_rows, 0)

    stores = {}

    def store(p, value):
        if p == 3:
            stores[7].wait()
        stage[p % 4] = value
        stores[p] = pltpu.make_async_copy(stage.at[p % 4], dw_h.at[p], dw_s.at[p])
        stores[p].start()

    halves, quarters = {}, {}

    def share_rows(index):
        return pl.ds(pl.multiple_of(index * ROWS, 64), ROWS)

    for copy in weight_loads:
        copy.wait()
    store(7, jnp.concatenate([dslab[...], jnp.zeros((D, 128), F32)], axis=1).astype(BF16))
    terms = jnp.zeros((TOK, 128), F32)
    for p in range(3):
        gheads[p] = dot(gatt[...], w9[4 + p]).astype(BF16)
        w9[4 + p] = dot_tn(gatt[...], heads[p]).astype(BF16)
        for to_z in range(4):
            copy = remote(
                w9.at[4 + p, share_rows(to_z * 2 + 1 - c)],
                rhalf.at[p, to_z],
                ra_s.at[p, to_z],
                ra_r.at[p, to_z],
                ctx=core_peer,
            )
            copy.start()
            halves[p, to_z] = copy
        prod = gheads[p].astype(F32) * heads[p].astype(F32)
        for i in range(2):
            term = jnp.sum(prod[:, i * 128 : (i + 1) * 128], axis=1, keepdims=True)
            terms = jnp.where(iota((TOK, 128), 1) == 2 * p + i, term, terms)
    lse_rows = jnp.transpose(lse_ref[...])
    term_rows = jnp.transpose(terms)
    dkv[...] = jnp.zeros_like(dkv)
    dq[...] = jnp.zeros_like(dq)
    seg_here = seg_ref[:, pl.ds(pl.multiple_of(ctx * TOK, TOK), TOK)]
    for p in range(3):
        for to_z in range(4):
            halves[p, to_z].wait_recv()
            rows = share_rows(to_z * 2 + c)
            w9[4 + p, rows, :] = (
                w9[4 + p, rows, :].astype(F32) + rhalf[p, to_z].astype(F32)
            ).astype(BF16)
        for d in (1, 3, 2):
            copy = remote(
                w9.at[4 + p, share_rows(lax.rem(z + d, 4) * 2 + c)],
                rquarter.at[p, d - 1],
                rb_s.at[p, d - 1],
                rb_r.at[p, d - 1],
                ctx=z_peer(d),
            )
            copy.start()
            quarters[p, d] = copy

    def key_block(b, carry):
        at = pl.ds(pl.multiple_of(b * TOK, TOK), TOK)
        seg_col = row_to_column(seg_ref[:, at])
        key_pos = b * TOK + iota((TOK, TOK), 0)
        query_pos = ctx * TOK + iota((TOK, TOK), 1)
        allowed = (key_pos <= query_pos) & (seg_here == seg_col)
        keys, values = kv[at, 0:128], kv[at, 128:256]
        dk = jnp.zeros((TOK, 128), F32)
        dv = jnp.zeros((TOK, 128), F32)
        for j in range(6):
            lanes = slice((j % 2) * 128, (j % 2) * 128 + 128)
            qj, gj = q[j // 2, :, lanes], gheads[j // 2, :, lanes]
            scores = dot_nt(keys, qj) * SCALE
            probs = jnp.where(allowed, jnp.exp(scores - lse_rows[j : j + 1, :]), 0.0)
            grad = dot_nt(values, gj)
            grad_scores = (probs * (grad - term_rows[j : j + 1, :]) * SCALE).astype(BF16)
            dv = dv + dot(probs.astype(BF16), gj)
            dk = dk + dot(grad_scores, qj)
            dq[j // 2, :, lanes] += dot_tn(grad_scores, keys)
        dkv[at, 0:128] = dk.astype(BF16)
        dkv[at, 128:256] = dv.astype(BF16)
        return carry

    lax.fori_loop(0, ctx + 1, key_block, 0)

    pair = []
    for to_z in range(4):
        src = dkv.at[pl.ds(pl.multiple_of((to_z * 2 + 1 - c) * TOK, TOK), TOK)]
        copy = remote(src, rkv.at[to_z], k1_s.at[to_z], k1_r.at[to_z], ctx=core_peer)
        copy.start()
        pair.append(copy)
    for p in range(3):
        store(p, dot_tn(nba[...], dq[p].astype(BF16)).astype(BF16))
    total = dot_nt(dq[0].astype(BF16), w9[0])
    total = total + dot_nt(dq[1].astype(BF16), w9[1])
    total = total + dot_nt(dq[2].astype(BF16), w9[2])
    for to_z in range(4):
        pair[to_z].wait_recv()
        own = dkv[pl.ds(pl.multiple_of((to_z * 2 + c) * TOK, TOK), TOK), :]
        skv[to_z] = (own.astype(F32) + rkv[to_z].astype(F32)).astype(BF16)
    ring = []
    for d in (1, 3, 2):
        copy = remote(
            skv.at[lax.rem(z + d, 4)], r2kv.at[d - 1], k2_s.at[d - 1], k2_r.at[d - 1], ctx=z_peer(d)
        )
        copy.start()
        ring.append(copy)
    for copy in ring:
        copy.wait_recv()
    gkv = skv[z].astype(F32) + r2kv[0].astype(F32) + r2kv[1].astype(F32) + r2kv[2].astype(F32)
    gkv = gkv.astype(BF16)
    store(3, dot_tn(nba[...], gkv).astype(BF16))
    total = total + dot_nt(gkv, w9[3])
    gna_ref[...] = total.astype(BF16)

    for k in range(3):
        for n in range(3):
            plane = plane_copies[k, n]

            @pl.when((c == OWNER_CORE[k]) & (ten == owner_plane(k)))
            def _(k=k, n=n, plane=plane):
                plane.wait_recv()
                at = slice(n * 256, (n + 1) * 256)
                msum_ref[:, at] = (
                    dw9[3 * k + n].astype(F32) + msum_ref[:, at].astype(F32)
                ).astype(BF16)

            @pl.when((c == OWNER_CORE[k]) & (ten != owner_plane(k)))
            def _(plane=plane):
                plane.wait_send()

            @pl.when(c != OWNER_CORE[k])
            def _(k=k, n=n):
                core_copies[k, n].wait_send()

    @pl.when(jnp.logical_not(is_owner(c, ten)))
    def _():
        msum_ref[...] = jnp.zeros_like(msum_ref)

    momentum(wait_block_sent)
    for copy in pair + ring:
        copy.wait_send()
    wait_return_sent(*g_args)
    wait_return_sent(*o_args)

    @pl.when(main)
    def _():
        wait_returned(*o_args)

    for p in range(3):
        total = w9[4 + p, share_rows(ctx), :].astype(F32)
        for d in (1, 3, 2):
            quarters[p, d].wait_recv()
            total = total + rquarter[p, d - 1].astype(F32)
        sums_ref[p] = total.astype(BF16)
    for copy in list(halves.values()) + list(quarters.values()):
        copy.wait_send()
    for p in range(4):
        stores[p].wait()


def run_backward(choice_rows, seg, fwd, og, mlow):
    (q, kv, heads, lse, w, resid, nba, nbb, gate, gain, router, wexp, xm, xl, om, ol) = fwd
    vmem = pl.BlockSpec(memory_space=pltpu.VMEM)
    hbm = pl.BlockSpec(memory_space=pl.ANY)
    S = jax.ShapeDtypeStruct
    V = pltpu.VMEM
    return pl.pallas_call(
        backward_kernel,
        out_shape=[
            S((8, D, 256), BF16),
            S((3, ROWS, 256), BF16),
            S((TOK, D), F32),
            S((TOK, D), BF16),
            S((D, FF), BF16),
            S((1024, D), BF16),
            S((512, HALF), BF16),
        ],
        in_specs=[vmem] * 6 + [hbm] * 14,
        out_specs=[hbm, vmem, vmem, vmem, vmem, hbm, hbm],
        scratch_shapes=[
            V((576, D), BF16),
            V((576, 128), BF16),
            V((256, HALF + 128), BF16),
            V((576, D), BF16),
            V((256, HALF), BF16),
            V((9, D, 256), BF16),
            V((576, FF), BF16),
            V((576, FF), BF16),
            V((8, 128), BF16),
            V((576, FF), BF16),
            V((512, D + 128), BF16),
            V((256, HALF + 128), BF16),
            V((256, HALF), BF16),
            V((9, D, 256), BF16),
            V((2, 3, D, 256), BF16),
            V((1024, D + 128), BF16),
            V((512, HALF + 128), BF16),
            V((TOK, 1024), BF16),
            V((TOK, 512), BF16),
            V((TOK, D + 128), BF16),
            V((2048, 256), BF16),
            V((3, TOK, 256), BF16),
            V((3, TOK, 256), BF16),
            V((TOK, D), BF16),
            V((TOK, D), BF16),
            V((TOK, D), F32),
            V((3, TOK, 256), BF16),
            V((TOK, D), BF16),
            V((D, 128), F32),
            V((3, TOK, 256), F32),
            V((2048, 256), BF16),
            V((4, TOK, 256), BF16),
            V((4, TOK, 256), BF16),
            V((3, TOK, 256), BF16),
            V((4, D, 256), BF16),
            V((3, 4, ROWS, 256), BF16),
            V((3, 3, ROWS, 256), BF16),
            sems(12),
            sems(9),
            sems(8),
            sems(3, 4),
            sems(3, 4),
            sems(3, 3),
            sems(3, 3),
            sems(2, 16),
            sems(2, 32),
            sems(2, 16),
            sems(2, 32),
            sems(3, 3),
            sems(3, 3),
            sems(3, 3),
            sems(3, 3),
            pltpu.SemaphoreType.DMA,
            pltpu.SemaphoreType.DMA,
            sems(4),
            sems(4),
            sems(3),
            sems(3),
            sems(4, 3, 2),
            sems(2, 8, 2),
        ],
        compiler_params=pltpu.CompilerParams(
            collective_id=1, has_side_effects=True, vmem_limit_bytes=61 * MiB
        ),
        name="backward",
    )(
        choice_rows, seg, gate, lse, gain, router, xm, xl, om, ol, wexp.reshape(3, D, FF),
        w, q, kv, heads, nba, nbb, resid, og, mlow,
    )
NS_A = 3.4445
NS_B = -4.775
NS_C = 2.0315
MUON_RATES = (0.15, 0.15, 0.6)


def update_kernel(
    choice_ref,
    gain_ref,
    hid_h,
    gna_h,
    msum_h,
    sums_h,
    dw_h,
    omain_h,
    oleft_h,
    agrad_ref,
    rgrad_ref,
    term_ref,
    moe_ref,
    ghome_h,
    ohome_h,
    fin_ref,
    hid_ref,
    gna_ref,
    msum_ref,
    own,
    r1,
    r2,
    r3,
    s2,
    slab,
    omain,
    oleft,
    ptm,
    ptl,
    moe_send,
    gnap,
    ns_x,
    ns_b,
    ld,
    a_s,
    a_r,
    b_s,
    b_r,
    c_s,
    c_r,
    d_s,
    d_r,
    l_s,
    l_r,
    gn_s,
    gn_r,
    gh_s,
    gh_r,
    oh_s,
    oh_r,
):
    dp, ctx, ten, z, c = place()
    main = c == ten
    core_peer = z * 2 + 1 - c

    def z_peer(d):
        return lax.rem(z + d, 4) * 2 + c

    barrier = pltpu.get_barrier_semaphore()
    greet_group(barrier)
    for j in range(1, 8):
        pl.semaphore_signal(
            barrier, inc=1, device_id={"dp": lax.rem(dp + j, 8)}, device_id_type=MESH
        )

    loads = [
        pltpu.make_async_copy(dw_h.at[7], slab, ld.at[0]),
        pltpu.make_async_copy(omain_h, omain, ld.at[1]),
        pltpu.make_async_copy(oleft_h, oleft, ld.at[2]),
        pltpu.make_async_copy(gna_h, gna_ref, ld.at[31]),
        pltpu.make_async_copy(msum_h, msum_ref, ld.at[32]),
        pltpu.make_async_copy(hid_h, hid_ref, ld.at[33]),
    ]
    sums_load = pltpu.make_async_copy(sums_h, s2.at[pl.ds(4, 3)], ld.at[30])
    sums_load.start()
    own_loads = []
    for p in range(4):
        for to_z in range(4):
            rows = pl.ds(pl.multiple_of((to_z * 2 + c) * ROWS, 64), ROWS)
            own_loads.append(
                pltpu.make_async_copy(dw_h.at[p, rows], own.at[p, to_z], ld.at[3 + p * 4 + to_z])
            )
    for copy in loads + own_loads:
        copy.start()

    owner = is_owner(c, ten)

    pl.semaphore_wait(barrier, 22)

    swap = remote(gna_ref, gnap, gn_s, gn_r, tensor=1 - ten)
    loads[3].wait()
    swap.start()

    def first(p, to_z):
        rows = pl.ds(pl.multiple_of((to_z * 2 + 1 - c) * ROWS, 64), ROWS)
        src = slab.at[rows] if p == 7 else dw_h.at[p, rows]
        return remote(src, r1.at[p, to_z], a_s.at[p, to_z], a_r.at[p, to_z], ctx=core_peer)

    def send_first(p):
        for to_z in range(4):
            first(p, to_z).start()

    for p in (0, 1, 2, 3):
        send_first(p)

    def spread(src, dst_h, send_sem, recv_sem, act):
        for k in range(3):

            @pl.when((c == OWNER_CORE[k]) & (ten == owner_plane(k)))
            def _(k=k):
                for j in range(8):
                    to = lax.rem(ctx + j, 8)
                    rows = pl.ds(pl.multiple_of(to * ROWS, 64), ROWS)
                    for i in range(2):
                        t = lax.rem(ten + i, 2)
                        act(
                            src.at[rows, half_columns(t)],
                            dst_h.at[z, k],
                            send_sem.at[to, t],
                            recv_sem.at[z, k],
                            to,
                            t,
                        )

    def second(p, d):
        return remote(
            own.at[p, lax.rem(z + d, 4)],
            r2.at[p, d - 1],
            b_s.at[p, d - 1],
            b_r.at[p, d - 1],
            ctx=z_peer(d),
        )

    def send_second(p):
        for to_z in range(4):
            first(p, to_z).wait_recv()
        own[p] = (own[p].astype(F32) + r1[p].astype(F32)).astype(BF16)
        for d in (1, 3, 2):
            second(p, d).start()

    def send_sum(p):
        @pl.when(p != dp)
        def _():
            remote(s2.at[p], r3.at[dp], c_s.at[p], c_r.at[dp], dp=p).start()

        @pl.when(p == dp)
        def _():
            r3[dp] = s2[p]

    for copy in loads[4:]:
        copy.wait()
    spread(msum_ref, ghome_h, gh_s, gh_r, send_block)
    sums_load.wait()
    for p in (4, 5, 6):
        send_sum(p)

    @pl.when(owner)
    def _():
        whole = msum_ref[...].astype(F32)
        norm = jnp.sqrt(jnp.sum(whole * whole)) + 1e-07
        ns_x[...] = (whole / norm).astype(BF16)

    def norm_and_first():
        loads[0].wait()
        swap.wait_recv()
        gna = gna_ref[...].astype(F32) + gnap[...].astype(F32)
        hid = hid_ref[...]
        inverse = lax.rsqrt(jnp.mean(hid * hid, axis=1, keepdims=True) + EPS)
        scaled = gna * gain_ref[0:1, :]
        inner = jnp.mean(scaled * hid, axis=1, keepdims=True)
        term_ref[...] = inverse * scaled - hid * (inverse * inverse * inverse) * inner
        flat = gna * hid * inverse
        high = flat.astype(BF16)
        low = (flat - high.astype(F32)).astype(BF16)
        ones = jnp.where(iota((TOK, 128), 1) == 33, 1.0, 0.0).astype(BF16)
        slab[:, 0:128] = (slab[:, 0:128].astype(F32) + dot_tn(high, ones) + dot_tn(low, ones)).astype(BF16)

        send_first(7)
        for to_z in range(4):
            rows = pl.ds(pl.multiple_of((to_z * 2 + c) * ROWS, 64), ROWS)
            own[7, to_z] = slab[rows, :]

    def finish(pairs):
        for p in pairs:
            total = own[p, z].astype(F32)
            for d in (1, 2, 3):
                second(p, d).wait_recv()
                total = total + r2[p, d - 1].astype(F32)
            s2[p] = total.astype(BF16)
            send_sum(p)

    def step(turn, carry):
        @pl.when(owner)
        def _():
            gram = dot_tn(ns_x[...], ns_x[...]).astype(BF16)
            ns_b[...] = gram
            square = dot(ns_b[...], ns_b[...])
            ns_b[...] = (NS_B * ns_b[...].astype(F32) + NS_C * square).astype(BF16)
            for r in range(6):
                at = slice(r * 256, (r + 1) * 256)
                ns_x[at, :] = (
                    NS_A * ns_x[at, :].astype(F32) + dot(ns_x[at, :], ns_b[...])
                ).astype(BF16)

        @pl.when(turn == 0)
        def _():
            for copy in own_loads:
                copy.wait()
            for p in (0, 1, 2, 3):
                send_second(p)

        @pl.when(turn == 4)
        def _():
            finish((0, 1))

        return carry

    lax.fori_loop(0, 5, step, 0)

    spread(ns_x, ohome_h, oh_s, oh_r, send_block)

    norm_and_first()
    finish((2, 3))
    send_second(7)
    finish((7,))

    def arrived(s, carry):
        @pl.when(s != dp)
        def _():
            remote(r3.at[s], r3.at[s], c_s.at[s], c_r.at[s], dp=s).wait_recv()

        return carry

    lax.fori_loop(0, 8, arrived, 0)
    total = r3[0].astype(F32)
    for index in range(1, 8):
        total = total + r3[index].astype(F32)
    fin_ref[dp] = total.astype(BF16)

    def give(j, carry):
        to = lax.rem(dp + j, 8)
        remote(fin_ref.at[dp], fin_ref.at[dp], d_s.at[to], d_r.at[dp], dp=to).start()
        return carry

    lax.fori_loop(1, 8, give, 0)

    _, code = codes_by_token(choice_ref[...])
    loads[1].wait()
    loads[2].wait()
    away = remote(moe_send, moe_ref, l_s, l_r, tensor=1 - ten)

    @pl.when(main)
    def _():
        fill_token_onehot(code, ptm, ptl)
        for m in range(4):
            at = slice(m * HALF, (m + 1) * HALF)
            total = dot(ptm[...], omain[:, at]) + dot(left_quarter(ptl, m), oleft[...])
            to = slice((m % 2) * HALF, (m % 2 + 1) * HALF)

            @pl.when(ten == m // 2)
            def _(total=total, to=to):
                moe_ref[:, to] = total.astype(BF16)

            @pl.when(ten != m // 2)
            def _(total=total, to=to):
                moe_send[:, to] = total.astype(BF16)

        away.start()

    spread(msum_ref, ghome_h, gh_s, gh_r, wait_block_sent)
    for i in range(4):
        for k in range(3):
            wait_block_received(ghome_h.at[i, k], gh_s.at[0, 0], gh_r.at[i, k])
    swap.wait_send()
    for p in (0, 1, 2, 3, 7):
        for to_z in range(4):
            first(p, to_z).wait_send()
        for d in (1, 2, 3):
            second(p, d).wait_send()

    def others(j, carry):
        to = lax.rem(dp + j, 8)
        remote(s2.at[to], r3.at[dp], c_s.at[to], c_r.at[dp], dp=to).wait_send()
        remote(fin_ref.at[dp], fin_ref.at[dp], d_s.at[to], d_r.at[dp], dp=to).wait_send()
        remote(fin_ref.at[to], fin_ref.at[to], d_s.at[to], d_r.at[to], dp=to).wait_recv()
        return carry

    lax.fori_loop(1, 8, others, 0)

    @pl.when(main)
    def _():
        away.wait_send()

    @pl.when(jnp.logical_not(main))
    def _():
        away.wait_recv()

    for p in range(7):
        agrad_ref[2 * p] = fin_ref[p, :, 0:128]
        agrad_ref[2 * p + 1] = fin_ref[p, :, 128:256]
    rgrad_ref[...] = fin_ref[7, :, 0:128].astype(F32)
    spread(ns_x, ohome_h, oh_s, oh_r, wait_block_sent)
    for i in range(4):
        for k in range(3):
            wait_block_received(ohome_h.at[i, k], oh_s.at[0, 0], oh_r.at[i, k])


def run_update(choice_rows, hid, gain, bwd):
    dw, sums, gres, gna, msum, omain, oleft = bwd
    vmem = pl.BlockSpec(memory_space=pltpu.VMEM)
    hbm = pl.BlockSpec(memory_space=pl.ANY)
    S = jax.ShapeDtypeStruct
    V = pltpu.VMEM
    return pl.pallas_call(
        update_kernel,
        out_shape=[
            S((14, ROWS, 128), BF16),
            S((ROWS, 128), F32),
            S((TOK, D), F32),
            S((TOK, FF), BF16),
            S((4, 3, ROWS, HALF), BF16),
            S((4, 3, ROWS, HALF), BF16),
        ],
        in_specs=[vmem] * 2 + [hbm] * 7,
        out_specs=[vmem, vmem, vmem, vmem, hbm, hbm],
        scratch_shapes=[
            V((8, ROWS, 256), BF16),
            V((TOK, D), F32),
            V((TOK, D), BF16),
            V((D, FF), BF16),
            V((8, 4, ROWS, 256), BF16),
            V((8, 4, ROWS, 256), BF16),
            V((8, 3, ROWS, 256), BF16),
            V((8, ROWS, 256), BF16),
            V((8, ROWS, 256), BF16),
            V((D, 256), BF16),
            V((1024, D), BF16),
            V((512, HALF), BF16),
            V((TOK, 1024), BF16),
            V((TOK, 512), BF16),
            V((TOK, FF), BF16),
            V((TOK, D), BF16),
            V((D, FF), BF16),
            V((FF, FF), BF16),
            sems(34),
            sems(8, 4),
            sems(8, 4),
            sems(8, 3),
            sems(8, 3),
            sems(8),
            sems(8),
            sems(8),
            sems(8),
            pltpu.SemaphoreType.DMA,
            pltpu.SemaphoreType.DMA,
            pltpu.SemaphoreType.DMA,
            pltpu.SemaphoreType.DMA,
            sems(8, 2),
            sems(4, 3),
            sems(8, 2),
            sems(4, 3),
        ],
        compiler_params=pltpu.CompilerParams(
            collective_id=2, has_side_effects=True, vmem_limit_bytes=60 * MiB
        ),
        name="update",
    )(choice_rows, gain, hid, gna, msum, sums, dw, omain, oleft)


def adam_update(weight, first, second, grad, rate, decay):
    first_new = 0.9 * first + 0.1 * grad
    second_new = 0.95 * second + 0.05 * grad * grad
    corrected = first_new / (1.0 - 0.9**10)
    denominator = jnp.sqrt(second_new / (1.0 - 0.95**10)) + 1e-08
    return (first_new, second_new, weight * (1.0 - rate * decay) - rate * corrected / denominator)


def shards(
    hidden_in,
    out_grad,
    expert_choice,
    segments,
    expert_weights,
    expert_moment,
    attention_weights,
    attention_first,
    attention_second,
    router_weights,
    router_first,
    router_second,
    norm_gains,
    gains_first,
    gains_second,
):
    tensor = lax.axis_index("tensor")
    choice_rows = expert_choice.T
    fwd = run_forward(
        hidden_in,
        out_grad,
        choice_rows,
        segments,
        attention_weights,
        router_weights,
        norm_gains,
        expert_weights,
    )
    resid, gain = fwd[5], fwd[9]
    mlow = (0.95 * expert_moment).astype(BF16)
    bwd = run_backward(choice_rows, segments, fwd, out_grad, mlow)
    gres = bwd[2]
    agrad, rgrad, term, moe, ghome, ohome = run_update(choice_rows, hidden_in, gain, bwd)

    layer_output = lax.dynamic_slice_in_dim(resid, tensor * FF, FF, 1) + moe.astype(F32)
    input_grad = gres + term
    moment_new = ghome.astype(F32)
    rates = jnp.array(MUON_RATES, F32)[None, :, None, None]
    expert_new = expert_weights * (1.0 - rates * 0.1) - rates * (0.2 * D**0.5) * ohome.astype(F32)
    slot_rates = jnp.where(jnp.arange(14) >= 8, 0.5, 0.05)[None, :, None, None]
    attention_out = adam_update(
        attention_weights,
        attention_first,
        attention_second,
        agrad.astype(F32)[None],
        slot_rates,
        0.1,
    )
    router_out = adam_update(
        router_weights.T, router_first.T, router_second.T, rgrad[:, 0:32].T, 0.025, 0.1
    )
    gains_grad = jnp.stack([rgrad[:, 33], rgrad[:, 32]])
    gains_out = adam_update(norm_gains, gains_first, gains_second, gains_grad, 1.0, 0.0)
    return (
        layer_output,
        input_grad,
        moment_new,
        expert_new,
        *attention_out,
        *(out.T for out in router_out),
        *gains_out,
    )


def solution(mesh):
    tokens = P(("dp", "ctx"), None)
    expert = P("dp", None, "ctx", "tensor")
    attention = P("tensor", None, "ctx", None)
    router = P("ctx", None)
    gains = P(None, "ctx")
    return jax.shard_map(
        shards,
        mesh=mesh,
        in_specs=(
            (tokens,) * 3
            + (P("dp", None),)
            + (expert,) * 2
            + (attention,) * 3
            + (router,) * 3
            + (gains,) * 3
        ),
        out_specs=(
            (P(("dp", "ctx"), "tensor"), tokens)
            + (expert,) * 2
            + (attention,) * 3
            + (router,) * 3
            + (gains,) * 3
        ),
        check_vma=False,
    )
```
